256 devices in a mesh: dp: 8 (over x, core), cluster: 32 (over z, y).
Axes of the slice: x: 4, y: 4, z: 8, core: 2. Of those that a mesh axis runs over, the one named last changes fastest.
Arguments:
- points: bfloat16 [2, 65536, 1024], P(None, ('dp', 'cluster')), may hold values from -400 to 400
- candidates: int32 [2, 2048, 4], P(None, ('dp', 'cluster')), may hold values from 0 to 31, all different within a row; in each aligned block of 8 rows (0 to 7, 8 to 15, ..., all dimensions but the last counted through in order) at most 2 rows name the same one
- centroids: bfloat16 [16384, 1024], P('cluster'), may hold values from -0.1875 to 0.1875
Outputs:
- final_sums: float32 [16384, 1024], P('cluster', 'dp')
- final_counts: float32 [16384], P('cluster')
The draws below stay inside these ranges and needn't reach their ends.
Inputs may be any that keep to these rules, and one draw needn't show every extreme that they name: `candidates`: each row names 4 different centroid blocks. In the 8 aligned rows of one step that belong to one device, no block is named more than 2 times, and in some such blocks of rows one block is named exactly 2 times.
All inputs are finite; a program needn't handle non-finite values.
Results may differ from the reference program's by a relative error of at most 0.015.
The reference program's roundings to bfloat16 on the way count: a program that leaves them out, or rounds other values in their place, can miss the bound.
Values may be sent and summed in bfloat16 or wider, within the bound.
A program may use at most 64 MiB of HBM per device.

```python
import math
import jax
import jax.numpy as jnp
import numpy as np
from jax import lax

D = 1024
CBS = 512
K = 4
PBLK_DEV = 8
PB = 32
STEPS = 2
CAP = 2
CENT = 16384
NPB = 2048
NPTS = 65536
N_CLUSTER = 32


def draw_points(key, part):
    key = jax.random.fold_in(key, 7)
    base_key = jax.random.fold_in(key, 0)
    draw_shape = (STEPS, NPTS, D)
    values = 2.0 * jax.random.truncated_normal(base_key, -6.0, 6.0, draw_shape, jnp.float32)
    return values.astype(jnp.bfloat16)


def level_of(stream_key, dims, cuts, smallest, high):
    def one(dim, parts):
        heights = jax.random.uniform(jax.random.fold_in(jax.random.fold_in(stream_key, 6), dim), (parts,), jnp.float32, smallest / len(cuts), high / len(cuts))
        return jnp.repeat(jnp.exp(heights), dims[dim] // parts).reshape((-1,) + (1,) * (len(dims) - dim - 1))

    level = one(*cuts[0])
    for cut in cuts[1:]:
        level = level * one(*cut)
    return level


def routed_block(key, own, number, rows, amount, top, limit, lean):
    ranking = jax.random.permutation(key, amount)
    packed, usual = shares(amount, rows * top, limit, lean, True), shares(amount, rows * top, limit, lean, False)
    places = jnp.arange(amount)

    def named(tallies, rotation):
        used = int((tallies > 0).sum())
        fixed = max(1, used // 4)
        moved = fixed + (places - fixed + rotation * (used - fixed)) % max(1, amount - fixed)
        return jnp.zeros((amount,), jnp.int32).at[ranking[jnp.where(places < fixed, places, moved)]].set(jnp.asarray(tallies, jnp.int32))

    tallies = jnp.where(number % 4 == 0, named(packed, number // 4), named(usual, number - number // 4 - 1))
    mixed = jax.random.permutation(jax.random.fold_in(own, 3), amount)
    giver, sink = mixed[0:amount // 2 * 2:2], mixed[1:amount // 2 * 2:2]
    margin = jnp.minimum(tallies[giver] - 1, limit - tallies[sink]) // 2
    margin = jnp.where((giver == ranking[0]) | (sink == ranking[0]) | (tallies[sink] == 0), 0, jnp.maximum(margin, 0))
    moved = jax.random.randint(jax.random.fold_in(own, 4), (amount // 2,), 0, 1 << 20) % (margin + 1)
    tallies = tallies.at[giver].add(-moved).at[sink].add(moved)
    items = jnp.searchsorted(jnp.cumsum(tallies), jnp.arange(rows * top), side="right").astype(jnp.int32)
    listing = items.reshape(top, rows).T
    listing = listing[jax.random.permutation(jax.random.fold_in(own, 1), rows)]
    rotation = jax.random.randint(jax.random.fold_in(own, 2), (rows, 1), 0, top)
    return jnp.take_along_axis(listing, (jnp.arange(top)[None, :] + rotation) % top, axis=1)


def shares(number_of, total, most, slope, full):
    portions = [(1 << 20) // math.isqrt(standing ** slope) + 1 for standing in range(1, number_of + 1)]
    largest = most if full else min(most, max(-(-total // number_of), total * portions[0] // sum(portions)))
    least = 1 if total - largest >= number_of - 1 else 0
    holding, spare = [largest] + [least] * (number_of - 1), total - largest - least * (number_of - 1)
    while spare > 0:
        free = [i for i in range(1, number_of) if holding[i] < largest] or [i for i in range(1, number_of) if holding[i] < most]
        pool, left = sum([portions[i] for i in free]), spare
        for i in free:
            extra = min(most - holding[i], max(1, left * portions[i] // pool), spare)
            holding[i] = holding[i] + extra
            spare = spare - extra
    return np.array(holding)


def scatter_about(rng, dims, deviation, bound, pieces=(), dtype=jnp.bfloat16):
    loudness = level_of(rng, dims, pieces, -0.22, 0.18) if pieces else 1.0
    array = jax.random.normal(rng, dims, jnp.float32) * deviation * loudness
    return jnp.minimum(jnp.maximum(array, -bound), bound).astype(dtype)


def setup_inputs(seed: int = 0) -> dict:
    seeds = jax.random.split(jax.random.key(seed), 4)
    points = draw_points(jax.random.fold_in(seeds[3], 71), 0)
    candidates_keys = jax.random.split(jax.random.fold_in(seeds[1], 1), STEPS * NPB // PBLK_DEV)
    candidates_turns = jax.random.permutation(jax.random.fold_in(seeds[1], 3), STEPS * NPB // PBLK_DEV)
    candidates = jax.vmap(lambda own, number: routed_block(jax.random.fold_in(seeds[1], 2), own, number, PBLK_DEV, N_CLUSTER, K, CAP, 2))(candidates_keys, candidates_turns).reshape((STEPS, NPB, K))
    centroids = scatter_about(seeds[2], (CENT, D), D ** -0.5, 0.1875, ((0, 32),))
    return dict(points=points, candidates=candidates, centroids=centroids)


def normalize_rows(vectors):
    return vectors / jnp.sqrt(lax.optimization_barrier(jnp.sum(vectors * vectors, axis=1, keepdims=True)) + 1e-06)

def soft_step(step_points, step_cands, centroid_rows):
    centroid_blocks = centroid_rows.reshape(N_CLUSTER, CBS, D)
    group_count = NPB // PBLK_DEV
    point_groups = step_points.reshape(group_count, PBLK_DEV, PB, D)
    cand_groups = step_cands.reshape(group_count, PBLK_DEV, K)

    def visit(running, current):
        block_sums, block_counts = running
        group_points, group_cands = current
        picked = centroid_blocks[group_cands]
        points_f32 = group_points.astype(jnp.float32)
        scores = jnp.einsum('gpd,gkcd->gpkc', points_f32, picked.astype(jnp.float32))
        row_max = lax.optimization_barrier(jnp.max(scores, axis=(2, 3), keepdims=True))
        shifted = jnp.exp(scores - row_max)
        row_total = lax.optimization_barrier(jnp.sum(shifted, axis=(2, 3), keepdims=True))
        weights = lax.optimization_barrier((shifted / row_total).astype(jnp.bfloat16)).astype(jnp.float32)
        part_sums = jnp.einsum('gpkc,gpd->gkcd', weights, points_f32)
        part_counts = lax.optimization_barrier(jnp.sum(weights, axis=1))
        block_ids = group_cands.reshape(-1).astype(jnp.int32)
        block_sums = block_sums.at[block_ids].add(part_sums.reshape(-1, CBS, D))
        block_counts = block_counts.at[block_ids].add(part_counts.reshape(-1, CBS))
        return ((block_sums, block_counts), None)
    zero_state = (jnp.zeros((N_CLUSTER, CBS, D), jnp.float32), jnp.zeros((N_CLUSTER, CBS), jnp.float32))
    (block_sums, block_counts), _ = lax.scan(visit, zero_state, (point_groups, cand_groups))
    return (block_sums.reshape(CENT, D), block_counts.reshape(CENT))

def reference(points, candidates, centroids):
    current = centroids
    for step_index in range(STEPS):
        block_sums, block_counts = soft_step(points[step_index], candidates[step_index], current)
        if step_index + 1 < STEPS:
            current = normalize_rows(current.astype(jnp.float32) + block_sums).astype(jnp.bfloat16)
    return (block_sums, block_counts)
```

```python
import jax
import jax.numpy as jnp
from jax import lax
from jax.experimental import pallas as pl
from jax.experimental.pallas import tpu as pltpu
from jax.sharding import PartitionSpec as P

MESH = pl.DeviceIdType.MESH
F32 = jnp.float32
BF16 = jnp.bfloat16
BIG = 3.0e38
NZ, NY, NX, NC = 8, 4, 4, 2
NB, PB, D, CBS = 8, 32, 1024, 512
PLUS = ((1, 0), (1, 1), (2, 0), (2, 1), (3, 0), (3, 1), (4, 0))
MINUS = ((7, 1), (7, 0), (6, 1), (6, 0), (5, 1), (5, 0), (4, 1))
SCHEDULE = (
    ("zs", 0, 0), ("zs", 0, 1), ("pick", 0, 0), ("relay", 0, 0), ("ze", 0, 0, 0), ("ze", 0, 1, 0), ("score", 0, 0),
    ("ze", 0, 0, 1), ("pick", 0, 1), ("ze", 0, 1, 1), ("pick", 0, 7), ("relay", 0, 1), ("ze", 0, 0, 2),
    ("ze", 0, 1, 2), ("relay", 0, 7), ("ze", 0, 0, 3), ("pick", 0, 2), ("ze", 0, 1, 3), ("pick", 0, 6),
    ("score", 0, 1), ("score", 0, 7), ("relay", 0, 2), ("ze", 0, 0, 4), ("ze", 0, 1, 4), ("relay", 0, 6),
    ("ze", 0, 0, 5), ("pick", 0, 3), ("ze", 0, 1, 5), ("pick", 0, 5), ("score", 0, 2), ("score", 0, 6),
    ("relay", 0, 3), ("ze", 0, 0, 6), ("ze", 0, 1, 6), ("zs", 1, 0), ("zs", 1, 1), ("pick", 0, 4), ("relay", 0, 5),
    ("score", 0, 3), ("ze", 1, 0, 0), ("relay", 0, 4), ("pick", 1, 0), ("ze", 1, 1, 0), ("score", 0, 5),
    ("ze", 1, 0, 1), ("pick", 1, 1), ("ze", 1, 1, 1), ("pick", 1, 7), ("relay", 1, 0), ("score", 0, 4), ("share", 0),
    ("partial", 0), ("ze", 1, 0, 2), ("ze", 1, 1, 2), ("relay", 1, 1), ("relay", 1, 7), ("whole", 0), ("ze", 1, 0, 3),
    ("ze", 1, 1, 3), ("pick", 1, 2), ("pick", 1, 6), ("weigh", 0), ("rf", 0), ("rf", 1), ("rf", 2), ("rf", 3),
    ("ro", 0), ("ze", 1, 0, 4), ("ze", 1, 1, 4), ("rc", 0), ("ro", 1), ("relay", 1, 2), ("rc", 1), ("ro", 2),
    ("rc", 2), ("ro", 3), ("rh", 0), ("rc", 3), ("rh", 1), ("rh", 2), ("ze", 1, 0, 5), ("pick", 1, 3), ("ze", 1, 1, 5),
    ("relay", 1, 6), ("pick", 1, 5), ("rh", 3), ("ze", 1, 0, 6), ("relay", 1, 3), ("ze", 1, 1, 6), ("pick", 1, 4),
    ("update",), ("relay", 1, 5), ("gather1",), ("gather2",), ("gather3",), ("score", 1, 0), ("relay", 1, 4),
    ("score", 1, 1), ("score", 1, 7), ("score", 1, 2), ("score", 1, 6), ("score", 1, 3), ("score", 1, 5),
    ("score", 1, 4), ("share", 1), ("partial", 1), ("whole", 1), ("weigh", 1), ("ls", 0), ("ls", 1), ("ls", 2),
    ("ls", 3), ("lq",), ("cnt",), ("lu",), ("own",), ("fin",),
)


def kernel(
    pts,
    cands,
    cent,
    out_sums,
    out_counts,
    zbufs,
    xs,
    outs,
    relays,
    tab,
    tab_in,
    tab_sm,
    scores,
    tops,
    w,
    lses,
    stats,
    sent_parts,
    parts_in,
    sent_shifts,
    shifts,
    psend,
    precv,
    phold,
    h1,
    h2,
    cur1,
    fb,
    fs,
    fr,
    g,
    q,
    u,
    cnts,
    z_send,
    z_recv,
    y_send,
    x_recv,
    r_recv,
    r_send,
    st_sem,
    tab_sem,
    dp_send,
    dp_recv,
    fin_send,
    fin_recv,
):
    dp = lax.axis_index("dp")
    cl = lax.axis_index("cluster")
    x, core = lax.div(dp, NC), lax.rem(dp, NC)
    z, y = lax.div(cl, NY), lax.rem(cl, NY)

    sign = 1 - 2 * core

    def at_cluster(k, dy):
        return {"cluster": lax.rem(z + sign * k + NZ, NZ) * NY + lax.rem(y + dy + NY, NY)}

    xp, xm, xo = lax.rem(x + 1, NX), lax.rem(x + 3, NX), lax.rem(x + 2, NX)
    dev_xp, dev_xm = {"dp": xp * NC + core}, {"dp": xm * NC + core}
    dev_core = {"dp": x * NC + 1 - core}
    z_devs = at_cluster(1, 0), at_cluster(-1, 0)
    y_up, y_down = at_cluster(0, 1), at_cluster(0, -1)

    barrier = pltpu.get_barrier_semaphore()
    for peer in [at_cluster(k, 0) for k in range(1, NZ)] + [at_cluster(0, p) for p in range(1, NY)]:
        pl.semaphore_signal(barrier, inc=1, device_id=peer, device_id_type=MESH)
    for j in range(1, NX * NC):
        pl.semaphore_signal(
            barrier, inc=1, device_id={"dp": lax.rem(dp + j, NX * NC)}, device_id_type=MESH
        )
    pl.semaphore_wait(barrier, NZ - 1 + NY - 1 + NX * NC - 1)

    drains = []

    def send(src, dst, ssem, rsem, dev):
        copy = pltpu.make_async_remote_copy(
            src_ref=src,
            dst_ref=dst,
            send_sem=ssem,
            recv_sem=rsem,
            device_id=dev,
            device_id_type=MESH,
        )
        copy.start()
        return copy

    def landed(ref, sem):
        pltpu.make_async_copy(ref, ref, sem).wait()

    def later(ref, sem):
        drains.append(lambda: landed(ref, sem))

    def drain():
        for wait in drains:
            wait()
        drains.clear()

    def half(ref, h):
        return ref.at[pl.ds(h * 4, 4)]

    def chunk(step, k):
        return pts.at[step] if k == 0 else zbufs[step * 7 + k - 1]

    def z_start(step, d):
        order = (PLUS, MINUS)[d]
        for i in range(2):
            k, h = order[i]
            src = half(pts.at[step], h)
            dst = half(chunk(step, k), h)
            send(src, dst, z_send.at[step, d, i], z_recv.at[step, d, i], z_devs[d])
            later(src, z_send.at[step, d, i])

    def z_event(step, d, i):
        order = (PLUS, MINUS)[d]
        k, h = order[i]
        here = half(chunk(step, k), h)
        landed(here, z_recv.at[step, d, i])
        if i < 5:
            dst = half(chunk(step, order[i + 2][0]), h)
            send(here, dst, z_send.at[step, d, i + 2], z_recv.at[step, d, i + 2], z_devs[d])
            later(here, z_send.at[step, d, i + 2])

    def tables():
        row = lax.broadcasted_iota(jnp.int32, (8, 128), 0)
        lane = lax.broadcasted_iota(jnp.int32, (8, 128), 1)
        oz = (z + sign * row) & (NZ - 1)
        second = ((lane >> 5) & 1) == 1
        for step in range(2):
            for t in range(2):
                owner = oz * NY + ((y + t * 2 + (lane >> 6)) & (NY - 1))
                first = jnp.full((8, 128), NB, jnp.int32)
                last = jnp.full((8, 128), -1, jnp.int32)
                for b in range(NB):
                    hit = owner == cands[step, b, 0]
                    for j in range(1, 4):
                        hit = hit | (owner == cands[step, b, j])
                    last = jnp.where(hit, b, last)
                    first = jnp.minimum(first, jnp.where(hit, b, NB))
                lone = jnp.where(first < NB, first, -1)
                bid = jnp.where(second, jnp.where(last > first, last, -1), lone)
                off = step * 256 + t * 128
                tab[:, :, off : off + 128] = bid.reshape(8, 1, 128)
        for k in range(1, NZ):
            send(tab.at[k], tab_in.at[k], tab_sem.at[0], tab_sem.at[1], at_cluster(k, 0))
        later(tab_in.at[pl.ds(1, 7)], tab_sem.at[0])
        tab_in[0] = tab[0]
        to_scalars(tab, 0, 1)

    def to_scalars(table, first, count):
        rows = pl.ds(first, count)
        copy = pltpu.make_async_copy(table.at[rows], tab_sm.at[rows], tab_sem.at[2])
        copy.start()
        copy.wait()

    def tables_in():
        landed(tab_in.at[pl.ds(1, 7)], tab_sem.at[1])
        to_scalars(tab_in, 1, 7)

    def pick(step, k):
        source, xr, box = chunk(step, k), xs[step], outs[step]

        def block(p, s):
            number = tab_sm[k, 0, step * 256 + p * 64 + s * 32]
            return source[jnp.maximum(number, 0)]

        sems = (y_send.at[step, k], x_recv.at[step, k])
        box[k, 2] = block(2, 0)
        send(box.at[k, 2], relays[step].at[k, 0], sems[0], r_recv.at[step, k, 0], y_up)
        box[k, 3] = block(2, 1)
        send(box.at[k, 3], relays[step].at[k, 1], sems[0], r_recv.at[step, k, 1], y_down)
        for p, dev in ((1, y_up), (3, y_down)):
            first = 0 if p == 1 else 4
            box[k, first] = block(p, 0)
            box[k, first + 1] = block(p, 1)
            send(
                box.at[k, pl.ds(first, 2)], xr.at[pl.ds(k * 8 + p * 2, 2)], sems[0], sems[1], dev
            )
        later(box.at[k], sems[0])
        xr[k * 8] = block(0, 0)
        xr[k * 8 + 1] = block(0, 1)

    def relay(step, k):
        for s, dev in enumerate((y_up, y_down)):
            here = relays[step].at[k, s]
            landed(here, r_recv.at[step, k, s])
            send(
                here,
                xs[step].at[k * 8 + 4 + s],
                r_send.at[step, k],
                x_recv.at[step, k],
                dev,
            )
        later(relays[step].at[k], r_send.at[step, k])

    def score(step, k):
        xr, centroids = xs[step], (cent, cur1)[step]
        landed(xr.at[pl.ds(k * 8 + 2, 6)], x_recv.at[step, k])
        rows = xr[k * 8 : k * 8 + 8].reshape(8 * PB, D)
        s = lax.dot_general(
            centroids[...], rows, (((1,), (1,)), ((), ())), preferred_element_type=F32
        )
        top = jnp.max(s, axis=0, keepdims=True)
        e = jnp.exp(s - top)
        scores[k] = e
        tops[k] = top
        total = jnp.sum(e, axis=0, keepdims=True)
        lse = top + jnp.log(total)
        for i in range(2):
            lses[step][i, k : k + 1, :] = lse[:, i * 128 : (i + 1) * 128]

    low = lax.broadcasted_iota(jnp.int32, (1, 128), 1) < 64
    group = lax.broadcasted_iota(jnp.int32, (1, 128), 1) >> 5

    def over_groups(op, value):
        value = op(value, pltpu.roll(value, 64, 1))
        return op(value, pltpu.roll(value, 32, 1))

    def block_ids(step):
        return [
            tab_in[:, :, step * 256 + i * 128 : step * 256 + i * 128 + 128].reshape(8, 128)
            for i in range(2)
        ]

    def share(step):
        for p in range(1, NY):
            send(
                lses[step].at[p >> 1],
                stats[step].at[p],
                st_sem.at[step, 0],
                st_sem.at[step, 1],
                at_cluster(0, -p),
            )
        stats[step][0] = lses[step][0]
        later(stats[step].at[pl.ds(1, 3)], st_sem.at[step, 0])

    def partial(step):
        got = stats[step]
        landed(got.at[pl.ds(1, 3)], st_sem.at[step, 1])
        have = [jnp.where(low, got[2 * i], got[2 * i + 1]) for i in range(2)]
        ids = block_ids(step)
        packed = [jnp.full((8, 128), -BIG, F32) for _ in range(2)]
        for b in range(NB):
            mine = [ids[i] == b for i in range(2)]
            masked = [jnp.where(mine[i], have[i], -BIG) for i in range(2)]
            top = over_groups(jnp.maximum, jnp.maximum(masked[0], masked[1]))
            each = [jnp.where(mine[i], jnp.exp(have[i] - top), 0.0) for i in range(2)]
            total = over_groups(jnp.add, each[0] + each[1])
            value = jnp.where(total > 0.0, top + jnp.log(total), -BIG)
            packed[b >> 2] = jnp.where(group == (b & 3), value, packed[b >> 2])
        out = sent_parts[step]
        for i in range(2):
            out[i * 8 : i * 8 + 8, :] = packed[i]
        for j in range(1, NZ):
            send(
                out,
                parts_in[step].at[j],
                st_sem.at[step, 2],
                st_sem.at[step, 3],
                at_cluster(j, 0),
            )
        later(parts_in[step].at[pl.ds(1, 7)], st_sem.at[step, 2])

    def whole(step):
        into = parts_in[step]
        landed(into.at[pl.ds(1, 7)], st_sem.at[step, 3])
        ids = block_ids(step)
        shift = [jnp.full((8, 128), BIG, F32) for _ in range(2)]
        for i in range(2):
            rows = slice(i * 8, i * 8 + 8)
            seen = [sent_parts[step][rows, :]]
            for j in range(1, NZ):
                seen.append(pltpu.roll(into[j, rows, :], j, 0))
            top = seen[0]
            for j in range(1, NZ):
                top = jnp.maximum(top, seen[j])
            total = jnp.exp(seen[0] - top)
            for j in range(1, NZ):
                total = total + jnp.exp(seen[j] - top)
            value = top + jnp.log(total)
            for b in range(4):
                spread = over_groups(jnp.maximum, jnp.where(group == b, value, -BIG))
                for t in range(2):
                    shift[t] = jnp.where(ids[t] == i * 4 + b, spread, shift[t])
        out, back = sent_shifts[step], shifts[step]
        for t in range(2):
            out[t] = shift[t]
        back[0] = shift[0]
        for p in range(1, NY):
            send(
                out.at[p >> 1],
                back.at[p],
                st_sem.at[step, 4],
                st_sem.at[step, 5],
                at_cluster(0, p),
            )
        later(back.at[pl.ds(1, 3)], st_sem.at[step, 4])

    def weigh(step):
        back = shifts[step]
        landed(back.at[pl.ds(1, 3)], st_sem.at[step, 5])
        for k in range(NZ):
            for t in range(2):
                shift = jnp.where(low, back[2 * t, k : k + 1, :], back[2 * t + 1, k : k + 1, :])
                lanes = pl.ds(k * 256 + t * 128, 128)
                scale = jnp.exp(tops[k, :, t * 128 : (t + 1) * 128] - shift)
                w[:, lanes] = (scores[k, :, t * 128 : (t + 1) * 128] * scale).astype(BF16)

    def half_sums(which, n):
        rows = w[pl.ds(pl.multiple_of(which * 256, 256), 256), :]
        cols = xs[0][:, :, n * 256 : (n + 1) * 256].reshape(64 * PB, 256)
        return jnp.dot(rows, cols, preferred_element_type=F32)

    def rows64(at, count=64, shift=0):
        return pl.ds(pl.multiple_of(at * 64 + shift, 32), count)

    def rf(n):
        psend[n] = half_sums(1 - core, n)
        send(psend.at[n], precv.at[n], dp_send.at[n], dp_recv.at[n], dev_core)
        later(psend.at[n], dp_send.at[n])

    def ro(n):
        phold[n] = half_sums(core, n)

    def rc(n):
        landed(precv.at[n], dp_recv.at[n])
        far = rows64(xo)
        phold[n, far, :] = phold[n, far, :] + precv[n, far, :]
        sides = ((rows64(xo, 32), dev_xp), (rows64(xo, 32, 32), dev_xm))
        for i, (part, dev) in enumerate(sides):
            sems = dp_send.at[4 + 4 * i + n], dp_recv.at[4 + 4 * i + n]
            send(phold.at[n, part, :], h1.at[i, n], sems[0], sems[1], dev)
            later(h1.at[i, n], sems[0])
        for at in (xp, xm, x):
            near = rows64(at)
            phold[n, near, :] = phold[n, near, :] + precv[n, near, :]

    def rh(n):
        sides = ((xp, 0, dev_xp), (xm, 32, dev_xm))
        for i, (at, shift, dev) in enumerate(sides):
            landed(h1.at[i, n], dp_recv.at[4 + 4 * i + n])
            part = rows64(at, 32, shift)
            phold[n, part, :] = phold[n, part, :] + h1[i, n]
            sems = dp_send.at[12 + 4 * i + n], dp_recv.at[12 + 4 * i + n]
            send(phold.at[n, rows64(at), :], h2.at[i, n], sems[0], sems[1], dev)
            later(h2.at[i, n], sems[0])

    def cur_rows(which_core, at, count=64, shift=0):
        return pl.ds(pl.multiple_of(which_core * 256 + at * 64 + shift, 32), count)

    def update():
        for n in range(4):
            landed(h2.at[0, n], dp_recv.at[12 + n])
            landed(h2.at[1, n], dp_recv.at[16 + n])
        own = rows64(x)
        mine = cur_rows(core, x)
        v = [
            cent[mine, n * 256 : (n + 1) * 256].astype(F32)
            + (phold[n, own, :] + h2[0, n] + h2[1, n])
            for n in range(4)
        ]
        square = sum(jnp.sum(part * part, axis=1, keepdims=True) for part in v)
        norm = jnp.sqrt(square + 1e-06)
        for n in range(4):
            cur1[mine, n * 256 : (n + 1) * 256] = (v[n] / norm).astype(BF16)
        here = cur1.at[mine]
        send(here, here, dp_send.at[20], dp_recv.at[20], dev_xp)
        send(here, here, dp_send.at[21], dp_recv.at[21], dev_xm)
        send(here, here, dp_send.at[22], dp_recv.at[24], dev_core)
        for i in (20, 21, 22):
            later(here, dp_send.at[i])

    def gather1():
        sides = ((xm, 0, dev_xp), (xp, 32, dev_xm))
        for i, (at, shift, dev) in enumerate(sides):
            here = cur1.at[cur_rows(core, at)]
            landed(here, dp_recv.at[20 + i])
            part = cur1.at[cur_rows(core, at, 32, shift)]
            send(part, part, dp_send.at[23 + i], dp_recv.at[22 + i], dev)
            later(part, dp_send.at[23 + i])
            send(here, here, dp_send.at[25 + i], dp_recv.at[24], dev_core)
            later(here, dp_send.at[25 + i])

    def gather2():
        for i, shift in enumerate((0, 32)):
            part = cur1.at[cur_rows(core, xo, 32, shift)]
            landed(part, dp_recv.at[22 + i])
            send(part, part, dp_send.at[27 + i], dp_recv.at[24], dev_core)
            later(part, dp_send.at[27 + i])

    def gather3():
        other = pl.ds(pl.multiple_of((1 - core) * 256, 256), 256)
        landed(cur1.at[other], dp_recv.at[24])

    def ls(j):
        lanes = pl.ds(pl.multiple_of((xo, xp, xm, x)[j] * 256, 256), 256)
        cols = xs[1][:, :, lanes].reshape(64 * PB, 256)
        part = jnp.dot(w[...], cols, preferred_element_type=F32)
        fb[j, 0] = part[:, :128]
        fb[j, 1] = part[:, 128:]
        fs[j] = fb[j, 1 - core].astype(BF16)
        send(fs.at[j], fr.at[j], fin_send.at[0], fin_recv.at[j], dev_core)
        if j == 3:
            later(fs, fin_send.at[0])

    def both(j):
        landed(fr.at[j], fin_recv.at[j])
        return fb[j, core] + fr[j].astype(F32)

    def lq():
        g[0] = both(0).astype(BF16)
        for i, dev in enumerate((dev_xp, dev_xm)):
            rows = pl.ds(256 * i, 256)
            send(g.at[0, rows], q.at[i], fin_send.at[2 + i], fin_recv.at[5 + i], dev)
            later(q.at[i], fin_send.at[2 + i])

    def lu():
        for i, dev in enumerate((dev_xp, dev_xm)):
            part = both(1 + i)
            landed(q.at[i], fin_recv.at[5 + i])
            with_q, rest = pl.ds(256 * i, 256), pl.ds(256 - 256 * i, 256)
            parts = part[:256], part[256:]
            g[1 + i, rest] = parts[1 - i].astype(BF16)
            g[1 + i, with_q] = (parts[i] + q[i].astype(F32)).astype(BF16)
            send(g.at[1 + i], u.at[i], fin_send.at[4 + i], fin_recv.at[7 + i], dev)
            later(u.at[i], fin_send.at[4 + i])

    def cnt():
        ones = jnp.ones((8, 64 * PB), BF16)
        count = lax.dot_general(
            ones, w[...], (((1,), (1,)), ((), ())), preferred_element_type=F32
        )
        cnts[dp] = count[0:1]
        for j in range(1, NX * NC):
            send(
                cnts.at[dp],
                cnts.at[dp],
                fin_send.at[1],
                fin_recv.at[4],
                {"dp": lax.rem(dp + j, NX * NC)},
            )
        later(cnts.at[pl.ds(0, 7)], fin_send.at[1])

    def own():
        fb[3, core] = both(3)
        landed(cnts.at[pl.ds(0, 7)], fin_recv.at[4])
        count = cnts[0]
        for j in range(1, NX * NC):
            count = count + cnts[j]
        for j in range(4):
            out_counts[j : j + 1, :] = count[:, j * 128 : (j + 1) * 128]
        drain()

    def fin():
        landed(u.at[0], fin_recv.at[7])
        landed(u.at[1], fin_recv.at[8])
        out_sums[...] = fb[3, core] + (u[0].astype(F32) + u[1].astype(F32))

    parts = dict(
        zs=z_start,
        ze=z_event,
        pick=pick,
        relay=relay,
        score=score,
        share=share,
        partial=partial,
        whole=whole,
        weigh=weigh,
        rf=rf,
        ro=ro,
        rc=rc,
        rh=rh,
        update=update,
        gather1=gather1,
        gather2=gather2,
        gather3=gather3,
        ls=ls,
        lq=lq,
        lu=lu,
        cnt=cnt,
        own=own,
        fin=fin,
    )
    for name, *numbers in SCHEDULE:
        parts[name](*numbers)
        if (name, *numbers) == ("zs", 0, 0):
            tables()
        if (name, *numbers) == ("relay", 0, 0):
            tables_in()


def on_device(points, candidates, centroids):
    vmem = pl.BlockSpec(memory_space=pltpu.VMEM)
    sem = pltpu.SemaphoreType.DMA
    steps = points.shape[0]
    sums, counts = pl.pallas_call(
        kernel,
        out_shape=(
            jax.ShapeDtypeStruct((CBS, D // (NX * NC)), F32),
            jax.ShapeDtypeStruct((4, 128), F32),
        ),
        in_specs=[vmem, pl.BlockSpec(memory_space=pltpu.SMEM), vmem],
        out_specs=(vmem, vmem),
        scratch_shapes=[
            [pltpu.VMEM((NB, PB, D), BF16) for _ in range(7 * steps)],
            [pltpu.VMEM((64, PB, D), BF16) for _ in range(steps)],
            [pltpu.VMEM((NZ, 6, PB, D), BF16) for _ in range(steps)],
            [pltpu.VMEM((NZ, 2, PB, D), BF16) for _ in range(steps)],
            pltpu.VMEM((NZ, 1, 512), jnp.int32),
            pltpu.VMEM((NZ, 1, 512), jnp.int32),
            pltpu.SMEM((NZ, 1, 512), jnp.int32),
            pltpu.VMEM((NZ, CBS, 256), F32),
            pltpu.VMEM((NZ, 1, 256), F32),
            pltpu.VMEM((CBS, 64 * PB), BF16),
            [pltpu.VMEM((2, 8, 128), F32) for _ in range(steps)],
            [pltpu.VMEM((4, 8, 128), F32) for _ in range(steps)],
            [pltpu.VMEM((16, 128), F32) for _ in range(steps)],
            [pltpu.VMEM((NZ, 16, 128), F32) for _ in range(steps)],
            [pltpu.VMEM((2, 8, 128), F32) for _ in range(steps)],
            [pltpu.VMEM((4, 8, 128), F32) for _ in range(steps)],
            pltpu.VMEM((4, 256, 256), F32),
            pltpu.VMEM((4, 256, 256), F32),
            pltpu.VMEM((4, 256, 256), F32),
            pltpu.VMEM((2, 4, 32, 256), F32),
            pltpu.VMEM((2, 4, 64, 256), F32),
            pltpu.VMEM((CBS, D), BF16),
            pltpu.VMEM((4, 2, CBS, 128), F32),
            pltpu.VMEM((4, CBS, 128), BF16),
            pltpu.VMEM((4, CBS, 128), BF16),
            pltpu.VMEM((3, CBS, 128), BF16),
            pltpu.VMEM((2, 256, 128), BF16),
            pltpu.VMEM((2, CBS, 128), BF16),
            pltpu.VMEM((NX * NC, 1, CBS), F32),
            sem((steps, 2, 7)),
            sem((steps, 2, 7)),
            sem((steps, NZ)),
            sem((steps, NZ)),
            sem((steps, NZ, 2)),
            sem((steps, NZ)),
            sem((steps, 6)),
            sem((3,)),
            sem((29,)),
            sem((25,)),
            sem((6,)),
            sem((9,)),
        ],
        compiler_params=pltpu.CompilerParams(
            collective_id=0, has_side_effects=True, vmem_limit_bytes=56 * 1024 * 1024
        ),
    )(points.reshape(steps, NB, PB, D), candidates, centroids)
    return sums, counts.reshape(CBS)


def solution(mesh):
    placed = (
        P(None, ("dp", "cluster"), None),
        P(None, ("dp", "cluster"), None),
        P("cluster", None),
    )
    return jax.shard_map(
        on_device,
        mesh=mesh,
        in_specs=placed,
        out_specs=(P("cluster", "dp"), P("cluster")),
        check_vma=False,
    )
```

```python
import jax
import jax.numpy as jnp
from jax import lax
from jax.experimental import pallas as pl
from jax.experimental.pallas import tpu as pltpu
from jax.sharding import PartitionSpec as P

MESH = pl.DeviceIdType.MESH
F32 = jnp.float32
BF16 = jnp.bfloat16
BIG = 3.0e38
NZ, NY, NX, NC = 8, 4, 4, 2
NB, PB, D, CBS = 8, 32, 1024, 512
PLUS = ((1, 0), (1, 1), (2, 0), (2, 1), (3, 0), (3, 1), (4, 0))
MINUS = ((7, 1), (7, 0), (6, 1), (6, 0), (5, 1), (5, 0), (4, 1))
SCHEDULE = (
    ("zs", 0, 0), ("zs", 0, 1), ("pick", 0, 0), ("pick", 1, 0), ("relay", 0, 0), ("ze", 0, 0, 0), ("ze", 0, 1, 0),
    ("relay", 1, 0), ("score", 0, 0), ("ze", 0, 0, 1), ("ze", 0, 1, 1), ("pick", 0, 1), ("pick", 0, 7),
    ("relay", 0, 1), ("ze", 0, 0, 2), ("ze", 0, 1, 2), ("relay", 0, 7), ("ze", 0, 0, 3), ("pick", 0, 2),
    ("ze", 0, 1, 3), ("pick", 0, 6), ("score", 0, 1), ("score", 0, 7), ("relay", 0, 2), ("ze", 0, 0, 4),
    ("ze", 0, 1, 4), ("relay", 0, 6), ("ze", 0, 0, 5), ("pick", 0, 3), ("ze", 0, 1, 5), ("pick", 0, 5),
    ("score", 0, 2), ("score", 0, 6), ("relay", 0, 3), ("ze", 0, 0, 6), ("ze", 0, 1, 6), ("zs", 1, 0), ("zs", 1, 1),
    ("pick", 0, 4), ("relay", 0, 5), ("ze", 1, 0, 0), ("ze", 1, 1, 0), ("score", 0, 3), ("relay", 0, 4),
    ("ze", 1, 0, 1), ("pick", 1, 1), ("ze", 1, 1, 1), ("pick", 1, 7), ("score", 0, 5), ("score", 0, 4), ("share", 0),
    ("relay", 1, 1), ("partial", 0), ("ze", 1, 0, 2), ("ze", 1, 1, 2), ("relay", 1, 7), ("whole", 0), ("ze", 1, 0, 3),
    ("pick", 1, 2), ("ze", 1, 1, 3), ("pick", 1, 6), ("weigh", 0), ("rf", 0), ("ro", 0), ("rf", 1), ("ro", 1),
    ("relay", 1, 2), ("rc", 0), ("rf", 2), ("rc", 1), ("ze", 1, 0, 4), ("ze", 1, 1, 4), ("ro", 2), ("rh", 0),
    ("rf", 3), ("rc", 2), ("rh", 1), ("relay", 1, 6), ("ro", 3), ("rc", 3), ("rh", 2), ("ze", 1, 0, 5), ("pick", 1, 3),
    ("ze", 1, 1, 5), ("pick", 1, 5), ("rh", 3), ("update",), ("relay", 1, 3), ("ze", 1, 0, 6), ("ze", 1, 1, 6),
    ("pick", 1, 4), ("gather1",), ("gather1b",), ("relay", 1, 5), ("gather2",), ("gather3",), ("score", 1, 0),
    ("score", 1, 1), ("score", 1, 7), ("score", 1, 2), ("relay", 1, 4), ("score", 1, 6), ("score", 1, 3),
    ("score", 1, 5), ("score", 1, 4), ("share", 1), ("partial", 1), ("whole", 1), ("weigh", 1), ("ls", 0), ("ls", 1),
    ("ls", 2), ("lq",), ("ls", 3), ("cnt",), ("lv",), ("lu",), ("own",), ("fin",),
)


def kernel(
    pts_hbm,
    cands,
    cent_hbm,
    out_sums,
    out_counts,
    pts,
    cent,
    zbufs,
    xs,
    outs,
    relays,
    tab,
    tab_in,
    tab_sm,
    scores,
    tops,
    w,
    lses,
    stats,
    sent_parts,
    parts_in,
    sent_shifts,
    shifts,
    psend,
    precv,
    phold,
    h1,
    h2,
    cur1,
    fb,
    fs,
    fr,
    g,
    q,
    u,
    cnts,
    z_send,
    z_recv,
    y_send,
    x_recv,
    r_recv,
    r_send,
    st_sem,
    tab_sem,
    dp_send,
    dp_recv,
    fin_send,
    fin_recv,
    load_sem,
):
    dp = lax.axis_index("dp")
    cl = lax.axis_index("cluster")
    x, core = lax.div(dp, NC), lax.rem(dp, NC)
    z, y = lax.div(cl, NY), lax.rem(cl, NY)

    sign = 1 - 2 * core

    def at_cluster(k, dy):
        return {"cluster": lax.rem(z + sign * k + NZ, NZ) * NY + lax.rem(y + dy + NY, NY)}

    xp, xm, xo = lax.rem(x + 1, NX), lax.rem(x + 3, NX), lax.rem(x + 2, NX)
    dev_xp, dev_xm = {"dp": xp * NC + core}, {"dp": xm * NC + core}
    dev_core = {"dp": x * NC + 1 - core}
    z_devs = at_cluster(1, 0), at_cluster(-1, 0)
    y_up, y_down = at_cluster(0, 1), at_cluster(0, -1)

    loads = [
        pltpu.make_async_copy(pts_hbm, pts, load_sem.at[0]),
        pltpu.make_async_copy(cent_hbm, cent, load_sem.at[1]),
    ]
    for load in loads:
        load.start()

    barrier = pltpu.get_barrier_semaphore()
    for peer in [at_cluster(k, 0) for k in range(1, NZ)] + [at_cluster(0, p) for p in range(1, NY)]:
        pl.semaphore_signal(barrier, inc=1, device_id=peer, device_id_type=MESH)
    for j in range(1, NX * NC):
        pl.semaphore_signal(
            barrier, inc=1, device_id={"dp": lax.rem(dp + j, NX * NC)}, device_id_type=MESH
        )
    pl.semaphore_wait(barrier, NZ - 1 + NY - 1 + NX * NC - 1)

    drains = []

    def send(src, dst, ssem, rsem, dev):
        copy = pltpu.make_async_remote_copy(
            src_ref=src,
            dst_ref=dst,
            send_sem=ssem,
            recv_sem=rsem,
            device_id=dev,
            device_id_type=MESH,
        )
        copy.start()
        return copy

    def send_cut(src, dst, ssem, rsem, dev):
        size = src.shape[0] // 2
        for i in range(2):
            part = pl.ds(i * size, size)
            send(src.at[part], dst.at[part], ssem, rsem, dev)

    def landed(ref, sem):
        pltpu.make_async_copy(ref, ref, sem).wait()

    def later(ref, sem):
        drains.append(lambda: landed(ref, sem))

    def drain():
        for wait in drains:
            wait()
        drains.clear()

    def half(ref, h):
        return ref.at[pl.ds(h * 4, 4)]

    def chunk(step, k):
        return pts.at[step] if k == 0 else zbufs[step * 7 + k - 1]

    def z_start(step, d):
        order = (PLUS, MINUS)[d]
        for i in range(2):
            k, h = order[i]
            src = half(pts_hbm.at[step], h)
            dst = half(chunk(step, k), h)
            send_cut(src, dst, z_send.at[step, d, i], z_recv.at[step, d, i], z_devs[d])
            later(src, z_send.at[step, d, i])

    def z_event(step, d, i):
        order = (PLUS, MINUS)[d]
        k, h = order[i]
        here = half(chunk(step, k), h)
        landed(here, z_recv.at[step, d, i])
        if i < 5:
            dst = half(chunk(step, order[i + 2][0]), h)
            send_cut(here, dst, z_send.at[step, d, i + 2], z_recv.at[step, d, i + 2], z_devs[d])
            later(here, z_send.at[step, d, i + 2])

    def tables():
        row = lax.broadcasted_iota(jnp.int32, (8, 128), 0)
        lane = lax.broadcasted_iota(jnp.int32, (8, 128), 1)
        oz = (z + sign * row) & (NZ - 1)
        second = ((lane >> 5) & 1) == 1
        for step in range(2):
            for t in range(2):
                owner = oz * NY + ((y + t * 2 + (lane >> 6)) & (NY - 1))
                first = jnp.full((8, 128), NB, jnp.int32)
                last = jnp.full((8, 128), -1, jnp.int32)
                for b in range(NB):
                    hit = owner == cands[step, 0, b]
                    for j in range(1, 4):
                        hit = hit | (owner == cands[step, j, b])
                    last = jnp.where(hit, b, last)
                    first = jnp.minimum(first, jnp.where(hit, b, NB))
                lone = jnp.where(first < NB, first, -1)
                bid = jnp.where(second, jnp.where(last > first, last, -1), lone)
                off = step * 256 + t * 128
                tab[:, :, off : off + 128] = bid.reshape(8, 1, 128)
        for k in range(1, NZ):
            send(tab.at[k], tab_in.at[k], tab_sem.at[0], tab_sem.at[1], at_cluster(k, 0))
        later(tab_in.at[pl.ds(1, 7)], tab_sem.at[0])
        tab_in[0] = tab[0]
        to_scalars(tab, 0, 1)

    def to_scalars(table, first, count):
        rows = pl.ds(first, count)
        copy = pltpu.make_async_copy(table.at[rows], tab_sm.at[rows], tab_sem.at[2])
        copy.start()
        copy.wait()

    def tables_in():
        landed(tab_in.at[pl.ds(1, 7)], tab_sem.at[1])
        to_scalars(tab_in, 1, 7)

    def pick(step, k):
        source, xr, box = chunk(step, k), xs[step], outs[step]

        def block(p, s):
            number = tab_sm[k, 0, step * 256 + p * 64 + s * 32]
            return source[jnp.maximum(number, 0)]

        sems = (y_send.at[step, k], x_recv.at[step, k])
        box[k, 2] = block(2, 0)
        send(box.at[k, 2], relays[step].at[k, 0], sems[0], r_recv.at[step, k, 0], y_up)
        box[k, 3] = block(2, 1)
        send(box.at[k, 3], relays[step].at[k, 1], sems[0], r_recv.at[step, k, 1], y_down)
        for p, dev in ((1, y_up), (3, y_down)):
            first = 0 if p == 1 else 4
            box[k, first] = block(p, 0)
            box[k, first + 1] = block(p, 1)
            send_cut(
                box.at[k, pl.ds(first, 2)], xr.at[pl.ds(k * 8 + p * 2, 2)], sems[0], sems[1], dev
            )
        later(box.at[k], sems[0])
        xr[k * 8] = block(0, 0)
        xr[k * 8 + 1] = block(0, 1)

    def relay(step, k):
        for s, dev in enumerate((y_up, y_down)):
            here = relays[step].at[k, s]
            landed(here, r_recv.at[step, k, s])
            send(
                here,
                xs[step].at[k * 8 + 4 + s],
                r_send.at[step, k],
                x_recv.at[step, k],
                dev,
            )
        later(relays[step].at[k], r_send.at[step, k])

    def score(step, k):
        xr, centroids = xs[step], (cent, cur1)[step]
        landed(xr.at[pl.ds(k * 8 + 2, 6)], x_recv.at[step, k])
        rows = xr[k * 8 : k * 8 + 8].reshape(8 * PB, D)
        s = lax.dot_general(
            centroids[...], rows, (((1,), (1,)), ((), ())), preferred_element_type=F32
        )
        top = jnp.max(s, axis=0, keepdims=True)
        e = jnp.exp(s - top)
        scores[k] = e
        tops[k] = top
        total = jnp.sum(e, axis=0, keepdims=True)
        lse = top + jnp.log(total)
        for i in range(2):
            lses[step][i, k : k + 1, :] = lse[:, i * 128 : (i + 1) * 128]

    low = lax.broadcasted_iota(jnp.int32, (1, 128), 1) < 64
    group = lax.broadcasted_iota(jnp.int32, (1, 128), 1) >> 5

    def over_groups(op, value):
        value = op(value, pltpu.roll(value, 64, 1))
        return op(value, pltpu.roll(value, 32, 1))

    def block_ids(step):
        return [
            tab_in[:, :, step * 256 + i * 128 : step * 256 + i * 128 + 128].reshape(8, 128)
            for i in range(2)
        ]

    def share(step):
        for p in range(1, NY):
            send(
                lses[step].at[p >> 1],
                stats[step].at[p],
                st_sem.at[step, 0],
                st_sem.at[step, 1],
                at_cluster(0, -p),
            )
        stats[step][0] = lses[step][0]
        later(stats[step].at[pl.ds(1, 3)], st_sem.at[step, 0])

    def partial(step):
        got = stats[step]
        landed(got.at[pl.ds(1, 3)], st_sem.at[step, 1])
        have = [jnp.where(low, got[2 * i], got[2 * i + 1]) for i in range(2)]
        ids = block_ids(step)
        packed = [jnp.full((8, 128), -BIG, F32) for _ in range(2)]
        for b in range(NB):
            mine = [ids[i] == b for i in range(2)]
            masked = [jnp.where(mine[i], have[i], -BIG) for i in range(2)]
            top = over_groups(jnp.maximum, jnp.maximum(masked[0], masked[1]))
            each = [jnp.where(mine[i], jnp.exp(have[i] - top), 0.0) for i in range(2)]
            total = over_groups(jnp.add, each[0] + each[1])
            value = jnp.where(total > 0.0, top + jnp.log(total), -BIG)
            packed[b >> 2] = jnp.where(group == (b & 3), value, packed[b >> 2])
        out = sent_parts[step]
        for i in range(2):
            out[i * 8 : i * 8 + 8, :] = packed[i]
        for j in range(1, NZ):
            send(
                out,
                parts_in[step].at[j],
                st_sem.at[step, 2],
                st_sem.at[step, 3],
                at_cluster(j, 0),
            )
        later(parts_in[step].at[pl.ds(1, 7)], st_sem.at[step, 2])

    def whole(step):
        into = parts_in[step]
        landed(into.at[pl.ds(1, 7)], st_sem.at[step, 3])
        ids = block_ids(step)
        shift = [jnp.full((8, 128), BIG, F32) for _ in range(2)]
        for i in range(2):
            rows = slice(i * 8, i * 8 + 8)
            seen = [sent_parts[step][rows, :]]
            for j in range(1, NZ):
                seen.append(pltpu.roll(into[j, rows, :], j, 0))
            top = seen[0]
            for j in range(1, NZ):
                top = jnp.maximum(top, seen[j])
            total = jnp.exp(seen[0] - top)
            for j in range(1, NZ):
                total = total + jnp.exp(seen[j] - top)
            value = top + jnp.log(total)
            for b in range(4):
                spread = over_groups(jnp.maximum, jnp.where(group == b, value, -BIG))
                for t in range(2):
                    shift[t] = jnp.where(ids[t] == i * 4 + b, spread, shift[t])
        out, back = sent_shifts[step], shifts[step]
        for t in range(2):
            out[t] = shift[t]
        back[0] = shift[0]
        for p in range(1, NY):
            send(
                out.at[p >> 1],
                back.at[p],
                st_sem.at[step, 4],
                st_sem.at[step, 5],
                at_cluster(0, p),
            )
        later(back.at[pl.ds(1, 3)], st_sem.at[step, 4])

    def weigh(step):
        back = shifts[step]
        landed(back.at[pl.ds(1, 3)], st_sem.at[step, 5])
        for k in range(NZ):
            for t in range(2):
                shift = jnp.where(low, back[2 * t, k : k + 1, :], back[2 * t + 1, k : k + 1, :])
                lanes = pl.ds(k * 256 + t * 128, 128)
                scale = jnp.exp(tops[k, :, t * 128 : (t + 1) * 128] - shift)
                w[:, lanes] = (scores[k, :, t * 128 : (t + 1) * 128] * scale).astype(BF16)

    def half_sums(which, n):
        rows = w[pl.ds(pl.multiple_of(which * 256, 256), 256), :]
        cols = xs[0][:, :, n * 256 : (n + 1) * 256].reshape(64 * PB, 256)
        return jnp.dot(rows, cols, preferred_element_type=F32)

    def rows64(at, count=64, shift=0):
        return pl.ds(pl.multiple_of(at * 64 + shift, 32), count)

    def rf(n):
        psend[n] = half_sums(1 - core, n)
        send(psend.at[n], precv.at[n], dp_send.at[n], dp_recv.at[n], dev_core)
        later(psend.at[n], dp_send.at[n])

    def ro(n):
        phold[n] = half_sums(core, n)

    def rc(n):
        landed(precv.at[n], dp_recv.at[n])
        far = rows64(xo)
        phold[n, far, :] = phold[n, far, :] + precv[n, far, :]
        sides = ((rows64(xo, 32), dev_xp), (rows64(xo, 32, 32), dev_xm))
        for i, (part, dev) in enumerate(sides):
            sems = dp_send.at[4 + 4 * i + n], dp_recv.at[4 + 4 * i + n]
            send(phold.at[n, part, :], h1.at[i, n], sems[0], sems[1], dev)
            later(h1.at[i, n], sems[0])
        for at in (xp, xm, x):
            near = rows64(at)
            phold[n, near, :] = phold[n, near, :] + precv[n, near, :]
        for i, (at, shift, dev) in enumerate(((xp, 32, dev_xp), (xm, 0, dev_xm))):
            second_hop(n, i, at, shift, dev)

    def second_hop(n, i, at, shift, dev):
        sems = dp_send.at[12 + 4 * i + n], dp_recv.at[12 + 4 * i + n]
        src = phold.at[n, rows64(at, 32, shift), :]
        send(src, h2.at[i, n, pl.ds(shift, 32)], sems[0], sems[1], dev)

    def rh(n):
        for i, (at, shift, dev) in enumerate(((xp, 0, dev_xp), (xm, 32, dev_xm))):
            landed(h1.at[i, n], dp_recv.at[4 + 4 * i + n])
            part = rows64(at, 32, shift)
            phold[n, part, :] = phold[n, part, :] + h1[i, n]
            second_hop(n, i, at, shift, dev)
            later(h2.at[i, n], dp_send.at[12 + 4 * i + n])

    def cur_rows(which_core, at, count=64, shift=0):
        return pl.ds(pl.multiple_of(which_core * 256 + at * 64 + shift, 32), count)

    def update():
        for n in range(4):
            landed(h2.at[0, n], dp_recv.at[12 + n])
            landed(h2.at[1, n], dp_recv.at[16 + n])
        own = rows64(x)
        mine = cur_rows(core, x)
        v = [
            cent[mine, n * 256 : (n + 1) * 256].astype(F32)
            + (phold[n, own, :] + h2[0, n] + h2[1, n])
            for n in range(4)
        ]
        square = sum(jnp.sum(part * part, axis=1, keepdims=True) for part in v)
        norm = jnp.sqrt(square + 1e-06)
        for n in range(4):
            cur1[mine, n * 256 : (n + 1) * 256] = (v[n] / norm).astype(BF16)
        pieces = ((0, dev_xp, 20), (32, dev_xm, 21), (32, dev_xp, 22), (0, dev_xm, 23))
        for i, (shift, dev, sem) in enumerate(pieces):
            part = cur1.at[cur_rows(core, x, 32, shift)]
            send(part, part, dp_send.at[sem], dp_recv.at[sem], dev)
            later(part, dp_send.at[sem])
            if i == 1:
                to_core(cur1.at[mine], 24)

    def to_core(part, sem):
        send(part, part, dp_send.at[sem], dp_recv.at[26], dev_core)
        later(part, dp_send.at[sem])

    def gather1():
        for i, (at, shift, dev) in enumerate(((xm, 0, dev_xp), (xp, 32, dev_xm))):
            part = cur1.at[cur_rows(core, at, 32, shift)]
            landed(part, dp_recv.at[20 + i])
            send(part, part, dp_send.at[25 + i], dp_recv.at[24 + i], dev)
            later(part, dp_send.at[25 + i])
            to_core(part, 27 + i)

    def gather1b():
        for i, (at, shift) in enumerate(((xm, 32), (xp, 0))):
            part = cur1.at[cur_rows(core, at, 32, shift)]
            landed(part, dp_recv.at[22 + i])
            to_core(part, 29 + i)

    def gather2():
        for i, shift in enumerate((0, 32)):
            part = cur1.at[cur_rows(core, xo, 32, shift)]
            landed(part, dp_recv.at[24 + i])
            to_core(part, 31 + i)

    def gather3():
        other = pl.ds(pl.multiple_of((1 - core) * 256, 256), 256)
        landed(cur1.at[other], dp_recv.at[26])

    def ls(j):
        lanes = pl.ds(pl.multiple_of((xo, xp, xm, x)[j] * 256, 256), 256)
        cols = xs[1][:, :, lanes].reshape(64 * PB, 256)
        part = jnp.dot(w[...], cols, preferred_element_type=F32)
        fb[j, 0] = part[:, :128]
        fb[j, 1] = part[:, 128:]
        fs[j] = fb[j, 1 - core].astype(BF16)
        send(fs.at[j], fr.at[j], fin_send.at[0], fin_recv.at[j], dev_core)
        if j == 3:
            later(fs, fin_send.at[0])

    def both(j):
        landed(fr.at[j], fin_recv.at[j])
        return fb[j, core] + fr[j].astype(F32)

    def lq():
        g[0] = both(0).astype(BF16)
        for i, dev in enumerate((dev_xp, dev_xm)):
            rows = pl.ds(256 * i, 256)
            send(g.at[0, rows], q.at[i], fin_send.at[2 + i], fin_recv.at[5 + i], dev)
            later(q.at[i], fin_send.at[2 + i])

    def last_hop(i, rows):
        dev = (dev_xp, dev_xm)[i]
        send(g.at[1 + i, rows], u.at[i, rows], fin_send.at[4 + i], fin_recv.at[7 + i], dev)

    def lv():
        for i in range(2):
            part = both(1 + i)
            rest = pl.ds(256 - 256 * i, 256)
            fb[1 + i, core] = part
            g[1 + i, rest] = part[256 - 256 * i : 512 - 256 * i].astype(BF16)
            last_hop(i, rest)

    def lu():
        for i in range(2):
            landed(q.at[i], fin_recv.at[5 + i])
            rows = pl.ds(256 * i, 256)
            g[1 + i, rows] = (fb[1 + i, core, rows, :] + q[i].astype(F32)).astype(BF16)
            last_hop(i, rows)
            later(u.at[i], fin_send.at[4 + i])

    def cnt():
        ones = jnp.ones((8, 64 * PB), BF16)
        count = lax.dot_general(
            ones, w[...], (((1,), (1,)), ((), ())), preferred_element_type=F32
        )
        cnts[dp] = count[0:1]
        for j in range(1, NX * NC):
            send(
                cnts.at[dp],
                cnts.at[dp],
                fin_send.at[1],
                fin_recv.at[4],
                {"dp": lax.rem(dp + j, NX * NC)},
            )
        later(cnts.at[pl.ds(0, 7)], fin_send.at[1])

    def own():
        fb[3, core] = both(3)
        landed(cnts.at[pl.ds(0, 7)], fin_recv.at[4])
        count = cnts[0]
        for j in range(1, NX * NC):
            count = count + cnts[j]
        for j in range(4):
            out_counts[j : j + 1, :] = count[:, j * 128 : (j + 1) * 128]
        drain()

    def fin():
        landed(u.at[0], fin_recv.at[7])
        landed(u.at[1], fin_recv.at[8])
        out_sums[...] = fb[3, core] + (u[0].astype(F32) + u[1].astype(F32))

    parts = dict(
        zs=z_start,
        ze=z_event,
        pick=pick,
        relay=relay,
        score=score,
        share=share,
        partial=partial,
        whole=whole,
        weigh=weigh,
        rf=rf,
        ro=ro,
        rc=rc,
        rh=rh,
        update=update,
        gather1=gather1,
        gather1b=gather1b,
        gather2=gather2,
        gather3=gather3,
        ls=ls,
        lq=lq,
        lu=lu,
        lv=lv,
        cnt=cnt,
        own=own,
        fin=fin,
    )
    for name, *numbers in SCHEDULE:
        parts[name](*numbers)
        if (name, *numbers) == ("zs", 0, 1):
            tables()
            for load in loads:
                load.wait()
        if (name, *numbers) == ("relay", 0, 0):
            tables_in()


def on_device(points, candidates, centroids):
    vmem, hbm = pl.BlockSpec(memory_space=pltpu.VMEM), pl.BlockSpec(memory_space=pl.ANY)
    sem = pltpu.SemaphoreType.DMA
    steps = points.shape[0]
    sums, counts = pl.pallas_call(
        kernel,
        out_shape=(
            jax.ShapeDtypeStruct((CBS, D // (NX * NC)), F32),
            jax.ShapeDtypeStruct((4, 128), F32),
        ),
        in_specs=[hbm, pl.BlockSpec(memory_space=pltpu.SMEM), hbm],
        out_specs=(vmem, vmem),
        scratch_shapes=[
            pltpu.VMEM((steps, NB, PB, D), BF16),
            pltpu.VMEM((CBS, D), BF16),
            [pltpu.VMEM((NB, PB, D), BF16) for _ in range(7 * steps)],
            [pltpu.VMEM((64, PB, D), BF16) for _ in range(steps)],
            [pltpu.VMEM((NZ, 6, PB, D), BF16) for _ in range(steps)],
            [pltpu.VMEM((NZ, 2, PB, D), BF16) for _ in range(steps)],
            pltpu.VMEM((NZ, 1, 512), jnp.int32),
            pltpu.VMEM((NZ, 1, 512), jnp.int32),
            pltpu.SMEM((NZ, 1, 512), jnp.int32),
            pltpu.VMEM((NZ, CBS, 256), F32),
            pltpu.VMEM((NZ, 1, 256), F32),
            pltpu.VMEM((CBS, 64 * PB), BF16),
            [pltpu.VMEM((2, 8, 128), F32) for _ in range(steps)],
            [pltpu.VMEM((4, 8, 128), F32) for _ in range(steps)],
            [pltpu.VMEM((16, 128), F32) for _ in range(steps)],
            [pltpu.VMEM((NZ, 16, 128), F32) for _ in range(steps)],
            [pltpu.VMEM((2, 8, 128), F32) for _ in range(steps)],
            [pltpu.VMEM((4, 8, 128), F32) for _ in range(steps)],
            pltpu.VMEM((4, 256, 256), F32),
            pltpu.VMEM((4, 256, 256), F32),
            pltpu.VMEM((4, 256, 256), F32),
            pltpu.VMEM((2, 4, 32, 256), F32),
            pltpu.VMEM((2, 4, 64, 256), F32),
            pltpu.VMEM((CBS, D), BF16),
            pltpu.VMEM((4, 2, CBS, 128), F32),
            pltpu.VMEM((4, CBS, 128), BF16),
            pltpu.VMEM((4, CBS, 128), BF16),
            pltpu.VMEM((3, CBS, 128), BF16),
            pltpu.VMEM((2, 256, 128), BF16),
            pltpu.VMEM((2, CBS, 128), BF16),
            pltpu.VMEM((NX * NC, 1, CBS), F32),
            sem((steps, 2, 7)),
            sem((steps, 2, 7)),
            sem((steps, NZ)),
            sem((steps, NZ)),
            sem((steps, NZ, 2)),
            sem((steps, NZ)),
            sem((steps, 6)),
            sem((3,)),
            sem((33,)),
            sem((27,)),
            sem((6,)),
            sem((9,)),
            sem((2,)),
        ],
        compiler_params=pltpu.CompilerParams(
            collective_id=0, has_side_effects=True, vmem_limit_bytes=56 * 1024 * 1024
        ),
    )(points.reshape(steps, NB, PB, D), jnp.transpose(candidates, (0, 2, 1)), centroids)
    return sums, counts.reshape(CBS)


def solution(mesh):
    placed = (
        P(None, ("dp", "cluster"), None),
        P(None, ("dp", "cluster"), None),
        P("cluster", None),
    )
    return jax.shard_map(
        on_device,
        mesh=mesh,
        in_specs=placed,
        out_specs=(P("cluster", "dp"), P("cluster")),
        check_vma=False,
    )
```

```python
import jax
import jax.numpy as jnp
from jax import lax
from jax.experimental import pallas as pl
from jax.experimental.pallas import tpu as pltpu
from jax.sharding import PartitionSpec as P

MESH = pl.DeviceIdType.MESH
F32 = jnp.float32
BF16 = jnp.bfloat16
BIG = 3.0e38
NZ, NY, NX, NC = 8, 4, 4, 2
NB, PB, D, CBS = 8, 32, 1024, 512
PLUS = ((1, 0), (1, 1), (2, 0), (2, 1), (3, 0), (3, 1), (4, 0))
MINUS = ((7, 1), (7, 0), (6, 1), (6, 0), (5, 1), (5, 0), (4, 1))
SCHEDULE = (
    ("zs", 0, 0), ("pick", 0, 0), ("pick", 1, 0), ("zs", 0, 1), ("relay", 0, 0), ("ze", 0, 0, 0), ("ze", 0, 1, 0),
    ("relay", 1, 0), ("score", 0, 0), ("ze", 0, 0, 1), ("ze", 0, 1, 1), ("pick", 0, 1), ("pick", 0, 7),
    ("relay", 0, 1), ("ze", 0, 0, 2), ("ze", 0, 1, 2), ("relay", 0, 7), ("ze", 0, 0, 3), ("ze", 0, 1, 3),
    ("pick", 0, 2), ("pick", 0, 6), ("score", 0, 1), ("score", 0, 7), ("relay", 0, 2), ("ze", 0, 0, 4),
    ("ze", 0, 1, 4), ("relay", 0, 6), ("ze", 0, 0, 5), ("pick", 0, 3), ("ze", 0, 1, 5), ("zs", 1, 0), ("pick", 0, 5),
    ("score", 0, 2), ("score", 0, 6), ("relay", 0, 3), ("ze", 0, 0, 6), ("ze", 0, 1, 6), ("zs", 1, 1), ("pick", 0, 4),
    ("relay", 0, 5), ("ze", 1, 0, 0), ("ze", 1, 1, 0), ("score", 0, 3), ("relay", 0, 4), ("ze", 1, 0, 1),
    ("ze", 1, 1, 1), ("pick", 1, 1), ("pick", 1, 7), ("score", 0, 5), ("score", 0, 4), ("share", 0), ("relay", 1, 1),
    ("partial", 0), ("ze", 1, 0, 2), ("ze", 1, 1, 2), ("relay", 1, 7), ("whole", 0), ("ze", 1, 0, 3), ("ze", 1, 1, 3),
    ("pick", 1, 2), ("pick", 1, 6), ("weigh", 0), ("rf", 0), ("ro", 0), ("relay", 1, 2), ("rf", 1), ("ro", 1),
    ("rc", 0), ("rf", 2), ("ro", 2), ("rc", 1), ("ze", 1, 0, 4), ("ze", 1, 1, 4), ("rh", 0), ("rf", 3),
    ("relay", 1, 6), ("rc", 2), ("rh", 1), ("ro", 3), ("rc", 3), ("rh", 2), ("ze", 1, 0, 5), ("pick", 1, 3),
    ("ze", 1, 1, 5), ("pick", 1, 5), ("rh", 3), ("relay", 1, 3), ("update",), ("ze", 1, 0, 6), ("ze", 1, 1, 6),
    ("pick", 1, 4), ("gather1",), ("relay", 1, 5), ("gather1b",), ("gather2",), ("gather3",), ("score", 1, 0),
    ("score", 1, 1), ("score", 1, 7), ("relay", 1, 4), ("score", 1, 2), ("score", 1, 6), ("score", 1, 3),
    ("score", 1, 5), ("score", 1, 4), ("share", 1), ("partial", 1), ("whole", 1), ("weigh", 1), ("ls", 0), ("ls", 1),
    ("ls", 2), ("lq",), ("ls", 3), ("cnt",), ("lv",), ("lu",), ("own",), ("fin",),
)


def kernel(
    pts_hbm,
    cands,
    cent_hbm,
    out_sums,
    out_counts,
    pts,
    cent,
    zbufs,
    xs,
    outs,
    relays,
    tab,
    tab_in,
    tab_sm,
    scores,
    tops,
    w,
    lses,
    stats,
    sent_parts,
    parts_in,
    sent_shifts,
    shifts,
    psend,
    precv,
    phold,
    h1,
    h2,
    cur1,
    fb,
    fs,
    fr,
    g,
    q,
    u,
    cnts,
    z_send,
    z_recv,
    y_send,
    x_recv,
    r_recv,
    r_send,
    st_sem,
    tab_sem,
    dp_send,
    dp_recv,
    fin_send,
    fin_recv,
    load_sem,
):
    dp = lax.axis_index("dp")
    cl = lax.axis_index("cluster")
    x, core = lax.div(dp, NC), lax.rem(dp, NC)
    z, y = lax.div(cl, NY), lax.rem(cl, NY)

    sign = 1 - 2 * core

    def at_cluster(k, dy):
        return {"cluster": lax.rem(z + sign * k + NZ, NZ) * NY + lax.rem(y + dy + NY, NY)}

    xp, xm, xo = lax.rem(x + 1, NX), lax.rem(x + 3, NX), lax.rem(x + 2, NX)
    dev_xp, dev_xm = {"dp": xp * NC + core}, {"dp": xm * NC + core}
    dev_core = {"dp": x * NC + 1 - core}
    z_devs = at_cluster(1, 0), at_cluster(-1, 0)
    y_up, y_down = at_cluster(0, 1), at_cluster(0, -1)

    loads = [
        pltpu.make_async_copy(pts_hbm, pts, load_sem.at[0]),
        pltpu.make_async_copy(cent_hbm, cent, load_sem.at[1]),
    ]
    for load in loads:
        load.start()

    barrier = pltpu.get_barrier_semaphore()
    for peer in [at_cluster(k, 0) for k in range(1, NZ)] + [at_cluster(0, p) for p in range(1, NY)]:
        pl.semaphore_signal(barrier, inc=1, device_id=peer, device_id_type=MESH)
    for j in range(1, NX * NC):
        pl.semaphore_signal(
            barrier, inc=1, device_id={"dp": lax.rem(dp + j, NX * NC)}, device_id_type=MESH
        )
    pl.semaphore_wait(barrier, NZ - 1 + NY - 1 + NX * NC - 1)

    drains = []

    def send(src, dst, ssem, rsem, dev):
        copy = pltpu.make_async_remote_copy(
            src_ref=src,
            dst_ref=dst,
            send_sem=ssem,
            recv_sem=rsem,
            device_id=dev,
            device_id_type=MESH,
        )
        copy.start()
        return copy

    def landed(ref, sem):
        pltpu.make_async_copy(ref, ref, sem).wait()

    def later(ref, sem):
        drains.append(lambda: landed(ref, sem))

    def drain():
        for wait in drains:
            wait()
        drains.clear()

    def half(ref, h):
        return ref.at[pl.ds(h * 4, 4)]

    def chunk(step, k):
        return pts.at[step] if k == 0 else zbufs[step * 7 + k - 1]

    def z_start(step, i):
        for d, order in enumerate((PLUS, MINUS)):
            k, h = order[i]
            src = half(pts_hbm.at[step], h)
            dst = half(chunk(step, k), h)
            send(src, dst, z_send.at[step, d, i], z_recv.at[step, d, i], z_devs[d])
            later(src, z_send.at[step, d, i])

    def z_event(step, d, i):
        order = (PLUS, MINUS)[d]
        k, h = order[i]
        here = half(chunk(step, k), h)
        landed(here, z_recv.at[step, d, i])
        if i < 5:
            dst = half(chunk(step, order[i + 2][0]), h)
            send(here, dst, z_send.at[step, d, i + 2], z_recv.at[step, d, i + 2], z_devs[d])
            later(here, z_send.at[step, d, i + 2])

    def tables():
        row = lax.broadcasted_iota(jnp.int32, (8, 128), 0)
        lane = lax.broadcasted_iota(jnp.int32, (8, 128), 1)
        oz = (z + sign * row) & (NZ - 1)
        second = ((lane >> 5) & 1) == 1
        for step in range(2):
            for t in range(2):
                owner = oz * NY + ((y + t * 2 + (lane >> 6)) & (NY - 1))
                first = jnp.full((8, 128), NB, jnp.int32)
                last = jnp.full((8, 128), -1, jnp.int32)
                for b in range(NB):
                    hit = owner == cands[step, 0, b]
                    for j in range(1, 4):
                        hit = hit | (owner == cands[step, j, b])
                    last = jnp.where(hit, b, last)
                    first = jnp.minimum(first, jnp.where(hit, b, NB))
                lone = jnp.where(first < NB, first, -1)
                bid = jnp.where(second, jnp.where(last > first, last, -1), lone)
                off = step * 256 + t * 128
                tab[:, :, off : off + 128] = bid.reshape(8, 1, 128)
        for k in range(1, NZ):
            send(tab.at[k], tab_in.at[k], tab_sem.at[0], tab_sem.at[1], at_cluster(k, 0))
        later(tab_in.at[pl.ds(1, 7)], tab_sem.at[0])
        tab_in[0] = tab[0]
        to_scalars(tab, 0, 1)

    def to_scalars(table, first, count):
        rows = pl.ds(first, count)
        copy = pltpu.make_async_copy(table.at[rows], tab_sm.at[rows], tab_sem.at[2])
        copy.start()
        copy.wait()

    def tables_in():
        landed(tab_in.at[pl.ds(1, 7)], tab_sem.at[1])
        to_scalars(tab_in, 1, 7)

    def pick(step, k):
        source, xr, box = chunk(step, k), xs[step], outs[step]

        def block(p, s):
            number = tab_sm[k, 0, step * 256 + p * 64 + s * 32]
            return source[jnp.maximum(number, 0)]

        sems = (y_send.at[step, k], x_recv.at[step, k])
        box[k, 2] = block(2, 0)
        send(box.at[k, 2], relays[step].at[k, 0], sems[0], r_recv.at[step, k, 0], y_up)
        box[k, 3] = block(2, 1)
        send(box.at[k, 3], relays[step].at[k, 1], sems[0], r_recv.at[step, k, 1], y_down)
        for p, dev in ((1, y_up), (3, y_down)):
            first = 0 if p == 1 else 4
            box[k, first] = block(p, 0)
            box[k, first + 1] = block(p, 1)
            send(
                box.at[k, pl.ds(first, 2)], xr.at[pl.ds(k * 8 + p * 2, 2)], sems[0], sems[1], dev
            )
        later(box.at[k], sems[0])
        xr[k * 8] = block(0, 0)
        xr[k * 8 + 1] = block(0, 1)

    def relay(step, k):
        for s, dev in enumerate((y_up, y_down)):
            here = relays[step].at[k, s]
            landed(here, r_recv.at[step, k, s])
            send(
                here,
                xs[step].at[k * 8 + 4 + s],
                r_send.at[step, k],
                x_recv.at[step, k],
                dev,
            )
        later(relays[step].at[k], r_send.at[step, k])

    def score(step, k):
        xr, centroids = xs[step], (cent, cur1)[step]
        landed(xr.at[pl.ds(k * 8 + 2, 6)], x_recv.at[step, k])
        rows = xr[k * 8 : k * 8 + 8].reshape(8 * PB, D)
        s = lax.dot_general(
            centroids[...], rows, (((1,), (1,)), ((), ())), preferred_element_type=F32
        )
        top = jnp.max(s, axis=0, keepdims=True)
        e = jnp.exp(s - top)
        scores[k] = e
        tops[k] = top
        total = jnp.sum(e, axis=0, keepdims=True)
        lse = top + jnp.log(total)
        for i in range(2):
            lses[step][i, k : k + 1, :] = lse[:, i * 128 : (i + 1) * 128]

    low = lax.broadcasted_iota(jnp.int32, (1, 128), 1) < 64
    group = lax.broadcasted_iota(jnp.int32, (1, 128), 1) >> 5

    def over_groups(op, value):
        value = op(value, pltpu.roll(value, 64, 1))
        return op(value, pltpu.roll(value, 32, 1))

    def block_ids(step):
        return [
            tab_in[:, :, step * 256 + i * 128 : step * 256 + i * 128 + 128].reshape(8, 128)
            for i in range(2)
        ]

    def share(step):
        for p in range(1, NY):
            send(
                lses[step].at[p >> 1],
                stats[step].at[p],
                st_sem.at[step, 0],
                st_sem.at[step, 1],
                at_cluster(0, -p),
            )
        stats[step][0] = lses[step][0]
        later(stats[step].at[pl.ds(1, 3)], st_sem.at[step, 0])

    def partial(step):
        got = stats[step]
        landed(got.at[pl.ds(1, 3)], st_sem.at[step, 1])
        have = [jnp.where(low, got[2 * i], got[2 * i + 1]) for i in range(2)]
        ids = block_ids(step)
        packed = [jnp.full((8, 128), -BIG, F32) for _ in range(2)]
        for b in range(NB):
            mine = [ids[i] == b for i in range(2)]
            masked = [jnp.where(mine[i], have[i], -BIG) for i in range(2)]
            top = over_groups(jnp.maximum, jnp.maximum(masked[0], masked[1]))
            each = [jnp.where(mine[i], jnp.exp(have[i] - top), 0.0) for i in range(2)]
            total = over_groups(jnp.add, each[0] + each[1])
            value = jnp.where(total > 0.0, top + jnp.log(total), -BIG)
            packed[b >> 2] = jnp.where(group == (b & 3), value, packed[b >> 2])
        out = sent_parts[step]
        for i in range(2):
            out[i * 8 : i * 8 + 8, :] = packed[i]
        for j in range(1, NZ):
            send(
                out,
                parts_in[step].at[j],
                st_sem.at[step, 2],
                st_sem.at[step, 3],
                at_cluster(j, 0),
            )
        later(parts_in[step].at[pl.ds(1, 7)], st_sem.at[step, 2])

    def whole(step):
        into = parts_in[step]
        landed(into.at[pl.ds(1, 7)], st_sem.at[step, 3])
        ids = block_ids(step)
        shift = [jnp.full((8, 128), BIG, F32) for _ in range(2)]
        for i in range(2):
            rows = slice(i * 8, i * 8 + 8)
            seen = [sent_parts[step][rows, :]]
            for j in range(1, NZ):
                seen.append(pltpu.roll(into[j, rows, :], j, 0))
            top = seen[0]
            for j in range(1, NZ):
                top = jnp.maximum(top, seen[j])
            total = jnp.exp(seen[0] - top)
            for j in range(1, NZ):
                total = total + jnp.exp(seen[j] - top)
            value = top + jnp.log(total)
            for b in range(4):
                spread = over_groups(jnp.maximum, jnp.where(group == b, value, -BIG))
                for t in range(2):
                    shift[t] = jnp.where(ids[t] == i * 4 + b, spread, shift[t])
        out, back = sent_shifts[step], shifts[step]
        for t in range(2):
            out[t] = shift[t]
        back[0] = shift[0]
        for p in range(1, NY):
            send(
                out.at[p >> 1],
                back.at[p],
                st_sem.at[step, 4],
                st_sem.at[step, 5],
                at_cluster(0, p),
            )
        later(back.at[pl.ds(1, 3)], st_sem.at[step, 4])

    def weigh(step):
        back = shifts[step]
        landed(back.at[pl.ds(1, 3)], st_sem.at[step, 5])
        for k in range(NZ):
            for t in range(2):
                shift = jnp.where(low, back[2 * t, k : k + 1, :], back[2 * t + 1, k : k + 1, :])
                lanes = pl.ds(k * 256 + t * 128, 128)
                scale = jnp.exp(tops[k, :, t * 128 : (t + 1) * 128] - shift)
                w[:, lanes] = (scores[k, :, t * 128 : (t + 1) * 128] * scale).astype(BF16)

    def half_sums(which, n):
        rows = w[pl.ds(pl.multiple_of(which * 256, 256), 256), :]
        cols = xs[0][:, :, n * 256 : (n + 1) * 256].reshape(64 * PB, 256)
        return jnp.dot(rows, cols, preferred_element_type=F32)

    def rows64(at, count=64, shift=0):
        return pl.ds(pl.multiple_of(at * 64 + shift, 32), count)

    def rf(n):
        psend[n] = half_sums(1 - core, n)
        send(psend.at[n], precv.at[n], dp_send.at[n], dp_recv.at[n], dev_core)
        later(psend.at[n], dp_send.at[n])

    def ro(n):
        phold[n] = half_sums(core, n)

    def rc(n):
        landed(precv.at[n], dp_recv.at[n])
        far = rows64(xo)
        phold[n, far, :] = phold[n, far, :] + precv[n, far, :]
        sides = ((rows64(xo, 32), dev_xp), (rows64(xo, 32, 32), dev_xm))
        for i, (part, dev) in enumerate(sides):
            sems = dp_send.at[4 + 4 * i + n], dp_recv.at[4 + 4 * i + n]
            send(phold.at[n, part, :], h1.at[i, n], sems[0], sems[1], dev)
            later(h1.at[i, n], sems[0])
        for at in (xp, xm, x):
            near = rows64(at)
            phold[n, near, :] = phold[n, near, :] + precv[n, near, :]
        for i, (at, shift, dev) in enumerate(((xp, 32, dev_xp), (xm, 0, dev_xm))):
            second_hop(n, i, at, shift, dev)

    def second_hop(n, i, at, shift, dev):
        sems = dp_send.at[12 + 4 * i + n], dp_recv.at[12 + 4 * i + n]
        src = phold.at[n, rows64(at, 32, shift), :]
        send(src, h2.at[i, n, pl.ds(shift, 32)], sems[0], sems[1], dev)

    def rh(n):
        for i, (at, shift, dev) in enumerate(((xp, 0, dev_xp), (xm, 32, dev_xm))):
            landed(h1.at[i, n], dp_recv.at[4 + 4 * i + n])
            part = rows64(at, 32, shift)
            phold[n, part, :] = phold[n, part, :] + h1[i, n]
            second_hop(n, i, at, shift, dev)
            later(h2.at[i, n], dp_send.at[12 + 4 * i + n])

    def cur_rows(which_core, at, count=64, shift=0):
        return pl.ds(pl.multiple_of(which_core * 256 + at * 64 + shift, 32), count)

    def update():
        for n in range(4):
            landed(h2.at[0, n], dp_recv.at[12 + n])
            landed(h2.at[1, n], dp_recv.at[16 + n])
        own = rows64(x)
        mine = cur_rows(core, x)
        v = [
            cent[mine, n * 256 : (n + 1) * 256].astype(F32)
            + (phold[n, own, :] + h2[0, n] + h2[1, n])
            for n in range(4)
        ]
        square = sum(jnp.sum(part * part, axis=1, keepdims=True) for part in v)
        norm = jnp.sqrt(square + 1e-06)
        for n in range(4):
            cur1[mine, n * 256 : (n + 1) * 256] = (v[n] / norm).astype(BF16)
        pieces = ((0, dev_xp, 20), (32, dev_xm, 21), (32, dev_xp, 22), (0, dev_xm, 23))
        for i, (shift, dev, sem) in enumerate(pieces):
            part = cur1.at[cur_rows(core, x, 32, shift)]
            send(part, part, dp_send.at[sem], dp_recv.at[sem], dev)
            later(part, dp_send.at[sem])
            if i == 1:
                to_core(cur1.at[mine], 24)

    def to_core(part, sem):
        send(part, part, dp_send.at[sem], dp_recv.at[26], dev_core)
        later(part, dp_send.at[sem])

    def gather1():
        for i, (at, shift, dev) in enumerate(((xm, 0, dev_xp), (xp, 32, dev_xm))):
            part = cur1.at[cur_rows(core, at, 32, shift)]
            landed(part, dp_recv.at[20 + i])
            send(part, part, dp_send.at[25 + i], dp_recv.at[24 + i], dev)
            later(part, dp_send.at[25 + i])
            to_core(part, 27 + i)

    def gather1b():
        for i, (at, shift) in enumerate(((xm, 32), (xp, 0))):
            part = cur1.at[cur_rows(core, at, 32, shift)]
            landed(part, dp_recv.at[22 + i])
            to_core(part, 29 + i)

    def gather2():
        for i, shift in enumerate((0, 32)):
            part = cur1.at[cur_rows(core, xo, 32, shift)]
            landed(part, dp_recv.at[24 + i])
            to_core(part, 31 + i)

    def gather3():
        other = pl.ds(pl.multiple_of((1 - core) * 256, 256), 256)
        landed(cur1.at[other], dp_recv.at[26])

    def ls(j):
        lanes = pl.ds(pl.multiple_of((xo, xp, xm, x)[j] * 256, 256), 256)
        cols = xs[1][:, :, lanes].reshape(64 * PB, 256)
        part = jnp.dot(w[...], cols, preferred_element_type=F32)
        fb[j, 0] = part[:, :128]
        fb[j, 1] = part[:, 128:]
        fs[j] = fb[j, 1 - core].astype(BF16)
        send(fs.at[j], fr.at[j], fin_send.at[0], fin_recv.at[j], dev_core)
        if j == 3:
            later(fs, fin_send.at[0])

    def both(j):
        landed(fr.at[j], fin_recv.at[j])
        return fb[j, core] + fr[j].astype(F32)

    def lq():
        g[0] = both(0).astype(BF16)
        for i, dev in enumerate((dev_xp, dev_xm)):
            rows = pl.ds(256 * i, 256)
            send(g.at[0, rows], q.at[i], fin_send.at[2 + i], fin_recv.at[5 + i], dev)
            later(q.at[i], fin_send.at[2 + i])

    def last_hop(i, rows):
        dev = (dev_xp, dev_xm)[i]
        send(g.at[1 + i, rows], u.at[i, rows], fin_send.at[4 + i], fin_recv.at[7 + i], dev)

    def lv():
        for i in range(2):
            part = both(1 + i)
            rest = pl.ds(256 - 256 * i, 256)
            fb[1 + i, core] = part
            g[1 + i, rest] = part[256 - 256 * i : 512 - 256 * i].astype(BF16)
            last_hop(i, rest)

    def lu():
        for i in range(2):
            landed(q.at[i], fin_recv.at[5 + i])
            rows = pl.ds(256 * i, 256)
            g[1 + i, rows] = (fb[1 + i, core, rows, :] + q[i].astype(F32)).astype(BF16)
            last_hop(i, rows)
            later(u.at[i], fin_send.at[4 + i])

    def cnt():
        ones = jnp.ones((8, 64 * PB), BF16)
        count = lax.dot_general(
            ones, w[...], (((1,), (1,)), ((), ())), preferred_element_type=F32
        )
        cnts[dp] = count[0:1]
        for j in range(1, NX * NC):
            send(
                cnts.at[dp],
                cnts.at[dp],
                fin_send.at[1],
                fin_recv.at[4],
                {"dp": lax.rem(dp + j, NX * NC)},
            )
        later(cnts.at[pl.ds(0, 7)], fin_send.at[1])

    def own():
        fb[3, core] = both(3)
        landed(cnts.at[pl.ds(0, 7)], fin_recv.at[4])
        count = cnts[0]
        for j in range(1, NX * NC):
            count = count + cnts[j]
        for j in range(4):
            out_counts[j : j + 1, :] = count[:, j * 128 : (j + 1) * 128]
        drain()

    def fin():
        landed(u.at[0], fin_recv.at[7])
        landed(u.at[1], fin_recv.at[8])
        out_sums[...] = fb[3, core] + (u[0].astype(F32) + u[1].astype(F32))

    parts = dict(
        zs=z_start,
        ze=z_event,
        pick=pick,
        relay=relay,
        score=score,
        share=share,
        partial=partial,
        whole=whole,
        weigh=weigh,
        rf=rf,
        ro=ro,
        rc=rc,
        rh=rh,
        update=update,
        gather1=gather1,
        gather1b=gather1b,
        gather2=gather2,
        gather3=gather3,
        ls=ls,
        lq=lq,
        lu=lu,
        lv=lv,
        cnt=cnt,
        own=own,
        fin=fin,
    )
    for name, *numbers in SCHEDULE:
        parts[name](*numbers)
        if (name, *numbers) == ("zs", 0, 0):
            tables()
            for load in loads:
                load.wait()
        if (name, *numbers) == ("relay", 0, 0):
            tables_in()


def on_device(points, candidates, centroids):
    vmem, hbm = pl.BlockSpec(memory_space=pltpu.VMEM), pl.BlockSpec(memory_space=pl.ANY)
    sem = pltpu.SemaphoreType.DMA
    steps = points.shape[0]
    sums, counts = pl.pallas_call(
        kernel,
        out_shape=(
            jax.ShapeDtypeStruct((CBS, D // (NX * NC)), F32),
            jax.ShapeDtypeStruct((4, 128), F32),
        ),
        in_specs=[hbm, pl.BlockSpec(memory_space=pltpu.SMEM), hbm],
        out_specs=(vmem, vmem),
        scratch_shapes=[
            pltpu.VMEM((steps, NB, PB, D), BF16),
            pltpu.VMEM((CBS, D), BF16),
            [pltpu.VMEM((NB, PB, D), BF16) for _ in range(7 * steps)],
            [pltpu.VMEM((64, PB, D), BF16) for _ in range(steps)],
            [pltpu.VMEM((NZ, 6, PB, D), BF16) for _ in range(steps)],
            [pltpu.VMEM((NZ, 2, PB, D), BF16) for _ in range(steps)],
            pltpu.VMEM((NZ, 1, 512), jnp.int32),
            pltpu.VMEM((NZ, 1, 512), jnp.int32),
            pltpu.SMEM((NZ, 1, 512), jnp.int32),
            pltpu.VMEM((NZ, CBS, 256), F32),
            pltpu.VMEM((NZ, 1, 256), F32),
            pltpu.VMEM((CBS, 64 * PB), BF16),
            [pltpu.VMEM((2, 8, 128), F32) for _ in range(steps)],
            [pltpu.VMEM((4, 8, 128), F32) for _ in range(steps)],
            [pltpu.VMEM((16, 128), F32) for _ in range(steps)],
            [pltpu.VMEM((NZ, 16, 128), F32) for _ in range(steps)],
            [pltpu.VMEM((2, 8, 128), F32) for _ in range(steps)],
            [pltpu.VMEM((4, 8, 128), F32) for _ in range(steps)],
            pltpu.VMEM((4, 256, 256), F32),
            pltpu.VMEM((4, 256, 256), F32),
            pltpu.VMEM((4, 256, 256), F32),
            pltpu.VMEM((2, 4, 32, 256), F32),
            pltpu.VMEM((2, 4, 64, 256), F32),
            pltpu.VMEM((CBS, D), BF16),
            pltpu.VMEM((4, 2, CBS, 128), F32),
            pltpu.VMEM((4, CBS, 128), BF16),
            pltpu.VMEM((4, CBS, 128), BF16),
            pltpu.VMEM((3, CBS, 128), BF16),
            pltpu.VMEM((2, 256, 128), BF16),
            pltpu.VMEM((2, CBS, 128), BF16),
            pltpu.VMEM((NX * NC, 1, CBS), F32),
            sem((steps, 2, 7)),
            sem((steps, 2, 7)),
            sem((steps, NZ)),
            sem((steps, NZ)),
            sem((steps, NZ, 2)),
            sem((steps, NZ)),
            sem((steps, 6)),
            sem((3,)),
            sem((33,)),
            sem((27,)),
            sem((6,)),
            sem((9,)),
            sem((2,)),
        ],
        compiler_params=pltpu.CompilerParams(
            collective_id=0, has_side_effects=True, vmem_limit_bytes=56 * 1024 * 1024
        ),
    )(points.reshape(steps, NB, PB, D), jnp.transpose(candidates, (0, 2, 1)), centroids)
    return sums, counts.reshape(CBS)


def solution(mesh):
    placed = (
        P(None, ("dp", "cluster"), None),
        P(None, ("dp", "cluster"), None),
        P("cluster", None),
    )
    return jax.shard_map(
        on_device,
        mesh=mesh,
        in_specs=placed,
        out_specs=(P("cluster", "dp"), P("cluster")),
        check_vma=False,
    )
```

```python
import jax
import jax.numpy as jnp
from jax import lax
from jax.experimental import pallas as pl
from jax.experimental.pallas import tpu as pltpu
from jax.sharding import PartitionSpec as P

MESH = pl.DeviceIdType.MESH
F32 = jnp.float32
BF16 = jnp.bfloat16
BIG = 3.0e38
NZ, NY, NX, NC = 8, 4, 4, 2
NB, PB, D, CBS = 8, 32, 1024, 512
PLUS = ((1, 0), (1, 1), (2, 0), (2, 1), (3, 0), (3, 1), (4, 0))
MINUS = ((7, 1), (7, 0), (6, 1), (6, 0), (5, 1), (5, 0), (4, 1))
SCHEDULE = (
    ("zs", 0, 0), ("pick", 0, 0), ("pick", 1, 0), ("zs", 0, 1), ("relay", 0, 0), ("relay", 1, 0), ("ze", 0, 0, 0),
    ("ze", 0, 1, 0), ("score", 0), ("ze", 0, 1, 1), ("ze", 0, 0, 1), ("pick", 0, 7), ("pick", 0, 1), ("ze", 0, 0, 2),
    ("relay", 0, 7), ("ze", 0, 1, 2), ("relay", 0, 1), ("ze", 0, 0, 3), ("pick", 0, 2), ("score", 1), ("ze", 0, 1, 3),
    ("pick", 0, 6), ("score", 7), ("ze", 0, 0, 4), ("relay", 0, 2), ("ze", 0, 1, 4), ("relay", 0, 6), ("ze", 0, 0, 5),
    ("pick", 0, 3), ("ze", 0, 1, 5), ("score", 2), ("pick", 0, 5), ("zs", 1, 0), ("relay", 0, 3), ("ze", 0, 0, 6),
    ("ze", 0, 1, 6), ("pick", 0, 4), ("zs", 1, 1), ("relay", 0, 5), ("score", 3), ("ze", 1, 0, 0), ("ze", 1, 1, 0),
    ("relay", 0, 4), ("score", 6), ("score", 5), ("ze", 1, 1, 1), ("pick", 1, 7), ("ze", 1, 0, 1), ("score", 4),
    ("share", 0), ("pick", 1, 1), ("partial", 0), ("ze", 1, 1, 2), ("relay", 1, 7), ("relay", 1, 1), ("ze", 1, 0, 2),
    ("whole", 0), ("ze", 1, 0, 3), ("ze", 1, 1, 3), ("pick", 1, 2), ("pick", 1, 6), ("weigh", 0), ("rf", 0), ("ro", 0),
    ("rf", 1), ("ro", 1), ("rf", 2), ("ro", 2), ("rc", 0), ("rf", 3), ("relay", 1, 6), ("rc", 1), ("ro", 3), ("rc", 2),
    ("relay", 1, 2), ("ze", 1, 0, 4), ("ze", 1, 0, 5), ("ze", 1, 1, 4), ("ze", 1, 1, 5), ("rc", 3), ("pick", 1, 5),
    ("rh", 0), ("rh", 2), ("rh", 1), ("pick", 1, 3), ("rh", 3), ("update",), ("ze", 1, 0, 6), ("relay", 1, 3),
    ("gw", 0), ("sc", 0, 7), ("sc", 0, 0), ("ze", 1, 1, 6), ("pick", 1, 4), ("sc", 0, 2), ("gather1",), ("gather1b",),
    ("sc", 0, 6), ("sc", 0, 1), ("relay", 1, 5), ("gw", 1), ("sc", 1, 0), ("sc", 1, 1), ("gather2",), ("sc", 1, 6),
    ("sc", 1, 7), ("sc", 1, 2), ("sc", 0, 3), ("relay", 1, 4), ("sc", 1, 3), ("gw", 2), ("sc", 2, 3), ("sc", 2, 2),
    ("sc", 2, 7), ("sc", 2, 1), ("sc", 0, 5), ("sc", 2, 0), ("sc", 2, 6), ("sc", 1, 5), ("sc", 2, 5), ("sc", 0, 4),
    ("sc", 1, 4), ("sc", 2, 4), ("share", 1), ("partial", 1), ("whole", 1), ("weigh", 1), ("ls", 0), ("ls", 1),
    ("ls", 2), ("ls", 3), ("lq",), ("cnt",), ("lv",), ("lu",), ("own",), ("fin",),
)


def kernel(
    pts_hbm,
    cands,
    cent_hbm,
    out_sums,
    out_counts,
    pts,
    cent,
    zbufs,
    xs,
    outs,
    relays,
    tab,
    tab_in,
    tab_sm,
    scores,
    tops,
    tops4,
    totals4,
    w,
    lses,
    stats,
    sent_parts,
    parts_in,
    sent_shifts,
    shifts,
    psend,
    precv,
    phold,
    h1,
    h2,
    cur1,
    fb,
    fs,
    fr,
    g,
    q,
    u,
    cnts,
    z_send,
    z_recv,
    y_send,
    x_recv,
    r_recv,
    r_send,
    st_sem,
    tab_sem,
    dp_send,
    dp_recv,
    fin_send,
    fin_recv,
    load_sem,
):
    dp = lax.axis_index("dp")
    cl = lax.axis_index("cluster")
    x, core = lax.div(dp, NC), lax.rem(dp, NC)
    z, y = lax.div(cl, NY), lax.rem(cl, NY)

    sign = 1 - 2 * core

    def at_cluster(k, dy):
        return {"cluster": lax.rem(z + sign * k + NZ, NZ) * NY + lax.rem(y + dy + NY, NY)}

    xp, xm, xo = lax.rem(x + 1, NX), lax.rem(x + 3, NX), lax.rem(x + 2, NX)
    dev_xp, dev_xm = {"dp": xp * NC + core}, {"dp": xm * NC + core}
    dev_core = {"dp": x * NC + 1 - core}
    z_devs = at_cluster(1, 0), at_cluster(-1, 0)
    y_up, y_down = at_cluster(0, 1), at_cluster(0, -1)

    loads = [
        pltpu.make_async_copy(pts_hbm, pts, load_sem.at[0]),
        pltpu.make_async_copy(cent_hbm, cent, load_sem.at[1]),
    ]
    for load in loads:
        load.start()

    barrier = pltpu.get_barrier_semaphore()
    for peer in [at_cluster(k, 0) for k in range(1, NZ)] + [at_cluster(0, p) for p in range(1, NY)]:
        pl.semaphore_signal(barrier, inc=1, device_id=peer, device_id_type=MESH)
    for j in range(1, NX * NC):
        pl.semaphore_signal(
            barrier, inc=1, device_id={"dp": lax.rem(dp + j, NX * NC)}, device_id_type=MESH
        )
    pl.semaphore_wait(barrier, NZ - 1 + NY - 1 + NX * NC - 1)

    drains = []

    def send(src, dst, ssem, rsem, dev):
        copy = pltpu.make_async_remote_copy(
            src_ref=src,
            dst_ref=dst,
            send_sem=ssem,
            recv_sem=rsem,
            device_id=dev,
            device_id_type=MESH,
        )
        copy.start()
        return copy

    def landed(ref, sem):
        pltpu.make_async_copy(ref, ref, sem).wait()

    def later(ref, sem):
        drains.append(lambda: landed(ref, sem))

    def drain():
        for wait in drains:
            wait()
        drains.clear()

    def half(ref, h):
        return ref.at[pl.ds(h * 4, 4)]

    def chunk(step, k):
        return pts.at[step] if k == 0 else zbufs[step * 7 + k - 1]

    def z_start(step, i):
        for d, order in enumerate((PLUS, MINUS)):
            k, h = order[i]
            src = half(pts_hbm.at[step], h)
            dst = half(chunk(step, k), h)
            send(src, dst, z_send.at[step, d, i], z_recv.at[step, d, i], z_devs[d])
            later(src, z_send.at[step, d, i])

    def z_event(step, d, i):
        order = (PLUS, MINUS)[d]
        k, h = order[i]
        here = half(chunk(step, k), h)
        landed(here, z_recv.at[step, d, i])
        if i < 5:
            dst = half(chunk(step, order[i + 2][0]), h)
            send(here, dst, z_send.at[step, d, i + 2], z_recv.at[step, d, i + 2], z_devs[d])
            later(here, z_send.at[step, d, i + 2])

    def tables():
        row = lax.broadcasted_iota(jnp.int32, (8, 128), 0)
        lane = lax.broadcasted_iota(jnp.int32, (8, 128), 1)
        oz = (z + sign * row) & (NZ - 1)
        second = ((lane >> 5) & 1) == 1
        for step in range(2):
            for t in range(2):
                owner = oz * NY + ((y + t * 2 + (lane >> 6)) & (NY - 1))
                first = jnp.full((8, 128), NB, jnp.int32)
                last = jnp.full((8, 128), -1, jnp.int32)
                for b in range(NB):
                    hit = owner == cands[step, 0, b]
                    for j in range(1, 4):
                        hit = hit | (owner == cands[step, j, b])
                    last = jnp.where(hit, b, last)
                    first = jnp.minimum(first, jnp.where(hit, b, NB))
                lone = jnp.where(first < NB, first, -1)
                bid = jnp.where(second, jnp.where(last > first, last, -1), lone)
                off = step * 256 + t * 128
                tab[:, :, off : off + 128] = bid.reshape(8, 1, 128)
        for k in range(1, NZ):
            send(tab.at[k], tab_in.at[k], tab_sem.at[0], tab_sem.at[1], at_cluster(k, 0))
        later(tab_in.at[pl.ds(1, 7)], tab_sem.at[0])
        tab_in[0] = tab[0]
        to_scalars(tab, 0, 1)

    def to_scalars(table, first, count):
        rows = pl.ds(first, count)
        copy = pltpu.make_async_copy(table.at[rows], tab_sm.at[rows], tab_sem.at[2])
        copy.start()
        copy.wait()

    def tables_in():
        landed(tab_in.at[pl.ds(1, 7)], tab_sem.at[1])
        to_scalars(tab_in, 1, 7)

    def pick(step, k):
        source, xr, box = chunk(step, k), xs[step], outs[step]

        def block(p, s):
            number = tab_sm[k, 0, step * 256 + p * 64 + s * 32]
            return source[jnp.maximum(number, 0)]

        sems = (y_send.at[step, k], x_recv.at[step, k])
        box[k, 2] = block(2, 0)
        send(box.at[k, 2], relays[step].at[k, 0], sems[0], r_recv.at[step, k, 0], y_up)
        box[k, 3] = block(2, 1)
        send(box.at[k, 3], relays[step].at[k, 1], sems[0], r_recv.at[step, k, 1], y_down)
        for p, dev in ((1, y_up), (3, y_down)):
            first = 0 if p == 1 else 4
            box[k, first] = block(p, 0)
            box[k, first + 1] = block(p, 1)
            send(
                box.at[k, pl.ds(first, 2)], xr.at[pl.ds(k * 8 + p * 2, 2)], sems[0], sems[1], dev
            )
        later(box.at[k], sems[0])
        xr[k * 8] = block(0, 0)
        xr[k * 8 + 1] = block(0, 1)

    def relay(step, k):
        for s, dev in enumerate((y_up, y_down)):
            here = relays[step].at[k, s]
            landed(here, r_recv.at[step, k, s])
            send(
                here,
                xs[step].at[k * 8 + 4 + s],
                r_send.at[step, k],
                x_recv.at[step, k],
                dev,
            )
        later(relays[step].at[k], r_send.at[step, k])

    def arrived(step, k):
        landed(xs[step].at[pl.ds(k * 8 + 2, 6)], x_recv.at[step, k])

    def against(step, k, centroids):
        rows = xs[step][k * 8 : k * 8 + 8].reshape(8 * PB, D)
        return lax.dot_general(
            centroids, rows, (((1,), (1,)), ((), ())), preferred_element_type=F32
        )

    def exps(s):
        top = jnp.max(s, axis=0, keepdims=True)
        e = jnp.exp(s - top)
        return e, top, jnp.sum(e, axis=0, keepdims=True)

    def keep(step, k, lse):
        for i in range(2):
            lses[step][i, k : k + 1, :] = lse[:, i * 128 : (i + 1) * 128]

    def score(k):
        arrived(0, k)
        e, top, total = exps(against(0, k, cent[...]))
        scores[k] = e
        tops[k] = top
        keep(0, k, top + jnp.log(total))

    def sc(part, k):
        if part == 0:
            arrived(1, k)
        which = ((x,), (xm, xp), (xo,))[part]
        places = [cur_rows(c, at) for at in which for c in range(2)]
        s = against(1, k, jnp.concatenate([cur1[rows, :] for rows in places], axis=0))
        for i, at in enumerate(which):
            e, top, total = exps(s[i * 128 : i * 128 + 128])
            scores[k, places[2 * i], :] = e[:64]
            scores[k, places[2 * i + 1], :] = e[64:]
            tops4[at, k] = top
            totals4[at, k] = total

    def join():
        for k in range(NZ):
            top = jnp.maximum(
                jnp.maximum(tops4[0, k], tops4[1, k]), jnp.maximum(tops4[2, k], tops4[3, k])
            )
            total = sum(totals4[i, k] * jnp.exp(tops4[i, k] - top) for i in range(NX))
            keep(1, k, top + jnp.log(total))

    low = lax.broadcasted_iota(jnp.int32, (1, 128), 1) < 64
    group = lax.broadcasted_iota(jnp.int32, (1, 128), 1) >> 5

    def over_groups(op, value):
        value = op(value, pltpu.roll(value, 64, 1))
        return op(value, pltpu.roll(value, 32, 1))

    def block_ids(step):
        return [
            tab_in[:, :, step * 256 + i * 128 : step * 256 + i * 128 + 128].reshape(8, 128)
            for i in range(2)
        ]

    def share(step):
        if step == 1:
            join()
        for p in range(1, NY):
            send(
                lses[step].at[p >> 1],
                stats[step].at[p],
                st_sem.at[step, 0],
                st_sem.at[step, 1],
                at_cluster(0, -p),
            )
        stats[step][0] = lses[step][0]
        later(stats[step].at[pl.ds(1, 3)], st_sem.at[step, 0])

    def partial(step):
        got = stats[step]
        landed(got.at[pl.ds(1, 3)], st_sem.at[step, 1])
        have = [jnp.where(low, got[2 * i], got[2 * i + 1]) for i in range(2)]
        ids = block_ids(step)
        packed = [jnp.full((8, 128), -BIG, F32) for _ in range(2)]
        for b in range(NB):
            mine = [ids[i] == b for i in range(2)]
            masked = [jnp.where(mine[i], have[i], -BIG) for i in range(2)]
            top = over_groups(jnp.maximum, jnp.maximum(masked[0], masked[1]))
            each = [jnp.where(mine[i], jnp.exp(have[i] - top), 0.0) for i in range(2)]
            total = over_groups(jnp.add, each[0] + each[1])
            value = jnp.where(total > 0.0, top + jnp.log(total), -BIG)
            packed[b >> 2] = jnp.where(group == (b & 3), value, packed[b >> 2])
        out = sent_parts[step]
        for i in range(2):
            out[i * 8 : i * 8 + 8, :] = packed[i]
        for j in range(1, NZ):
            send(
                out,
                parts_in[step].at[j],
                st_sem.at[step, 2],
                st_sem.at[step, 3],
                at_cluster(j, 0),
            )
        later(parts_in[step].at[pl.ds(1, 7)], st_sem.at[step, 2])

    def whole(step):
        into = parts_in[step]
        landed(into.at[pl.ds(1, 7)], st_sem.at[step, 3])
        ids = block_ids(step)
        shift = [jnp.full((8, 128), BIG, F32) for _ in range(2)]
        for i in range(2):
            rows = slice(i * 8, i * 8 + 8)
            seen = [sent_parts[step][rows, :]]
            for j in range(1, NZ):
                seen.append(pltpu.roll(into[j, rows, :], j, 0))
            top = seen[0]
            for j in range(1, NZ):
                top = jnp.maximum(top, seen[j])
            total = jnp.exp(seen[0] - top)
            for j in range(1, NZ):
                total = total + jnp.exp(seen[j] - top)
            value = top + jnp.log(total)
            for b in range(4):
                spread = over_groups(jnp.maximum, jnp.where(group == b, value, -BIG))
                for t in range(2):
                    shift[t] = jnp.where(ids[t] == i * 4 + b, spread, shift[t])
        out, back = sent_shifts[step], shifts[step]
        for t in range(2):
            out[t] = shift[t]
        back[0] = shift[0]
        for p in range(1, NY):
            send(
                out.at[p >> 1],
                back.at[p],
                st_sem.at[step, 4],
                st_sem.at[step, 5],
                at_cluster(0, p),
            )
        later(back.at[pl.ds(1, 3)], st_sem.at[step, 4])

    def weigh(step):
        back = shifts[step]
        landed(back.at[pl.ds(1, 3)], st_sem.at[step, 5])
        for k in range(NZ):
            for t in range(2):
                shift = jnp.where(low, back[2 * t, k : k + 1, :], back[2 * t + 1, k : k + 1, :])
                lanes = pl.ds(k * 256 + t * 128, 128)
                half_lanes = slice(t * 128, (t + 1) * 128)
                if step == 0:
                    scale = jnp.exp(tops[k, :, half_lanes] - shift)
                    w[:, lanes] = (scores[k, :, half_lanes] * scale).astype(BF16)
                    continue
                for at in range(NX):
                    scale = jnp.exp(tops4[at, k, :, half_lanes] - shift)
                    for first in (at * 64, 256 + at * 64):
                        rows = slice(first, first + 64)
                        w[rows, lanes] = (scores[k, rows, half_lanes] * scale).astype(BF16)

    def half_sums(which, n):
        rows = w[pl.ds(pl.multiple_of(which * 256, 256), 256), :]
        cols = xs[0][:, :, n * 256 : (n + 1) * 256].reshape(64 * PB, 256)
        return jnp.dot(rows, cols, preferred_element_type=F32)

    def rows64(at, count=64, shift=0):
        return pl.ds(pl.multiple_of(at * 64 + shift, 32), count)

    def rf(n):
        psend[n] = half_sums(1 - core, n)
        send(psend.at[n], precv.at[n], dp_send.at[n], dp_recv.at[n], dev_core)
        later(psend.at[n], dp_send.at[n])

    def ro(n):
        phold[n] = half_sums(core, n)

    def rc(n):
        landed(precv.at[n], dp_recv.at[n])
        far = rows64(xo)
        phold[n, far, :] = phold[n, far, :] + precv[n, far, :]
        sides = ((rows64(xo, 32), dev_xp), (rows64(xo, 32, 32), dev_xm))
        for i, (part, dev) in enumerate(sides):
            sems = dp_send.at[4 + 4 * i + n], dp_recv.at[4 + 4 * i + n]
            send(phold.at[n, part, :], h1.at[i, n], sems[0], sems[1], dev)
            later(h1.at[i, n], sems[0])
        for at in (xp, xm, x):
            near = rows64(at)
            phold[n, near, :] = phold[n, near, :] + precv[n, near, :]
        for i, (at, shift, dev) in enumerate(((xp, 32, dev_xp), (xm, 0, dev_xm))):
            second_hop(n, i, at, shift, dev)

    def second_hop(n, i, at, shift, dev):
        sems = dp_send.at[12 + 4 * i + n], dp_recv.at[12 + 4 * i + n]
        src = phold.at[n, rows64(at, 32, shift), :]
        send(src, h2.at[i, n, pl.ds(shift, 32)], sems[0], sems[1], dev)

    def rh(n):
        for i, (at, shift, dev) in enumerate(((xp, 0, dev_xp), (xm, 32, dev_xm))):
            landed(h1.at[i, n], dp_recv.at[4 + 4 * i + n])
            part = rows64(at, 32, shift)
            phold[n, part, :] = phold[n, part, :] + h1[i, n]
            second_hop(n, i, at, shift, dev)
            later(h2.at[i, n], dp_send.at[12 + 4 * i + n])

    def cur_rows(which_core, at, count=64, shift=0):
        return pl.ds(pl.multiple_of(which_core * 256 + at * 64 + shift, 32), count)

    def update():
        for n in range(4):
            landed(h2.at[0, n], dp_recv.at[12 + n])
            landed(h2.at[1, n], dp_recv.at[16 + n])
        own = rows64(x)
        mine = cur_rows(core, x)
        v = [
            cent[mine, n * 256 : (n + 1) * 256].astype(F32)
            + (phold[n, own, :] + h2[0, n] + h2[1, n])
            for n in range(4)
        ]
        square = sum(jnp.sum(part * part, axis=1, keepdims=True) for part in v)
        norm = jnp.sqrt(square + 1e-06)
        for n in range(4):
            cur1[mine, n * 256 : (n + 1) * 256] = (v[n] / norm).astype(BF16)
        pieces = ((0, dev_xp, 20), (32, dev_xm, 21), (32, dev_xp, 22), (0, dev_xm, 23))
        for i, (shift, dev, sem) in enumerate(pieces):
            part = cur1.at[cur_rows(core, x, 32, shift)]
            send(part, part, dp_send.at[sem], dp_recv.at[sem], dev)
            later(part, dp_send.at[sem])
            if i == 1:
                to_core(cur1.at[mine], 24, 0)

    def to_core(part, sem, group):
        send(part, part, dp_send.at[sem], dp_recv.at[26 + group], dev_core)
        later(part, dp_send.at[sem])

    def gather1():
        for i, (at, shift, dev) in enumerate(((xm, 0, dev_xp), (xp, 32, dev_xm))):
            part = cur1.at[cur_rows(core, at, 32, shift)]
            landed(part, dp_recv.at[20 + i])
            send(part, part, dp_send.at[25 + i], dp_recv.at[24 + i], dev)
            later(part, dp_send.at[25 + i])
            to_core(part, 27 + i, 1)

    def gather1b():
        for i, (at, shift) in enumerate(((xm, 32), (xp, 0))):
            part = cur1.at[cur_rows(core, at, 32, shift)]
            landed(part, dp_recv.at[22 + i])
            to_core(part, 29 + i, 1)

    def gather2():
        for i, shift in enumerate((0, 32)):
            part = cur1.at[cur_rows(core, xo, 32, shift)]
            landed(part, dp_recv.at[24 + i])
            to_core(part, 31 + i, 2)

    def gw(group):
        landed(cur1.at[pl.ds(0, (64, 128, 64)[group])], dp_recv.at[26 + group])

    def ls(j):
        lanes = pl.ds(pl.multiple_of((xo, xp, xm, x)[j] * 256, 256), 256)
        cols = xs[1][:, :, lanes].reshape(64 * PB, 256)
        part = jnp.dot(w[...], cols, preferred_element_type=F32)
        fb[j, 0] = part[:, :128]
        fb[j, 1] = part[:, 128:]
        fs[j] = fb[j, 1 - core].astype(BF16)
        send(fs.at[j], fr.at[j], fin_send.at[0], fin_recv.at[j], dev_core)
        if j == 3:
            later(fs, fin_send.at[0])

    def both(j):
        landed(fr.at[j], fin_recv.at[j])
        return fb[j, core] + fr[j].astype(F32)

    def lq():
        g[0] = both(0).astype(BF16)
        for i, dev in enumerate((dev_xp, dev_xm)):
            rows = pl.ds(256 * i, 256)
            send(g.at[0, rows], q.at[i], fin_send.at[2 + i], fin_recv.at[5 + i], dev)
            later(q.at[i], fin_send.at[2 + i])

    def last_hop(i, rows):
        dev = (dev_xp, dev_xm)[i]
        send(g.at[1 + i, rows], u.at[i, rows], fin_send.at[4 + i], fin_recv.at[7 + i], dev)

    def lv():
        for i in range(2):
            part = both(1 + i)
            rest = pl.ds(256 - 256 * i, 256)
            fb[1 + i, core] = part
            g[1 + i, rest] = part[256 - 256 * i : 512 - 256 * i].astype(BF16)
            last_hop(i, rest)

    def lu():
        for i in range(2):
            landed(q.at[i], fin_recv.at[5 + i])
            rows = pl.ds(256 * i, 256)
            g[1 + i, rows] = (fb[1 + i, core, rows, :] + q[i].astype(F32)).astype(BF16)
            last_hop(i, rows)
            later(u.at[i], fin_send.at[4 + i])

    def cnt():
        ones = jnp.ones((8, 64 * PB), BF16)
        count = lax.dot_general(
            ones, w[...], (((1,), (1,)), ((), ())), preferred_element_type=F32
        )
        cnts[dp] = count[0:1]
        for j in range(1, NX * NC):
            send(
                cnts.at[dp],
                cnts.at[dp],
                fin_send.at[1],
                fin_recv.at[4],
                {"dp": lax.rem(dp + j, NX * NC)},
            )
        later(cnts.at[pl.ds(0, 7)], fin_send.at[1])

    def own():
        fb[3, core] = both(3)
        landed(cnts.at[pl.ds(0, 7)], fin_recv.at[4])
        count = cnts[0]
        for j in range(1, NX * NC):
            count = count + cnts[j]
        for j in range(4):
            out_counts[j : j + 1, :] = count[:, j * 128 : (j + 1) * 128]
        drain()

    def fin():
        landed(u.at[0], fin_recv.at[7])
        landed(u.at[1], fin_recv.at[8])
        out_sums[...] = fb[3, core] + (u[0].astype(F32) + u[1].astype(F32))

    parts = dict(
        zs=z_start,
        ze=z_event,
        pick=pick,
        relay=relay,
        score=score,
        share=share,
        partial=partial,
        whole=whole,
        weigh=weigh,
        rf=rf,
        ro=ro,
        rc=rc,
        rh=rh,
        update=update,
        gather1=gather1,
        gather1b=gather1b,
        gather2=gather2,
        gw=gw,
        sc=sc,
        ls=ls,
        lq=lq,
        lu=lu,
        lv=lv,
        cnt=cnt,
        own=own,
        fin=fin,
    )
    for name, *numbers in SCHEDULE:
        parts[name](*numbers)
        if (name, *numbers) == ("zs", 0, 0):
            tables()
            for load in loads:
                load.wait()
        if (name, *numbers) == ("relay", 0, 0):
            tables_in()


def on_device(points, candidates, centroids):
    vmem, hbm = pl.BlockSpec(memory_space=pltpu.VMEM), pl.BlockSpec(memory_space=pl.ANY)
    sem = pltpu.SemaphoreType.DMA
    steps = points.shape[0]
    sums, counts = pl.pallas_call(
        kernel,
        out_shape=(
            jax.ShapeDtypeStruct((CBS, D // (NX * NC)), F32),
            jax.ShapeDtypeStruct((4, 128), F32),
        ),
        in_specs=[hbm, pl.BlockSpec(memory_space=pltpu.SMEM), hbm],
        out_specs=(vmem, vmem),
        scratch_shapes=[
            pltpu.VMEM((steps, NB, PB, D), BF16),
            pltpu.VMEM((CBS, D), BF16),
            [pltpu.VMEM((NB, PB, D), BF16) for _ in range(7 * steps)],
            [pltpu.VMEM((64, PB, D), BF16) for _ in range(steps)],
            [pltpu.VMEM((NZ, 6, PB, D), BF16) for _ in range(steps)],
            [pltpu.VMEM((NZ, 2, PB, D), BF16) for _ in range(steps)],
            pltpu.VMEM((NZ, 1, 512), jnp.int32),
            pltpu.VMEM((NZ, 1, 512), jnp.int32),
            pltpu.SMEM((NZ, 1, 512), jnp.int32),
            pltpu.VMEM((NZ, CBS, 256), F32),
            pltpu.VMEM((NZ, 1, 256), F32),
            pltpu.VMEM((NX, NZ, 1, 256), F32),
            pltpu.VMEM((NX, NZ, 1, 256), F32),
            pltpu.VMEM((CBS, 64 * PB), BF16),
            [pltpu.VMEM((2, 8, 128), F32) for _ in range(steps)],
            [pltpu.VMEM((4, 8, 128), F32) for _ in range(steps)],
            [pltpu.VMEM((16, 128), F32) for _ in range(steps)],
            [pltpu.VMEM((NZ, 16, 128), F32) for _ in range(steps)],
            [pltpu.VMEM((2, 8, 128), F32) for _ in range(steps)],
            [pltpu.VMEM((4, 8, 128), F32) for _ in range(steps)],
            pltpu.VMEM((4, 256, 256), F32),
            pltpu.VMEM((4, 256, 256), F32),
            pltpu.VMEM((4, 256, 256), F32),
            pltpu.VMEM((2, 4, 32, 256), F32),
            pltpu.VMEM((2, 4, 64, 256), F32),
            pltpu.VMEM((CBS, D), BF16),
            pltpu.VMEM((4, 2, CBS, 128), F32),
            pltpu.VMEM((4, CBS, 128), BF16),
            pltpu.VMEM((4, CBS, 128), BF16),
            pltpu.VMEM((3, CBS, 128), BF16),
            pltpu.VMEM((2, 256, 128), BF16),
            pltpu.VMEM((2, CBS, 128), BF16),
            pltpu.VMEM((NX * NC, 1, CBS), F32),
            sem((steps, 2, 7)),
            sem((steps, 2, 7)),
            sem((steps, NZ)),
            sem((steps, NZ)),
            sem((steps, NZ, 2)),
            sem((steps, NZ)),
            sem((steps, 6)),
            sem((3,)),
            sem((33,)),
            sem((29,)),
            sem((6,)),
            sem((9,)),
            sem((2,)),
        ],
        compiler_params=pltpu.CompilerParams(
            collective_id=0, has_side_effects=True, vmem_limit_bytes=56 * 1024 * 1024
        ),
    )(points.reshape(steps, NB, PB, D), jnp.transpose(candidates, (0, 2, 1)), centroids)
    return sums, counts.reshape(CBS)


def solution(mesh):
    placed = (
        P(None, ("dp", "cluster"), None),
        P(None, ("dp", "cluster"), None),
        P("cluster", None),
    )
    return jax.shard_map(
        on_device,
        mesh=mesh,
        in_specs=placed,
        out_specs=(P("cluster", "dp"), P("cluster")),
        check_vma=False,
    )
```

```python
import jax
import jax.numpy as jnp
from jax import lax
from jax.experimental import pallas as pl
from jax.experimental.pallas import tpu as pltpu
from jax.sharding import PartitionSpec as P

MESH = pl.DeviceIdType.MESH
F32 = jnp.float32
BF16 = jnp.bfloat16
BIG = 3.0e38
NZ, NY, NX, NC = 8, 4, 4, 2
NB, PB, D, CBS = 8, 32, 1024, 512
PLUS = ((1, 0), (1, 1), (2, 0), (2, 1), (3, 0), (3, 1), (4, 0))
MINUS = ((7, 1), (7, 0), (6, 1), (6, 0), (5, 1), (5, 0), (4, 1))
SCHEDULE = (
    ("zs", 0, 0, 0), ("pr", 0, 0), ("zs", 0, 0, 1), ("pp", 0, 0), ("pr", 1, 0), ("pp", 1, 0), ("zs", 0, 1, 0),
    ("relay", 0, 0), ("zs", 0, 1, 1), ("relay", 1, 0), ("ze", 0, 0, 0), ("ze", 0, 1, 0), ("ze", 0, 0, 1), ("pr", 0, 1),
    ("pp", 0, 1), ("ze", 0, 1, 1), ("pr", 0, 7), ("pp", 0, 7), ("ze", 0, 0, 2), ("relay", 0, 1), ("relay", 0, 7),
    ("ze", 0, 1, 2), ("ze", 0, 0, 3), ("pr", 0, 2), ("pp", 0, 2), ("score", 1), ("score", 0), ("ze", 0, 1, 3),
    ("pr", 0, 6), ("relay", 0, 2), ("pp", 0, 6), ("ze", 0, 0, 4), ("relay", 0, 6), ("score", 7), ("ze", 0, 1, 4),
    ("ze", 0, 0, 5), ("pr", 0, 3), ("pp", 0, 3), ("ze", 0, 1, 5), ("score", 2), ("zs", 1, 0, 0), ("pr", 0, 5),
    ("zs", 1, 1, 0), ("relay", 0, 3), ("pp", 0, 5), ("score", 6), ("zs", 1, 1, 1), ("ze", 0, 1, 6), ("ze", 0, 0, 6),
    ("pr", 0, 4), ("zs", 1, 0, 1), ("relay", 0, 5), ("pp", 0, 4), ("score", 3), ("relay", 0, 4), ("ze", 1, 0, 0),
    ("ze", 1, 1, 0), ("score", 5), ("ze", 1, 1, 1), ("pr", 1, 7), ("pp", 1, 7), ("score", 4), ("share", 0),
    ("ze", 1, 0, 1), ("pr", 1, 1), ("pp", 1, 1), ("partial", 0), ("relay", 1, 7), ("ze", 1, 1, 2), ("ze", 1, 0, 2),
    ("relay", 1, 1), ("whole", 0), ("ze", 1, 1, 3), ("pr", 1, 6), ("pp", 1, 6), ("ze", 1, 0, 3), ("pr", 1, 2),
    ("pp", 1, 2), ("weigh", 0), ("rf", 0), ("ro", 0), ("rf", 1), ("ro", 1), ("rf", 2), ("ro", 2), ("rc", 0), ("re", 0),
    ("rf", 3), ("rc", 1), ("re", 1), ("relay", 1, 6), ("rc", 2), ("relay", 1, 2), ("re", 2), ("ro", 3), ("rc", 3),
    ("re", 3), ("ze", 1, 1, 4), ("ze", 1, 0, 4), ("ze", 1, 1, 5), ("pr", 1, 5), ("rh", 1), ("pp", 1, 5), ("rh", 0),
    ("rh", 2), ("ze", 1, 0, 5), ("rh", 3), ("pr", 1, 3), ("pp", 1, 3), ("update",), ("ze", 1, 0, 6), ("ze", 1, 1, 6),
    ("ub",), ("gw", 0), ("sc", 0, 6), ("relay", 1, 3), ("sc", 0, 7), ("sc", 0, 2), ("sc", 0, 0), ("gather1",),
    ("gather1b",), ("pr", 1, 4), ("sc", 0, 1), ("relay", 1, 5), ("pp", 1, 4), ("sc", 0, 3), ("gw", 1), ("sc", 1, 6),
    ("sc", 1, 0), ("gather2",), ("sc", 1, 2), ("sc", 1, 1), ("sc", 1, 3), ("relay", 1, 4), ("sc", 1, 7), ("gw", 2),
    ("sc", 2, 2), ("sc", 2, 1), ("sc", 0, 5), ("sc", 1, 5), ("sc", 2, 3), ("sc", 2, 0), ("sc", 2, 7), ("sc", 2, 5),
    ("sc", 0, 4), ("sc", 2, 4), ("sc", 1, 4), ("sc", 2, 6), ("share", 1), ("partial", 1), ("whole", 1), ("weigh", 1),
    ("ls", 0), ("ls", 1), ("ls", 2), ("lq",), ("ls", 3), ("lv",), ("cnt",), ("lu",), ("own",), ("fin",),
)


def kernel(
    pts_hbm,
    cands,
    cent_hbm,
    out_sums,
    out_counts,
    pts,
    cent,
    zbufs,
    xs,
    outs,
    relays,
    tab,
    tab_in,
    tab_sm,
    scores,
    tops,
    tops4,
    totals4,
    w,
    lses,
    stats,
    sent_parts,
    parts_in,
    sent_shifts,
    shifts,
    psend,
    precv,
    phold,
    h1,
    h2,
    cur1,
    fb,
    fs,
    fr,
    g,
    q,
    u,
    cnts,
    z_send,
    z_recv,
    y_send,
    x_recv,
    r_recv,
    r_send,
    st_sem,
    tab_sem,
    dp_send,
    dp_recv,
    fin_send,
    fin_recv,
    load_sem,
):
    dp = lax.axis_index("dp")
    cl = lax.axis_index("cluster")
    x, core = lax.div(dp, NC), lax.rem(dp, NC)
    z, y = lax.div(cl, NY), lax.rem(cl, NY)

    sign = 1 - 2 * core

    def at_cluster(k, dy):
        return {"cluster": lax.rem(z + sign * k + NZ, NZ) * NY + lax.rem(y + dy + NY, NY)}

    xp, xm, xo = lax.rem(x + 1, NX), lax.rem(x + 3, NX), lax.rem(x + 2, NX)
    dev_xp, dev_xm = {"dp": xp * NC + core}, {"dp": xm * NC + core}
    dev_core = {"dp": x * NC + 1 - core}
    z_devs = at_cluster(1, 0), at_cluster(-1, 0)
    y_up, y_down = at_cluster(0, 1), at_cluster(0, -1)

    loads = [
        pltpu.make_async_copy(pts_hbm, pts, load_sem.at[0]),
        pltpu.make_async_copy(cent_hbm, cent, load_sem.at[1]),
    ]
    for load in loads:
        load.start()

    barrier = pltpu.get_barrier_semaphore()
    for peer in [at_cluster(k, 0) for k in range(1, NZ)] + [at_cluster(0, p) for p in range(1, NY)]:
        pl.semaphore_signal(barrier, inc=1, device_id=peer, device_id_type=MESH)
    for j in range(1, NX * NC):
        pl.semaphore_signal(
            barrier, inc=1, device_id={"dp": lax.rem(dp + j, NX * NC)}, device_id_type=MESH
        )
    pl.semaphore_wait(barrier, NZ - 1 + NY - 1 + NX * NC - 1)

    drains = []

    def send(src, dst, ssem, rsem, dev):
        copy = pltpu.make_async_remote_copy(
            src_ref=src,
            dst_ref=dst,
            send_sem=ssem,
            recv_sem=rsem,
            device_id=dev,
            device_id_type=MESH,
        )
        copy.start()
        return copy

    def landed(ref, sem):
        pltpu.make_async_copy(ref, ref, sem).wait()

    def later(ref, sem):
        drains.append(lambda: landed(ref, sem))

    def drain():
        for wait in drains:
            wait()
        drains.clear()

    def half(ref, h):
        return ref.at[pl.ds(h * 4, 4)]

    def chunk(step, k):
        return pts.at[step] if k == 0 else zbufs[step * 7 + k - 1]

    def z_start(step, d, i):
        k, h = (PLUS, MINUS)[d][i]
        src = half(pts_hbm.at[step], h)
        dst = half(chunk(step, k), h)
        send(src, dst, z_send.at[step, d, i], z_recv.at[step, d, i], z_devs[d])
        later(src, z_send.at[step, d, i])

    def z_event(step, d, i):
        order = (PLUS, MINUS)[d]
        k, h = order[i]
        here = half(chunk(step, k), h)
        landed(here, z_recv.at[step, d, i])
        if i < 5:
            dst = half(chunk(step, order[i + 2][0]), h)
            send(here, dst, z_send.at[step, d, i + 2], z_recv.at[step, d, i + 2], z_devs[d])
            later(here, z_send.at[step, d, i + 2])

    def tables():
        row = lax.broadcasted_iota(jnp.int32, (8, 128), 0)
        lane = lax.broadcasted_iota(jnp.int32, (8, 128), 1)
        oz = (z + sign * row) & (NZ - 1)
        second = ((lane >> 5) & 1) == 1
        for step in range(2):
            for t in range(2):
                owner = oz * NY + ((y + t * 2 + (lane >> 6)) & (NY - 1))
                first = jnp.full((8, 128), NB, jnp.int32)
                last = jnp.full((8, 128), -1, jnp.int32)
                for b in range(NB):
                    hit = owner == cands[step, 0, b]
                    for j in range(1, 4):
                        hit = hit | (owner == cands[step, j, b])
                    last = jnp.where(hit, b, last)
                    first = jnp.minimum(first, jnp.where(hit, b, NB))
                lone = jnp.where(first < NB, first, -1)
                bid = jnp.where(second, jnp.where(last > first, last, -1), lone)
                off = step * 256 + t * 128
                tab[:, :, off : off + 128] = bid.reshape(8, 1, 128)
        for k in range(1, NZ):
            send(tab.at[k], tab_in.at[k], tab_sem.at[0], tab_sem.at[1], at_cluster(k, 0))
        later(tab_in.at[pl.ds(1, 7)], tab_sem.at[0])
        tab_in[0] = tab[0]
        to_scalars(tab, 0, 1)

    def to_scalars(table, first, count):
        rows = pl.ds(first, count)
        copy = pltpu.make_async_copy(table.at[rows], tab_sm.at[rows], tab_sem.at[2])
        copy.start()
        copy.wait()

    def tables_in():
        landed(tab_in.at[pl.ds(1, 7)], tab_sem.at[1])
        to_scalars(tab_in, 1, 7)

    def block(step, k, p, s):
        number = tab_sm[k, 0, step * 256 + p * 64 + s * 32]
        return chunk(step, k)[jnp.maximum(number, 0)]

    def pr(step, k):
        for s, dev in enumerate((y_up, y_down)):
            box = outs[step].at[k, 2 + s]
            box[...] = block(step, k, 2, s)
            send(box, relays[step].at[k, s], y_send.at[step, k], r_recv.at[step, k, s], dev)

    def pp(step, k):
        xr, box = xs[step], outs[step]
        for p, dev in ((1, y_up), (3, y_down)):
            first = 0 if p == 1 else 4
            for s in range(2):
                box[k, first + s] = block(step, k, p, s)
            there = xr.at[pl.ds(k * 8 + p * 2, 2)]
            send(box.at[k, pl.ds(first, 2)], there, y_send.at[step, k], x_recv.at[step, k], dev)
        later(box.at[k], y_send.at[step, k])
        for s in range(2):
            xr[k * 8 + s] = block(step, k, 0, s)

    def relay(step, k):
        for s, dev in enumerate((y_up, y_down)):
            here = relays[step].at[k, s]
            landed(here, r_recv.at[step, k, s])
            send(
                here,
                xs[step].at[k * 8 + 4 + s],
                r_send.at[step, k],
                x_recv.at[step, k],
                dev,
            )
        later(relays[step].at[k], r_send.at[step, k])

    def arrived(step, k):
        landed(xs[step].at[pl.ds(k * 8 + 2, 6)], x_recv.at[step, k])

    def against(step, k, centroids):
        rows = xs[step][k * 8 : k * 8 + 8].reshape(8 * PB, D)
        return lax.dot_general(
            centroids, rows, (((1,), (1,)), ((), ())), preferred_element_type=F32
        )

    def exps(s):
        top = jnp.max(s, axis=0, keepdims=True)
        e = jnp.exp(s - top)
        return e, top, jnp.sum(e, axis=0, keepdims=True)

    def keep(step, k, lse):
        for i in range(2):
            lses[step][i, k : k + 1, :] = lse[:, i * 128 : (i + 1) * 128]

    def score(k):
        arrived(0, k)
        e, top, total = exps(against(0, k, cent[...]))
        scores[k] = e
        tops[k] = top
        keep(0, k, top + jnp.log(total))

    def sc(part, k):
        if part == 0:
            arrived(1, k)
        which = ((x,), (xm, xp), (xo,))[part]
        places = [cur_rows(c, at) for at in which for c in range(2)]
        s = against(1, k, jnp.concatenate([cur1[rows, :] for rows in places], axis=0))
        for i, at in enumerate(which):
            e, top, total = exps(s[i * 128 : i * 128 + 128])
            scores[k, places[2 * i], :] = e[:64]
            scores[k, places[2 * i + 1], :] = e[64:]
            tops4[at, k] = top
            totals4[at, k] = total

    def join():
        for k in range(NZ):
            top = jnp.maximum(
                jnp.maximum(tops4[0, k], tops4[1, k]), jnp.maximum(tops4[2, k], tops4[3, k])
            )
            total = sum(totals4[i, k] * jnp.exp(tops4[i, k] - top) for i in range(NX))
            keep(1, k, top + jnp.log(total))

    low = lax.broadcasted_iota(jnp.int32, (1, 128), 1) < 64
    group = lax.broadcasted_iota(jnp.int32, (1, 128), 1) >> 5

    def over_groups(op, value):
        value = op(value, pltpu.roll(value, 64, 1))
        return op(value, pltpu.roll(value, 32, 1))

    def block_ids(step):
        return [
            tab_in[:, :, step * 256 + i * 128 : step * 256 + i * 128 + 128].reshape(8, 128)
            for i in range(2)
        ]

    def share(step):
        if step == 1:
            join()
        for p in range(1, NY):
            send(
                lses[step].at[p >> 1],
                stats[step].at[p],
                st_sem.at[step, 0],
                st_sem.at[step, 1],
                at_cluster(0, -p),
            )
        stats[step][0] = lses[step][0]
        later(stats[step].at[pl.ds(1, 3)], st_sem.at[step, 0])

    def partial(step):
        got = stats[step]
        landed(got.at[pl.ds(1, 3)], st_sem.at[step, 1])
        have = [jnp.where(low, got[2 * i], got[2 * i + 1]) for i in range(2)]
        ids = block_ids(step)
        packed = [jnp.full((8, 128), -BIG, F32) for _ in range(2)]
        for b in range(NB):
            mine = [ids[i] == b for i in range(2)]
            masked = [jnp.where(mine[i], have[i], -BIG) for i in range(2)]
            top = over_groups(jnp.maximum, jnp.maximum(masked[0], masked[1]))
            each = [jnp.where(mine[i], jnp.exp(have[i] - top), 0.0) for i in range(2)]
            total = over_groups(jnp.add, each[0] + each[1])
            value = jnp.where(total > 0.0, top + jnp.log(total), -BIG)
            packed[b >> 2] = jnp.where(group == (b & 3), value, packed[b >> 2])
        out = sent_parts[step]
        for i in range(2):
            out[i * 8 : i * 8 + 8, :] = packed[i]
        for j in (4, 3, 5, 2, 6, 1, 7):
            send(
                out,
                parts_in[step].at[j],
                st_sem.at[step, 2],
                st_sem.at[step, 3],
                at_cluster(j, 0),
            )
        later(parts_in[step].at[pl.ds(1, 7)], st_sem.at[step, 2])

    def whole(step):
        into = parts_in[step]
        landed(into.at[pl.ds(1, 7)], st_sem.at[step, 3])
        ids = block_ids(step)
        shift = [jnp.full((8, 128), BIG, F32) for _ in range(2)]
        for i in range(2):
            rows = slice(i * 8, i * 8 + 8)
            seen = [sent_parts[step][rows, :]]
            for j in range(1, NZ):
                seen.append(pltpu.roll(into[j, rows, :], j, 0))
            top = seen[0]
            for j in range(1, NZ):
                top = jnp.maximum(top, seen[j])
            total = jnp.exp(seen[0] - top)
            for j in range(1, NZ):
                total = total + jnp.exp(seen[j] - top)
            value = top + jnp.log(total)
            for b in range(4):
                spread = over_groups(jnp.maximum, jnp.where(group == b, value, -BIG))
                for t in range(2):
                    shift[t] = jnp.where(ids[t] == i * 4 + b, spread, shift[t])
        out, back = sent_shifts[step], shifts[step]
        for t in range(2):
            out[t] = shift[t]
        back[0] = shift[0]
        for p in range(1, NY):
            send(
                out.at[p >> 1],
                back.at[p],
                st_sem.at[step, 4],
                st_sem.at[step, 5],
                at_cluster(0, p),
            )
        later(back.at[pl.ds(1, 3)], st_sem.at[step, 4])

    def weigh(step):
        back = shifts[step]
        landed(back.at[pl.ds(1, 3)], st_sem.at[step, 5])
        for k in range(NZ):
            for t in range(2):
                shift = jnp.where(low, back[2 * t, k : k + 1, :], back[2 * t + 1, k : k + 1, :])
                lanes = pl.ds(k * 256 + t * 128, 128)
                half_lanes = slice(t * 128, (t + 1) * 128)
                if step == 0:
                    scale = jnp.exp(tops[k, :, half_lanes] - shift)
                    w[:, lanes] = (scores[k, :, half_lanes] * scale).astype(BF16)
                    continue
                for at in range(NX):
                    scale = jnp.exp(tops4[at, k, :, half_lanes] - shift)
                    for first in (at * 64, 256 + at * 64):
                        rows = slice(first, first + 64)
                        w[rows, lanes] = (scores[k, rows, half_lanes] * scale).astype(BF16)

    def half_sums(which, n):
        rows = w[pl.ds(pl.multiple_of(which * 256, 256), 256), :]
        cols = xs[0][:, :, n * 256 : (n + 1) * 256].reshape(64 * PB, 256)
        return jnp.dot(rows, cols, preferred_element_type=F32)

    def rows64(at, count=64, shift=0):
        return pl.ds(pl.multiple_of(at * 64 + shift, 32), count)

    def rf(n):
        psend[n] = half_sums(1 - core, n)
        send(psend.at[n], precv.at[n], dp_send.at[n], dp_recv.at[n], dev_core)
        later(psend.at[n], dp_send.at[n])

    def ro(n):
        phold[n] = half_sums(core, n)

    def rc(n):
        landed(precv.at[n], dp_recv.at[n])
        far = rows64(xo)
        phold[n, far, :] = phold[n, far, :] + precv[n, far, :]
        sides = ((rows64(xo, 32), dev_xp), (rows64(xo, 32, 32), dev_xm))
        for i, (part, dev) in enumerate(sides):
            sems = dp_send.at[4 + 4 * i + n], dp_recv.at[4 + 4 * i + n]
            send(phold.at[n, part, :], h1.at[i, n], sems[0], sems[1], dev)
            later(h1.at[i, n], sems[0])

    def re(n):
        for at in (xp, xm, x):
            near = rows64(at)
            phold[n, near, :] = phold[n, near, :] + precv[n, near, :]
        for i, (at, shift, dev) in enumerate(((xp, 32, dev_xp), (xm, 0, dev_xm))):
            second_hop(n, i, at, shift, dev)

    def second_hop(n, i, at, shift, dev):
        sems = dp_send.at[12 + 4 * i + n], dp_recv.at[12 + 4 * i + n]
        src = phold.at[n, rows64(at, 32, shift), :]
        send(src, h2.at[i, n, pl.ds(shift, 32)], sems[0], sems[1], dev)

    def rh(n):
        for i, (at, shift, dev) in enumerate(((xp, 0, dev_xp), (xm, 32, dev_xm))):
            landed(h1.at[i, n], dp_recv.at[4 + 4 * i + n])
            part = rows64(at, 32, shift)
            phold[n, part, :] = phold[n, part, :] + h1[i, n]
            second_hop(n, i, at, shift, dev)
            later(h2.at[i, n], dp_send.at[12 + 4 * i + n])

    def cur_rows(which_core, at, count=64, shift=0):
        return pl.ds(pl.multiple_of(which_core * 256 + at * 64 + shift, 32), count)

    def update():
        for n in range(4):
            landed(h2.at[0, n], dp_recv.at[12 + n])
            landed(h2.at[1, n], dp_recv.at[16 + n])
        own = rows64(x)
        mine = cur_rows(core, x)
        v = [
            cent[mine, n * 256 : (n + 1) * 256].astype(F32)
            + (phold[n, own, :] + h2[0, n] + h2[1, n])
            for n in range(4)
        ]
        square = sum(jnp.sum(part * part, axis=1, keepdims=True) for part in v)
        norm = jnp.sqrt(square + 1e-06)
        for n in range(4):
            cur1[mine, n * 256 : (n + 1) * 256] = (v[n] / norm).astype(BF16)
        own_rows(0)
        to_core(cur1.at[mine], 24, 0)

    def own_rows(second):
        for i, (shift, dev) in enumerate(((0, dev_xp), (32, dev_xm))):
            part = cur1.at[cur_rows(core, x, 32, 32 - shift if second else shift)]
            sem = 20 + 2 * second + i
            send(part, part, dp_send.at[sem], dp_recv.at[sem], dev)
            later(part, dp_send.at[sem])

    def ub():
        own_rows(1)

    def to_core(part, sem, group):
        send(part, part, dp_send.at[sem], dp_recv.at[26 + group], dev_core)
        later(part, dp_send.at[sem])

    def gather1():
        for i, (at, shift, dev) in enumerate(((xm, 0, dev_xp), (xp, 32, dev_xm))):
            part = cur1.at[cur_rows(core, at, 32, shift)]
            landed(part, dp_recv.at[20 + i])
            send(part, part, dp_send.at[25 + i], dp_recv.at[24 + i], dev)
            later(part, dp_send.at[25 + i])
            to_core(part, 27 + i, 1)

    def gather1b():
        for i, (at, shift) in enumerate(((xm, 32), (xp, 0))):
            part = cur1.at[cur_rows(core, at, 32, shift)]
            landed(part, dp_recv.at[22 + i])
            to_core(part, 29 + i, 1)

    def gather2():
        for i, shift in enumerate((0, 32)):
            part = cur1.at[cur_rows(core, xo, 32, shift)]
            landed(part, dp_recv.at[24 + i])
            to_core(part, 31 + i, 2)

    def gw(group):
        landed(cur1.at[pl.ds(0, (64, 128, 64)[group])], dp_recv.at[26 + group])

    def ls(j):
        lanes = pl.ds(pl.multiple_of((xo, xp, xm, x)[j] * 256, 256), 256)
        cols = xs[1][:, :, lanes].reshape(64 * PB, 256)
        part = jnp.dot(w[...], cols, preferred_element_type=F32)
        fb[j, 0] = part[:, :128]
        fb[j, 1] = part[:, 128:]
        fs[j] = fb[j, 1 - core].astype(BF16)
        send(fs.at[j], fr.at[j], fin_send.at[0], fin_recv.at[j], dev_core)
        if j == 3:
            later(fs, fin_send.at[0])

    def both(j):
        landed(fr.at[j], fin_recv.at[j])
        return fb[j, core] + fr[j].astype(F32)

    def lq():
        g[0] = both(0).astype(BF16)
        for i, dev in enumerate((dev_xp, dev_xm)):
            rows = pl.ds(256 * i, 256)
            send(g.at[0, rows], q.at[i], fin_send.at[2 + i], fin_recv.at[5 + i], dev)
            later(q.at[i], fin_send.at[2 + i])

    def last_hop(i, rows):
        dev = (dev_xp, dev_xm)[i]
        send(g.at[1 + i, rows], u.at[i, rows], fin_send.at[4 + i], fin_recv.at[7 + i], dev)

    def lv():
        for i in range(2):
            part = both(1 + i)
            rest = pl.ds(256 - 256 * i, 256)
            fb[1 + i, core] = part
            g[1 + i, rest] = part[256 - 256 * i : 512 - 256 * i].astype(BF16)
            last_hop(i, rest)

    def lu():
        for i in range(2):
            landed(q.at[i], fin_recv.at[5 + i])
            rows = pl.ds(256 * i, 256)
            g[1 + i, rows] = (fb[1 + i, core, rows, :] + q[i].astype(F32)).astype(BF16)
            last_hop(i, rows)
            later(u.at[i], fin_send.at[4 + i])

    def cnt():
        ones = jnp.ones((8, 64 * PB), BF16)
        count = lax.dot_general(
            ones, w[...], (((1,), (1,)), ((), ())), preferred_element_type=F32
        )
        cnts[dp] = count[0:1]
        for j in range(1, NX * NC):
            send(
                cnts.at[dp],
                cnts.at[dp],
                fin_send.at[1],
                fin_recv.at[4],
                {"dp": lax.rem(dp + j, NX * NC)},
            )
        later(cnts.at[pl.ds(0, 7)], fin_send.at[1])

    def own():
        fb[3, core] = both(3)
        landed(cnts.at[pl.ds(0, 7)], fin_recv.at[4])
        count = cnts[0]
        for j in range(1, NX * NC):
            count = count + cnts[j]
        for j in range(4):
            out_counts[j : j + 1, :] = count[:, j * 128 : (j + 1) * 128]
        drain()

    def fin():
        landed(u.at[0], fin_recv.at[7])
        landed(u.at[1], fin_recv.at[8])
        out_sums[...] = fb[3, core] + (u[0].astype(F32) + u[1].astype(F32))

    parts = dict(
        zs=z_start,
        ze=z_event,
        pr=pr,
        pp=pp,
        re=re,
        ub=ub,
        relay=relay,
        score=score,
        share=share,
        partial=partial,
        whole=whole,
        weigh=weigh,
        rf=rf,
        ro=ro,
        rc=rc,
        rh=rh,
        update=update,
        gather1=gather1,
        gather1b=gather1b,
        gather2=gather2,
        gw=gw,
        sc=sc,
        ls=ls,
        lq=lq,
        lu=lu,
        lv=lv,
        cnt=cnt,
        own=own,
        fin=fin,
    )
    for name, *numbers in SCHEDULE:
        if (name, *numbers) == ("pr", 0, 0):
            tables()
            for load in loads:
                load.wait()
        parts[name](*numbers)
        if (name, *numbers) == ("relay", 0, 0):
            tables_in()
        if (name, *numbers) in (("share", 1), ("whole", 1)):
            drain()


def on_device(points, candidates, centroids):
    vmem, hbm = pl.BlockSpec(memory_space=pltpu.VMEM), pl.BlockSpec(memory_space=pl.ANY)
    sem = pltpu.SemaphoreType.DMA
    steps = points.shape[0]
    sums, counts = pl.pallas_call(
        kernel,
        out_shape=(
            jax.ShapeDtypeStruct((CBS, D // (NX * NC)), F32),
            jax.ShapeDtypeStruct((4, 128), F32),
        ),
        in_specs=[hbm, pl.BlockSpec(memory_space=pltpu.SMEM), hbm],
        out_specs=(vmem, vmem),
        scratch_shapes=[
            pltpu.VMEM((steps, NB, PB, D), BF16),
            pltpu.VMEM((CBS, D), BF16),
            [pltpu.VMEM((NB, PB, D), BF16) for _ in range(7 * steps)],
            [pltpu.VMEM((64, PB, D), BF16) for _ in range(steps)],
            [pltpu.VMEM((NZ, 6, PB, D), BF16) for _ in range(steps)],
            [pltpu.VMEM((NZ, 2, PB, D), BF16) for _ in range(steps)],
            pltpu.VMEM((NZ, 1, 512), jnp.int32),
            pltpu.VMEM((NZ, 1, 512), jnp.int32),
            pltpu.SMEM((NZ, 1, 512), jnp.int32),
            pltpu.VMEM((NZ, CBS, 256), F32),
            pltpu.VMEM((NZ, 1, 256), F32),
            pltpu.VMEM((NX, NZ, 1, 256), F32),
            pltpu.VMEM((NX, NZ, 1, 256), F32),
            pltpu.VMEM((CBS, 64 * PB), BF16),
            [pltpu.VMEM((2, 8, 128), F32) for _ in range(steps)],
            [pltpu.VMEM((4, 8, 128), F32) for _ in range(steps)],
            [pltpu.VMEM((16, 128), F32) for _ in range(steps)],
            [pltpu.VMEM((NZ, 16, 128), F32) for _ in range(steps)],
            [pltpu.VMEM((2, 8, 128), F32) for _ in range(steps)],
            [pltpu.VMEM((4, 8, 128), F32) for _ in range(steps)],
            pltpu.VMEM((4, 256, 256), F32),
            pltpu.VMEM((4, 256, 256), F32),
            pltpu.VMEM((4, 256, 256), F32),
            pltpu.VMEM((2, 4, 32, 256), F32),
            pltpu.VMEM((2, 4, 64, 256), F32),
            pltpu.VMEM((CBS, D), BF16),
            pltpu.VMEM((4, 2, CBS, 128), F32),
            pltpu.VMEM((4, CBS, 128), BF16),
            pltpu.VMEM((4, CBS, 128), BF16),
            pltpu.VMEM((3, CBS, 128), BF16),
            pltpu.VMEM((2, 256, 128), BF16),
            pltpu.VMEM((2, CBS, 128), BF16),
            pltpu.VMEM((NX * NC, 1, CBS), F32),
            sem((steps, 2, 7)),
            sem((steps, 2, 7)),
            sem((steps, NZ)),
            sem((steps, NZ)),
            sem((steps, NZ, 2)),
            sem((steps, NZ)),
            sem((steps, 6)),
            sem((3,)),
            sem((33,)),
            sem((29,)),
            sem((6,)),
            sem((9,)),
            sem((2,)),
        ],
        compiler_params=pltpu.CompilerParams(
            collective_id=0, has_side_effects=True, vmem_limit_bytes=54250 * 1024
        ),
    )(points.reshape(steps, NB, PB, D), jnp.transpose(candidates, (0, 2, 1)), centroids)
    return sums, counts.reshape(CBS)


def solution(mesh):
    placed = (
        P(None, ("dp", "cluster"), None),
        P(None, ("dp", "cluster"), None),
        P("cluster", None),
    )
    return jax.shard_map(
        on_device,
        mesh=mesh,
        in_specs=placed,
        out_specs=(P("cluster", "dp"), P("cluster")),
        check_vma=False,
    )
```

```python
import jax
import jax.numpy as jnp
from jax import lax
from jax.experimental import pallas as pl
from jax.experimental.pallas import tpu as pltpu
from jax.sharding import PartitionSpec as P

MESH = pl.DeviceIdType.MESH
F32 = jnp.float32
BF16 = jnp.bfloat16
BIG = 3.0e38
NZ, NY, NX, NC = 8, 4, 4, 2
NB, PB, D, CBS = 8, 32, 1024, 512
PLUS = ((1, 0), (1, 1), (2, 0), (2, 1), (3, 0), (3, 1), (4, 0))
MINUS = ((7, 1), (7, 0), (6, 1), (6, 0), (5, 1), (5, 0), (4, 1))
SCHEDULE = (
    ("zs", 0, 0, 0), ("pr", 0, 0), ("zs", 0, 0, 1), ("pp", 0, 0), ("pr", 1, 0), ("pp", 1, 0), ("zs", 0, 1, 0),
    ("relay", 0, 0), ("zs", 0, 1, 1), ("relay", 1, 0), ("ze", 0, 0, 0), ("ze", 0, 1, 0), ("ze", 0, 0, 1), ("pr", 0, 1),
    ("pp", 0, 1), ("ze", 0, 1, 1), ("pr", 0, 7), ("pp", 0, 7), ("ze", 0, 0, 2), ("relay", 0, 1), ("relay", 0, 7),
    ("ze", 0, 1, 2), ("ze", 0, 0, 3), ("pr", 0, 2), ("pp", 0, 2), ("score", 1), ("score", 0), ("ze", 0, 1, 3),
    ("pr", 0, 6), ("relay", 0, 2), ("pp", 0, 6), ("ze", 0, 0, 4), ("relay", 0, 6), ("score", 7), ("ze", 0, 1, 4),
    ("ze", 0, 0, 5), ("pr", 0, 3), ("pp", 0, 3), ("ze", 0, 1, 5), ("score", 2), ("zs", 1, 0, 0), ("pr", 0, 5),
    ("zs", 1, 1, 0), ("relay", 0, 3), ("pp", 0, 5), ("score", 6), ("zs", 1, 1, 1), ("ze", 0, 1, 6), ("ze", 0, 0, 6),
    ("pr", 0, 4), ("zs", 1, 0, 1), ("relay", 0, 5), ("pp", 0, 4), ("score", 3), ("relay", 0, 4), ("ze", 1, 0, 0),
    ("ze", 1, 1, 0), ("score", 5), ("ze", 1, 1, 1), ("pr", 1, 7), ("pp", 1, 7), ("score", 4), ("share", 0),
    ("ze", 1, 0, 1), ("pr", 1, 1), ("pp", 1, 1), ("partial", 0), ("relay", 1, 7), ("ze", 1, 1, 2), ("ze", 1, 0, 2),
    ("relay", 1, 1), ("whole", 0), ("ze", 1, 1, 3), ("pr", 1, 6), ("pp", 1, 6), ("ze", 1, 0, 3), ("pr", 1, 2),
    ("pp", 1, 2), ("weigh", 0), ("rf", 0), ("ro", 0), ("rf", 1), ("ro", 1), ("rf", 2), ("ro", 2), ("rc", 0), ("re", 0),
    ("rf", 3), ("rc", 1), ("re", 1), ("relay", 1, 6), ("rc", 2), ("relay", 1, 2), ("re", 2), ("ro", 3), ("rc", 3),
    ("re", 3), ("ze", 1, 1, 4), ("ze", 1, 0, 4), ("ze", 1, 1, 5), ("pr", 1, 5), ("rh", 1), ("pp", 1, 5), ("rh", 0),
    ("rh", 2), ("ze", 1, 0, 5), ("rh", 3), ("pr", 1, 3), ("pp", 1, 3), ("update",), ("ze", 1, 0, 6), ("ze", 1, 1, 6),
    ("ub",), ("gw", 0), ("sc", 0, 6), ("relay", 1, 3), ("sc", 0, 7), ("sc", 0, 2), ("sc", 0, 0), ("gather1",),
    ("gather1b",), ("pr", 1, 4), ("sc", 0, 1), ("relay", 1, 5), ("pp", 1, 4), ("sc", 0, 3), ("gw", 1), ("sc", 1, 6),
    ("sc", 1, 0), ("gather2",), ("sc", 1, 2), ("sc", 1, 1), ("sc", 1, 3), ("relay", 1, 4), ("sc", 1, 7), ("gw", 2),
    ("sc", 2, 2), ("sc", 2, 1), ("sc", 0, 5), ("sc", 1, 5), ("sc", 2, 3), ("sc", 2, 0), ("sc", 2, 7), ("sc", 2, 5),
    ("sc", 0, 4), ("sc", 2, 4), ("sc", 1, 4), ("sc", 2, 6), ("share", 1), ("partial", 1), ("whole", 1), ("weigh", 1),
    ("ls", 0), ("ls", 1), ("ls", 2), ("lq",), ("ls", 3), ("lv",), ("cnt",), ("lu",), ("own",), ("fin",),
)


def kernel(
    pts_hbm,
    cands,
    cent_hbm,
    out_sums,
    out_counts,
    pts,
    cent,
    zbufs,
    xs,
    outs,
    relays,
    tab,
    tab_in,
    tab_sm,
    scores,
    tops,
    tops4,
    totals4,
    w,
    lses,
    stats,
    sent_parts,
    parts_in,
    sent_shifts,
    shifts,
    psend,
    precv,
    phold,
    h1,
    h2,
    cur1,
    fb,
    fs,
    fr,
    g,
    q,
    u,
    cnts,
    z_send,
    z_recv,
    y_send,
    x_recv,
    r_recv,
    r_send,
    st_sem,
    tab_sem,
    dp_send,
    dp_recv,
    fin_send,
    fin_recv,
    load_sem,
):
    dp = lax.axis_index("dp")
    cl = lax.axis_index("cluster")
    x, core = lax.div(dp, NC), lax.rem(dp, NC)
    z, y = lax.div(cl, NY), lax.rem(cl, NY)

    sign = 1 - 2 * core

    def at_cluster(k, dy):
        return {"cluster": lax.rem(z + sign * k + NZ, NZ) * NY + lax.rem(y + dy + NY, NY)}

    xp, xm, xo = lax.rem(x + 1, NX), lax.rem(x + 3, NX), lax.rem(x + 2, NX)
    dev_xp, dev_xm = {"dp": xp * NC + core}, {"dp": xm * NC + core}
    dev_core = {"dp": x * NC + 1 - core}
    z_devs = at_cluster(1, 0), at_cluster(-1, 0)
    y_up, y_down = at_cluster(0, 1), at_cluster(0, -1)

    loads = [
        pltpu.make_async_copy(pts_hbm, pts, load_sem.at[0]),
        pltpu.make_async_copy(cent_hbm, cent, load_sem.at[1]),
    ]
    for load in loads:
        load.start()

    barrier = pltpu.get_barrier_semaphore()
    for peer in [at_cluster(k, 0) for k in range(1, NZ)] + [at_cluster(0, p) for p in range(1, NY)]:
        pl.semaphore_signal(barrier, inc=1, device_id=peer, device_id_type=MESH)
    for j in range(1, NX * NC):
        pl.semaphore_signal(
            barrier, inc=1, device_id={"dp": lax.rem(dp + j, NX * NC)}, device_id_type=MESH
        )
    pl.semaphore_wait(barrier, NZ - 1 + NY - 1 + NX * NC - 1)

    drains = []

    def send(src, dst, ssem, rsem, dev):
        copy = pltpu.make_async_remote_copy(
            src_ref=src,
            dst_ref=dst,
            send_sem=ssem,
            recv_sem=rsem,
            device_id=dev,
            device_id_type=MESH,
        )
        copy.start()
        return copy

    def landed(ref, sem):
        pltpu.make_async_copy(ref, ref, sem).wait()

    def later(ref, sem):
        drains.append(lambda: landed(ref, sem))

    def drain():
        for wait in drains:
            wait()
        drains.clear()

    def half(ref, h):
        return ref.at[pl.ds(h * 4, 4)]

    def chunk(step, k):
        return pts.at[step] if k == 0 else zbufs[step * 7 + k - 1]

    def z_start(step, d, i):
        k, h = (PLUS, MINUS)[d][i]
        src = half(pts_hbm.at[step], h)
        dst = half(chunk(step, k), h)
        send(src, dst, z_send.at[step], z_recv.at[step, d, i], z_devs[d])

    def z_event(step, d, i):
        order = (PLUS, MINUS)[d]
        k, h = order[i]
        here = half(chunk(step, k), h)
        landed(here, z_recv.at[step, d, i])
        if i < 5:
            dst = half(chunk(step, order[i + 2][0]), h)
            send(here, dst, z_send.at[step], z_recv.at[step, d, i + 2], z_devs[d])

    def tables():
        row = lax.broadcasted_iota(jnp.int32, (8, 128), 0)
        lane = lax.broadcasted_iota(jnp.int32, (8, 128), 1)
        oz = (z + sign * row) & (NZ - 1)
        second = ((lane >> 5) & 1) == 1
        for step in range(2):
            for t in range(2):
                owner = oz * NY + ((y + t * 2 + (lane >> 6)) & (NY - 1))
                first = jnp.full((8, 128), NB, jnp.int32)
                last = jnp.full((8, 128), -1, jnp.int32)
                for b in range(NB):
                    hit = owner == cands[step, 0, b]
                    for j in range(1, 4):
                        hit = hit | (owner == cands[step, j, b])
                    last = jnp.where(hit, b, last)
                    first = jnp.minimum(first, jnp.where(hit, b, NB))
                lone = jnp.where(first < NB, first, -1)
                bid = jnp.where(second, jnp.where(last > first, last, -1), lone)
                off = step * 256 + t * 128
                tab[:, :, off : off + 128] = bid.reshape(8, 1, 128)
        for k in range(1, NZ):
            send(tab.at[k], tab_in.at[k], tab_sem.at[0], tab_sem.at[1], at_cluster(k, 0))
        later(tab_in.at[pl.ds(1, 7)], tab_sem.at[0])
        tab_in[0] = tab[0]
        to_scalars(tab, 0, 1)

    def to_scalars(table, first, count):
        rows = pl.ds(first, count)
        copy = pltpu.make_async_copy(table.at[rows], tab_sm.at[rows], tab_sem.at[2])
        copy.start()
        copy.wait()

    def tables_in():
        landed(tab_in.at[pl.ds(1, 7)], tab_sem.at[1])
        to_scalars(tab_in, 1, 7)

    def block(step, k, p, s):
        number = tab_sm[k, 0, step * 256 + p * 64 + s * 32]
        return chunk(step, k)[jnp.maximum(number, 0)]

    def pr(step, k):
        for s, dev in enumerate((y_up, y_down)):
            box = outs[step].at[k, 2 + s]
            box[...] = block(step, k, 2, s)
            send(box, relays[step].at[k, s], y_send.at[step], r_recv.at[step, k], dev)

    def pp(step, k):
        xr, box = xs[step], outs[step]
        for p, dev in ((1, y_up), (3, y_down)):
            first = 0 if p == 1 else 4
            for s in range(2):
                box[k, first + s] = block(step, k, p, s)
            there = xr.at[pl.ds(k * 8 + p * 2, 2)]
            send(box.at[k, pl.ds(first, 2)], there, y_send.at[step], x_recv.at[step, k], dev)
        for s in range(2):
            xr[k * 8 + s] = block(step, k, 0, s)

    def relay(step, k):
        landed(relays[step].at[k], r_recv.at[step, k])
        for s, dev in enumerate((y_up, y_down)):
            here, there = relays[step].at[k, s], xs[step].at[k * 8 + 4 + s]
            send(here, there, r_send.at[step], x_recv.at[step, k], dev)

    def points_sent(step):
        landed(xs[step].at[pl.ds(0, 56)], z_send.at[step])
        landed(outs[step], y_send.at[step])
        landed(relays[step], r_send.at[step])

    def arrived(step, k):
        landed(xs[step].at[pl.ds(k * 8 + 2, 6)], x_recv.at[step, k])

    def against(step, k, centroids):
        rows = xs[step][k * 8 : k * 8 + 8].reshape(8 * PB, D)
        return lax.dot_general(
            centroids, rows, (((1,), (1,)), ((), ())), preferred_element_type=F32
        )

    def exps(s):
        top = jnp.max(s, axis=0, keepdims=True)
        e = jnp.exp(s - top)
        return e, top, jnp.sum(e, axis=0, keepdims=True)

    def keep(step, k, lse):
        for i in range(2):
            lses[step][i, k : k + 1, :] = lse[:, i * 128 : (i + 1) * 128]

    def score(k):
        arrived(0, k)
        e, top, total = exps(against(0, k, cent[...]))
        scores[k] = e
        tops[k] = top
        keep(0, k, top + jnp.log(total))

    def sc(part, k):
        if part == 0:
            arrived(1, k)
        which = ((x,), (xm, xp), (xo,))[part]
        places = [cur_rows(c, at) for at in which for c in range(2)]
        s = against(1, k, jnp.concatenate([cur1[rows, :] for rows in places], axis=0))
        for i, at in enumerate(which):
            e, top, total = exps(s[i * 128 : i * 128 + 128])
            scores[k, places[2 * i], :] = e[:64]
            scores[k, places[2 * i + 1], :] = e[64:]
            tops4[at, k] = top
            totals4[at, k] = total

    def join():
        for k in range(NZ):
            top = jnp.maximum(
                jnp.maximum(tops4[0, k], tops4[1, k]), jnp.maximum(tops4[2, k], tops4[3, k])
            )
            total = sum(totals4[i, k] * jnp.exp(tops4[i, k] - top) for i in range(NX))
            keep(1, k, top + jnp.log(total))

    low = lax.broadcasted_iota(jnp.int32, (1, 128), 1) < 64
    group = lax.broadcasted_iota(jnp.int32, (1, 128), 1) >> 5

    def over_groups(op, value):
        value = op(value, pltpu.roll(value, 64, 1))
        return op(value, pltpu.roll(value, 32, 1))

    def block_ids(step):
        return [
            tab_in[:, :, step * 256 + i * 128 : step * 256 + i * 128 + 128].reshape(8, 128)
            for i in range(2)
        ]

    def share(step):
        if step == 1:
            join()
        for p in range(1, NY):
            send(
                lses[step].at[p >> 1],
                stats[step].at[p],
                st_sem.at[step, 0],
                st_sem.at[step, 1],
                at_cluster(0, -p),
            )
        stats[step][0] = lses[step][0]
        later(stats[step].at[pl.ds(1, 3)], st_sem.at[step, 0])

    def partial(step):
        got = stats[step]
        landed(got.at[pl.ds(1, 3)], st_sem.at[step, 1])
        have = [jnp.where(low, got[2 * i], got[2 * i + 1]) for i in range(2)]
        ids = block_ids(step)
        packed = [jnp.full((8, 128), -BIG, F32) for _ in range(2)]
        for b in range(NB):
            mine = [ids[i] == b for i in range(2)]
            masked = [jnp.where(mine[i], have[i], -BIG) for i in range(2)]
            top = over_groups(jnp.maximum, jnp.maximum(masked[0], masked[1]))
            each = [jnp.where(mine[i], jnp.exp(have[i] - top), 0.0) for i in range(2)]
            total = over_groups(jnp.add, each[0] + each[1])
            value = jnp.where(total > 0.0, top + jnp.log(total), -BIG)
            packed[b >> 2] = jnp.where(group == (b & 3), value, packed[b >> 2])
        out = sent_parts[step]
        for i in range(2):
            out[i * 8 : i * 8 + 8, :] = packed[i]
        for j in (4, 3, 5, 2, 6, 1, 7):
            send(
                out,
                parts_in[step].at[j],
                st_sem.at[step, 2],
                st_sem.at[step, 3],
                at_cluster(j, 0),
            )
        later(parts_in[step].at[pl.ds(1, 7)], st_sem.at[step, 2])

    def whole(step):
        into = parts_in[step]
        landed(into.at[pl.ds(1, 7)], st_sem.at[step, 3])
        ids = block_ids(step)
        shift = [jnp.full((8, 128), BIG, F32) for _ in range(2)]
        for i in range(2):
            rows = slice(i * 8, i * 8 + 8)
            seen = [sent_parts[step][rows, :]]
            for j in range(1, NZ):
                seen.append(pltpu.roll(into[j, rows, :], j, 0))
            top = seen[0]
            for j in range(1, NZ):
                top = jnp.maximum(top, seen[j])
            total = jnp.exp(seen[0] - top)
            for j in range(1, NZ):
                total = total + jnp.exp(seen[j] - top)
            value = top + jnp.log(total)
            for b in range(4):
                spread = over_groups(jnp.maximum, jnp.where(group == b, value, -BIG))
                for t in range(2):
                    shift[t] = jnp.where(ids[t] == i * 4 + b, spread, shift[t])
        out, back = sent_shifts[step], shifts[step]
        for t in range(2):
            out[t] = shift[t]
        back[0] = shift[0]
        for p in range(1, NY):
            send(
                out.at[p >> 1],
                back.at[p],
                st_sem.at[step, 4],
                st_sem.at[step, 5],
                at_cluster(0, p),
            )
        later(back.at[pl.ds(1, 3)], st_sem.at[step, 4])

    def weigh(step):
        back = shifts[step]
        landed(back.at[pl.ds(1, 3)], st_sem.at[step, 5])
        for k in range(NZ):
            for t in range(2):
                shift = jnp.where(low, back[2 * t, k : k + 1, :], back[2 * t + 1, k : k + 1, :])
                lanes = pl.ds(k * 256 + t * 128, 128)
                half_lanes = slice(t * 128, (t + 1) * 128)
                if step == 0:
                    scale = jnp.exp(tops[k, :, half_lanes] - shift)
                    w[:, lanes] = (scores[k, :, half_lanes] * scale).astype(BF16)
                    continue
                for at in range(NX):
                    scale = jnp.exp(tops4[at, k, :, half_lanes] - shift)
                    for first in (at * 64, 256 + at * 64):
                        rows = slice(first, first + 64)
                        w[rows, lanes] = (scores[k, rows, half_lanes] * scale).astype(BF16)

    def half_sums(which, n):
        rows = w[pl.ds(pl.multiple_of(which * 256, 256), 256), :]
        cols = xs[0][:, :, n * 256 : (n + 1) * 256].reshape(64 * PB, 256)
        return jnp.dot(rows, cols, preferred_element_type=F32)

    def rows64(at, count=64, shift=0):
        return pl.ds(pl.multiple_of(at * 64 + shift, 32), count)

    def rf(n):
        psend[n] = half_sums(1 - core, n)
        send(psend.at[n], precv.at[n], dp_send.at[0], dp_recv.at[n], dev_core)

    def ro(n):
        phold[n] = half_sums(core, n)

    def rc(n):
        landed(precv.at[n], dp_recv.at[n])
        far = rows64(xo)
        phold[n, far, :] = phold[n, far, :] + precv[n, far, :]
        sides = ((rows64(xo, 32), dev_xp), (rows64(xo, 32, 32), dev_xm))
        for i, (part, dev) in enumerate(sides):
            send(phold.at[n, part, :], h1.at[i, n], dp_send.at[1], dp_recv.at[4 + n], dev)

    def re(n):
        for at in (xp, xm, x):
            near = rows64(at)
            phold[n, near, :] = phold[n, near, :] + precv[n, near, :]
        for i, (at, shift, dev) in enumerate(((xp, 32, dev_xp), (xm, 0, dev_xm))):
            second_hop(n, i, at, shift, dev)

    def second_hop(n, i, at, shift, dev):
        src = phold.at[n, rows64(at, 32, shift), :]
        send(src, h2.at[i, n, pl.ds(shift, 32)], dp_send.at[2], dp_recv.at[8], dev)

    def rh(n):
        landed(h2.at[0, n], dp_recv.at[4 + n])
        for i, (at, shift, dev) in enumerate(((xp, 0, dev_xp), (xm, 32, dev_xm))):
            part = rows64(at, 32, shift)
            phold[n, part, :] = phold[n, part, :] + h1[i, n]
            second_hop(n, i, at, shift, dev)

    def cur_rows(which_core, at, count=64, shift=0):
        return pl.ds(pl.multiple_of(which_core * 256 + at * 64 + shift, 32), count)

    def update():
        landed(h2, dp_recv.at[8])
        own = rows64(x)
        mine = cur_rows(core, x)
        v = [
            cent[mine, n * 256 : (n + 1) * 256].astype(F32)
            + (phold[n, own, :] + h2[0, n] + h2[1, n])
            for n in range(4)
        ]
        square = sum(jnp.sum(part * part, axis=1, keepdims=True) for part in v)
        norm = jnp.sqrt(square + 1e-06)
        for n in range(4):
            cur1[mine, n * 256 : (n + 1) * 256] = (v[n] / norm).astype(BF16)
        own_rows(0)
        to_core(cur1.at[mine], 0)

    def own_rows(second):
        for i, (shift, dev) in enumerate(((0, dev_xp), (32, dev_xm))):
            part = cur1.at[cur_rows(core, x, 32, 32 - shift if second else shift)]
            send(part, part, dp_send.at[3], dp_recv.at[9 + 2 * second + i], dev)

    def ub():
        own_rows(1)

    def to_core(part, group):
        send(part, part, dp_send.at[3], dp_recv.at[15 + group], dev_core)

    def gather1():
        for i, (at, shift, dev) in enumerate(((xm, 0, dev_xp), (xp, 32, dev_xm))):
            part = cur1.at[cur_rows(core, at, 32, shift)]
            landed(part, dp_recv.at[9 + i])
            send(part, part, dp_send.at[3], dp_recv.at[13 + i], dev)
            to_core(part, 1)

    def gather1b():
        for i, (at, shift) in enumerate(((xm, 32), (xp, 0))):
            part = cur1.at[cur_rows(core, at, 32, shift)]
            landed(part, dp_recv.at[11 + i])
            to_core(part, 1)

    def gather2():
        for i, shift in enumerate((0, 32)):
            part = cur1.at[cur_rows(core, xo, 32, shift)]
            landed(part, dp_recv.at[13 + i])
            to_core(part, 2)

    def gw(group):
        landed(cur1.at[pl.ds(0, (64, 128, 64)[group])], dp_recv.at[15 + group])

    def ls(j):
        lanes = pl.ds(pl.multiple_of((xo, xp, xm, x)[j] * 256, 256), 256)
        cols = xs[1][:, :, lanes].reshape(64 * PB, 256)
        part = jnp.dot(w[...], cols, preferred_element_type=F32)
        fb[j, 0] = part[:, :128]
        fb[j, 1] = part[:, 128:]
        fs[j] = fb[j, 1 - core].astype(BF16)
        send(fs.at[j], fr.at[j], fin_send.at[0], fin_recv.at[j], dev_core)
        if j == 3:
            later(fs, fin_send.at[0])

    def both(j):
        landed(fr.at[j], fin_recv.at[j])
        return fb[j, core] + fr[j].astype(F32)

    def lq():
        g[0] = both(0).astype(BF16)
        for i, dev in enumerate((dev_xp, dev_xm)):
            rows = pl.ds(256 * i, 256)
            send(g.at[0, rows], q.at[i], fin_send.at[2], fin_recv.at[5 + i], dev)

    def last_hop(i, rows):
        dev = (dev_xp, dev_xm)[i]
        send(g.at[1 + i, rows], u.at[i, rows], fin_send.at[3], fin_recv.at[7 + i], dev)

    def lv():
        for i in range(2):
            part = both(1 + i)
            rest = pl.ds(256 - 256 * i, 256)
            fb[1 + i, core] = part
            g[1 + i, rest] = part[256 - 256 * i : 512 - 256 * i].astype(BF16)
            last_hop(i, rest)

    def lu():
        for i in range(2):
            landed(q.at[i], fin_recv.at[5 + i])
            rows = pl.ds(256 * i, 256)
            g[1 + i, rows] = (fb[1 + i, core, rows, :] + q[i].astype(F32)).astype(BF16)
            last_hop(i, rows)

    def cnt():
        ones = jnp.ones((8, 64 * PB), BF16)
        count = lax.dot_general(
            ones, w[...], (((1,), (1,)), ((), ())), preferred_element_type=F32
        )
        cnts[dp] = count[0:1]
        for j in range(1, NX * NC):
            send(
                cnts.at[dp],
                cnts.at[dp],
                fin_send.at[1],
                fin_recv.at[4],
                {"dp": lax.rem(dp + j, NX * NC)},
            )
        later(cnts.at[pl.ds(0, 7)], fin_send.at[1])

    def own():
        fb[3, core] = both(3)
        landed(cnts.at[pl.ds(0, 7)], fin_recv.at[4])
        count = cnts[0]
        for j in range(1, NX * NC):
            count = count + cnts[j]
        for j in range(4):
            out_counts[j : j + 1, :] = count[:, j * 128 : (j + 1) * 128]
        drain()
        landed(q, fin_send.at[2])

    def fin():
        landed(u.at[0], fin_recv.at[7])
        landed(u.at[1], fin_recv.at[8])
        landed(u, fin_send.at[3])
        out_sums[...] = fb[3, core] + (u[0].astype(F32) + u[1].astype(F32))

    parts = dict(
        zs=z_start,
        ze=z_event,
        pr=pr,
        pp=pp,
        re=re,
        ub=ub,
        relay=relay,
        score=score,
        share=share,
        partial=partial,
        whole=whole,
        weigh=weigh,
        rf=rf,
        ro=ro,
        rc=rc,
        rh=rh,
        update=update,
        gather1=gather1,
        gather1b=gather1b,
        gather2=gather2,
        gw=gw,
        sc=sc,
        ls=ls,
        lq=lq,
        lu=lu,
        lv=lv,
        cnt=cnt,
        own=own,
        fin=fin,
    )
    for name, *numbers in SCHEDULE:
        if (name, *numbers) == ("pr", 0, 0):
            tables()
            for load in loads:
                load.wait()
        parts[name](*numbers)
        if (name, *numbers) == ("relay", 0, 0):
            tables_in()
        if (name, *numbers) == ("partial", 1):
            points_sent(0)
            points_sent(1)
            landed(psend, dp_send.at[0])
            landed(h1, dp_send.at[1])
            landed(h2, dp_send.at[2])
            landed(cur1.at[pl.ds(0, 448)], dp_send.at[3])


def on_device(points, candidates, centroids):
    vmem, hbm = pl.BlockSpec(memory_space=pltpu.VMEM), pl.BlockSpec(memory_space=pl.ANY)
    sem = pltpu.SemaphoreType.DMA
    steps = points.shape[0]
    sums, counts = pl.pallas_call(
        kernel,
        out_shape=(
            jax.ShapeDtypeStruct((CBS, D // (NX * NC)), F32),
            jax.ShapeDtypeStruct((4, 128), F32),
        ),
        in_specs=[hbm, pl.BlockSpec(memory_space=pltpu.SMEM), hbm],
        out_specs=(vmem, vmem),
        scratch_shapes=[
            pltpu.VMEM((steps, NB, PB, D), BF16),
            pltpu.VMEM((CBS, D), BF16),
            [pltpu.VMEM((NB, PB, D), BF16) for _ in range(7 * steps)],
            [pltpu.VMEM((64, PB, D), BF16) for _ in range(steps)],
            [pltpu.VMEM((NZ, 6, PB, D), BF16) for _ in range(steps)],
            [pltpu.VMEM((NZ, 2, PB, D), BF16) for _ in range(steps)],
            pltpu.VMEM((NZ, 1, 512), jnp.int32),
            pltpu.VMEM((NZ, 1, 512), jnp.int32),
            pltpu.SMEM((NZ, 1, 512), jnp.int32),
            pltpu.VMEM((NZ, CBS, 256), F32),
            pltpu.VMEM((NZ, 1, 256), F32),
            pltpu.VMEM((NX, NZ, 1, 256), F32),
            pltpu.VMEM((NX, NZ, 1, 256), F32),
            pltpu.VMEM((CBS, 64 * PB), BF16),
            [pltpu.VMEM((2, 8, 128), F32) for _ in range(steps)],
            [pltpu.VMEM((4, 8, 128), F32) for _ in range(steps)],
            [pltpu.VMEM((16, 128), F32) for _ in range(steps)],
            [pltpu.VMEM((NZ, 16, 128), F32) for _ in range(steps)],
            [pltpu.VMEM((2, 8, 128), F32) for _ in range(steps)],
            [pltpu.VMEM((4, 8, 128), F32) for _ in range(steps)],
            pltpu.VMEM((4, 256, 256), F32),
            pltpu.VMEM((4, 256, 256), F32),
            pltpu.VMEM((4, 256, 256), F32),
            pltpu.VMEM((2, 4, 32, 256), F32),
            pltpu.VMEM((2, 4, 64, 256), F32),
            pltpu.VMEM((CBS, D), BF16),
            pltpu.VMEM((4, 2, CBS, 128), F32),
            pltpu.VMEM((4, CBS, 128), BF16),
            pltpu.VMEM((4, CBS, 128), BF16),
            pltpu.VMEM((3, CBS, 128), BF16),
            pltpu.VMEM((2, 256, 128), BF16),
            pltpu.VMEM((2, CBS, 128), BF16),
            pltpu.VMEM((NX * NC, 1, CBS), F32),
            sem((steps,)),
            sem((steps, 2, 7)),
            sem((steps,)),
            sem((steps, NZ)),
            sem((steps, NZ)),
            sem((steps,)),
            sem((steps, 6)),
            sem((3,)),
            sem((4,)),
            sem((18,)),
            sem((4,)),
            sem((9,)),
            sem((2,)),
        ],
        compiler_params=pltpu.CompilerParams(
            collective_id=0, has_side_effects=True, vmem_limit_bytes=54250 * 1024
        ),
    )(points.reshape(steps, NB, PB, D), jnp.transpose(candidates, (0, 2, 1)), centroids)
    return sums, counts.reshape(CBS)


def solution(mesh):
    placed = (
        P(None, ("dp", "cluster"), None),
        P(None, ("dp", "cluster"), None),
        P("cluster", None),
    )
    return jax.shard_map(
        on_device,
        mesh=mesh,
        in_specs=placed,
        out_specs=(P("cluster", "dp"), P("cluster")),
        check_vma=False,
    )
```

```python
import jax
import jax.numpy as jnp
from jax import lax
from jax.experimental import pallas as pl
from jax.experimental.pallas import tpu as pltpu
from jax.sharding import PartitionSpec as P

MESH = pl.DeviceIdType.MESH
F32 = jnp.float32
BF16 = jnp.bfloat16
BIG = 3.0e38
NZ, NY, NX, NC = 8, 4, 4, 2
NB, PB, D, CBS = 8, 32, 1024, 512
PLUS = ((1, 0), (1, 1), (2, 0), (2, 1), (3, 0), (3, 1), (4, 0))
MINUS = ((7, 1), (7, 0), (6, 1), (6, 0), (5, 1), (5, 0), (4, 1))
SCHEDULE = (
    ("zs", 0, 0, 0), ("zs", 0, 1, 0), ("pr", 0, 0), ("pp", 0, 0), ("pr", 1, 0), ("pp", 1, 0), ("zs", 0, 0, 1),
    ("zs", 0, 1, 1), ("ze", 0, 0, 0), ("relay", 0, 0), ("relay", 1, 0), ("ze", 0, 1, 0), ("ze", 0, 0, 1), ("pr", 0, 1),
    ("ze", 0, 1, 1), ("pr", 0, 7), ("pp", 0, 7), ("relay", 0, 1), ("pp", 0, 1), ("relay", 0, 7), ("ze", 0, 0, 2),
    ("ze", 0, 1, 2), ("ze", 0, 0, 3), ("pr", 0, 2), ("pp", 0, 2), ("score", 7), ("score", 1), ("ze", 0, 1, 3),
    ("pr", 0, 6), ("pp", 0, 6), ("score", 0), ("ze", 0, 1, 4), ("relay", 0, 2), ("relay", 0, 6), ("ze", 0, 0, 4),
    ("ze", 0, 0, 5), ("pr", 0, 3), ("pp", 0, 3), ("ze", 0, 1, 5), ("pr", 0, 5), ("zs", 1, 0, 0), ("pp", 0, 5),
    ("zs", 1, 1, 0), ("ze", 0, 1, 6), ("ze", 0, 0, 6), ("pr", 0, 4), ("relay", 0, 3), ("score", 2), ("pp", 0, 4),
    ("zs", 1, 1, 1), ("zs", 1, 0, 1), ("score", 6), ("relay", 0, 5), ("ze", 1, 0, 0), ("relay", 0, 4), ("score", 3),
    ("ze", 1, 1, 0), ("score", 5), ("ze", 1, 1, 1), ("pr", 1, 7), ("pp", 1, 7), ("score", 4), ("share", 0),
    ("ze", 1, 0, 1), ("pr", 1, 1), ("pp", 1, 1), ("relay", 1, 7), ("partial", 0), ("relay", 1, 1), ("ze", 1, 0, 2),
    ("ze", 1, 1, 2), ("whole", 0), ("ze", 1, 0, 3), ("ze", 1, 1, 3), ("pr", 1, 2), ("pp", 1, 2), ("pr", 1, 6),
    ("pp", 1, 6), ("weigh", 0), ("rf", 0), ("ro", 0), ("rf", 1), ("ro", 1), ("rf", 2), ("ro", 2), ("rc", 0), ("re", 0),
    ("rf", 3), ("rc", 1), ("rc", 2), ("re", 1), ("ze", 1, 0, 4), ("relay", 1, 6), ("re", 2), ("ro", 3), ("rc", 3),
    ("relay", 1, 2), ("rh", 1), ("ze", 1, 1, 4), ("ze", 1, 0, 5), ("pr", 1, 3), ("re", 3), ("rh", 0), ("pp", 1, 3),
    ("ze", 1, 1, 5), ("pr", 1, 5), ("rh", 2), ("rh", 3), ("update",), ("pp", 1, 5), ("ze", 1, 1, 6), ("ub",),
    ("gw", 0), ("sc", 0, 7), ("sc", 0, 2), ("sc", 0, 0), ("ze", 1, 0, 6), ("relay", 1, 3), ("pr", 1, 4), ("gather1",),
    ("gather1b",), ("sc", 0, 1), ("pp", 1, 4), ("sc", 0, 6), ("relay", 1, 5), ("gw", 1), ("sc", 1, 6), ("sc", 1, 1),
    ("gather2",), ("sc", 1, 7), ("sc", 1, 0), ("sc", 1, 2), ("sc", 0, 3), ("relay", 1, 4), ("gw", 2), ("sc", 2, 3),
    ("sc", 2, 1), ("sc", 1, 3), ("sc", 2, 7), ("sc", 0, 5), ("sc", 1, 5), ("sc", 2, 6), ("sc", 2, 5), ("sc", 2, 2),
    ("sc", 2, 0), ("sc", 0, 4), ("sc", 1, 4), ("sc", 2, 4), ("share", 1), ("partial", 1), ("whole", 1), ("weigh", 1),
    ("ls", 0), ("ls", 1), ("ls", 2), ("lq",), ("ls", 3), ("lv",), ("cnt",), ("lu",), ("own",), ("fin",),
)


def kernel(
    pts_hbm,
    cands,
    cent_hbm,
    out_sums,
    out_counts,
    pts,
    cent,
    zbufs,
    xs,
    outs,
    relays,
    tab,
    tab_in,
    tab_sm,
    scores,
    tops,
    tops4,
    totals4,
    w,
    lses,
    stats,
    sent_parts,
    parts_in,
    sent_shifts,
    shifts,
    psend,
    precv,
    phold,
    h1,
    h2,
    cur1,
    fb,
    fs,
    fr,
    g,
    q,
    u,
    cnts,
    z_send,
    z_recv,
    y_send,
    x_recv,
    r_recv,
    r_send,
    st_sem,
    tab_sem,
    dp_send,
    dp_recv,
    fin_send,
    fin_recv,
    load_sem,
):
    dp = lax.axis_index("dp")
    cl = lax.axis_index("cluster")
    x, core = lax.div(dp, NC), lax.rem(dp, NC)
    z, y = lax.div(cl, NY), lax.rem(cl, NY)

    sign = 1 - 2 * core

    def at_cluster(k, dy):
        return {"cluster": lax.rem(z + sign * k + NZ, NZ) * NY + lax.rem(y + dy + NY, NY)}

    xp, xm, xo = lax.rem(x + 1, NX), lax.rem(x + 3, NX), lax.rem(x + 2, NX)
    dev_xp, dev_xm = {"dp": xp * NC + core}, {"dp": xm * NC + core}
    dev_core = {"dp": x * NC + 1 - core}
    z_devs = at_cluster(1, 0), at_cluster(-1, 0)
    y_up, y_down = at_cluster(0, 1), at_cluster(0, -1)

    loads = [
        pltpu.make_async_copy(pts_hbm, pts, load_sem.at[0]),
        pltpu.make_async_copy(cent_hbm, cent, load_sem.at[1]),
    ]
    for load in loads:
        load.start()

    barrier = pltpu.get_barrier_semaphore()
    for peer in [at_cluster(k, 0) for k in range(1, NZ)] + [at_cluster(0, p) for p in range(1, NY)]:
        pl.semaphore_signal(barrier, inc=1, device_id=peer, device_id_type=MESH)
    for j in range(1, NX * NC):
        pl.semaphore_signal(
            barrier, inc=1, device_id={"dp": lax.rem(dp + j, NX * NC)}, device_id_type=MESH
        )
    pl.semaphore_wait(barrier, NZ - 1 + NY - 1 + NX * NC - 1)

    drains = []

    def send(src, dst, ssem, rsem, dev):
        copy = pltpu.make_async_remote_copy(
            src_ref=src,
            dst_ref=dst,
            send_sem=ssem,
            recv_sem=rsem,
            device_id=dev,
            device_id_type=MESH,
        )
        copy.start()
        return copy

    def landed(ref, sem):
        pltpu.make_async_copy(ref, ref, sem).wait()

    def later(ref, sem):
        drains.append(lambda: landed(ref, sem))

    def drain():
        for wait in drains:
            wait()
        drains.clear()

    def half(ref, h):
        return ref.at[pl.ds(h * 4, 4)]

    def chunk(step, k):
        return pts.at[step] if k == 0 else zbufs[step * 7 + k - 1]

    def z_start(step, d, i):
        k, h = (PLUS, MINUS)[d][i]
        src = half(pts_hbm.at[step], h)
        dst = half(chunk(step, k), h)
        send(src, dst, z_send.at[step], z_recv.at[step, d, i], z_devs[d])

    def z_event(step, d, i):
        order = (PLUS, MINUS)[d]
        k, h = order[i]
        here = half(chunk(step, k), h)
        landed(here, z_recv.at[step, d, i])
        if i < 5:
            dst = half(chunk(step, order[i + 2][0]), h)
            send(here, dst, z_send.at[step], z_recv.at[step, d, i + 2], z_devs[d])

    def tables():
        row = lax.broadcasted_iota(jnp.int32, (8, 128), 0)
        lane = lax.broadcasted_iota(jnp.int32, (8, 128), 1)
        oz = (z + sign * row) & (NZ - 1)
        second = ((lane >> 5) & 1) == 1
        for step in range(2):
            for t in range(2):
                owner = oz * NY + ((y + t * 2 + (lane >> 6)) & (NY - 1))
                first = jnp.full((8, 128), NB, jnp.int32)
                last = jnp.full((8, 128), -1, jnp.int32)
                for b in range(NB):
                    hit = owner == cands[step, 0, b]
                    for j in range(1, 4):
                        hit = hit | (owner == cands[step, j, b])
                    last = jnp.where(hit, b, last)
                    first = jnp.minimum(first, jnp.where(hit, b, NB))
                lone = jnp.where(first < NB, first, -1)
                bid = jnp.where(second, jnp.where(last > first, last, -1), lone)
                off = step * 256 + t * 128
                tab[:, :, off : off + 128] = bid.reshape(8, 1, 128)
        for k in range(1, NZ):
            send(tab.at[k], tab_in.at[k], tab_sem.at[0], tab_sem.at[1], at_cluster(k, 0))
        later(tab_in.at[pl.ds(1, 7)], tab_sem.at[0])
        tab_in[0] = tab[0]
        to_scalars(tab, 0, 1)

    def to_scalars(table, first, count):
        rows = pl.ds(first, count)
        copy = pltpu.make_async_copy(table.at[rows], tab_sm.at[rows], tab_sem.at[2])
        copy.start()
        copy.wait()

    def tables_in():
        landed(tab_in.at[pl.ds(1, 7)], tab_sem.at[1])
        to_scalars(tab_in, 1, 7)

    def block(step, k, p, s):
        number = tab_sm[k, 0, step * 256 + p * 64 + s * 32]
        return chunk(step, k)[jnp.maximum(number, 0)]

    def pr(step, k):
        for s, dev in enumerate((y_up, y_down)):
            box = outs[step].at[k, 2 + s]
            box[...] = block(step, k, 2, s)
            send(box, relays[step].at[k, s], y_send.at[step], r_recv.at[step, k], dev)

    def pp(step, k):
        xr, box = xs[step], outs[step]
        for p, dev in ((1, y_up), (3, y_down)):
            first = 0 if p == 1 else 4
            for s in range(2):
                box[k, first + s] = block(step, k, p, s)
            there = xr.at[pl.ds(k * 8 + p * 2, 2)]
            send(box.at[k, pl.ds(first, 2)], there, y_send.at[step], x_recv.at[step, k], dev)
        for s in range(2):
            xr[k * 8 + s] = block(step, k, 0, s)

    def relay(step, k):
        landed(relays[step].at[k], r_recv.at[step, k])
        for s, dev in enumerate((y_up, y_down)):
            here, there = relays[step].at[k, s], xs[step].at[k * 8 + 4 + s]
            send(here, there, r_send.at[step], x_recv.at[step, k], dev)

    def points_sent(step):
        landed(xs[step].at[pl.ds(0, 56)], z_send.at[step])
        landed(outs[step], y_send.at[step])
        landed(relays[step], r_send.at[step])

    def arrived(step, k):
        landed(xs[step].at[pl.ds(k * 8 + 2, 6)], x_recv.at[step, k])

    def against(step, k, centroids):
        rows = xs[step][k * 8 : k * 8 + 8].reshape(8 * PB, D)
        return lax.dot_general(
            centroids, rows, (((1,), (1,)), ((), ())), preferred_element_type=F32
        )

    def exps(s):
        top = jnp.max(s, axis=0, keepdims=True)
        e = jnp.exp(s - top)
        return e, top, jnp.sum(e, axis=0, keepdims=True)

    def keep(step, k, lse):
        for i in range(2):
            lses[step][i, k : k + 1, :] = lse[:, i * 128 : (i + 1) * 128]

    def score(k):
        arrived(0, k)
        e, top, total = exps(against(0, k, cent[...]))
        scores[k] = e
        tops[k] = top
        keep(0, k, top + jnp.log(total))

    def sc(part, k):
        if part == 0:
            arrived(1, k)
        which = ((x,), (xm, xp), (xo,))[part]
        places = [cur_rows(c, at) for at in which for c in range(2)]
        s = against(1, k, jnp.concatenate([cur1[rows, :] for rows in places], axis=0))
        for i, at in enumerate(which):
            e, top, total = exps(s[i * 128 : i * 128 + 128])
            scores[k, places[2 * i], :] = e[:64]
            scores[k, places[2 * i + 1], :] = e[64:]
            tops4[at, k] = top
            totals4[at, k] = total

    def join():
        for k in range(NZ):
            top = jnp.maximum(
                jnp.maximum(tops4[0, k], tops4[1, k]), jnp.maximum(tops4[2, k], tops4[3, k])
            )
            total = sum(totals4[i, k] * jnp.exp(tops4[i, k] - top) for i in range(NX))
            keep(1, k, top + jnp.log(total))

    low = lax.broadcasted_iota(jnp.int32, (1, 128), 1) < 64
    group = lax.broadcasted_iota(jnp.int32, (1, 128), 1) >> 5

    def over_groups(op, value):
        value = op(value, pltpu.roll(value, 64, 1))
        return op(value, pltpu.roll(value, 32, 1))

    def block_ids(step):
        return [
            tab_in[:, :, step * 256 + i * 128 : step * 256 + i * 128 + 128].reshape(8, 128)
            for i in range(2)
        ]

    def share(step):
        if step == 1:
            join()
        for p in range(1, NY):
            send(
                lses[step].at[p >> 1],
                stats[step].at[p],
                st_sem.at[step, 0],
                st_sem.at[step, 1],
                at_cluster(0, -p),
            )
        stats[step][0] = lses[step][0]
        later(stats[step].at[pl.ds(1, 3)], st_sem.at[step, 0])

    def partial(step):
        got = stats[step]
        landed(got.at[pl.ds(1, 3)], st_sem.at[step, 1])
        have = [jnp.where(low, got[2 * i], got[2 * i + 1]) for i in range(2)]
        ids = block_ids(step)
        packed = [jnp.full((8, 128), -BIG, F32) for _ in range(2)]
        for b in range(NB):
            mine = [ids[i] == b for i in range(2)]
            masked = [jnp.where(mine[i], have[i], -BIG) for i in range(2)]
            top = over_groups(jnp.maximum, jnp.maximum(masked[0], masked[1]))
            each = [jnp.where(mine[i], jnp.exp(have[i] - top), 0.0) for i in range(2)]
            total = over_groups(jnp.add, each[0] + each[1])
            value = jnp.where(total > 0.0, top + jnp.log(total), -BIG)
            packed[b >> 2] = jnp.where(group == (b & 3), value, packed[b >> 2])
        out = sent_parts[step]
        for i in range(2):
            out[i * 8 : i * 8 + 8, :] = packed[i]
        for j in (4, 3, 5, 2, 6, 1, 7):
            send(
                out,
                parts_in[step].at[j],
                st_sem.at[step, 2],
                st_sem.at[step, 3],
                at_cluster(j, 0),
            )
        later(parts_in[step].at[pl.ds(1, 7)], st_sem.at[step, 2])

    def whole(step):
        into = parts_in[step]
        landed(into.at[pl.ds(1, 7)], st_sem.at[step, 3])
        ids = block_ids(step)
        shift = [jnp.full((8, 128), BIG, F32) for _ in range(2)]
        for i in range(2):
            rows = slice(i * 8, i * 8 + 8)
            seen = [sent_parts[step][rows, :]]
            for j in range(1, NZ):
                seen.append(pltpu.roll(into[j, rows, :], j, 0))
            top = seen[0]
            for j in range(1, NZ):
                top = jnp.maximum(top, seen[j])
            total = jnp.exp(seen[0] - top)
            for j in range(1, NZ):
                total = total + jnp.exp(seen[j] - top)
            value = top + jnp.log(total)
            for b in range(4):
                spread = over_groups(jnp.maximum, jnp.where(group == b, value, -BIG))
                for t in range(2):
                    shift[t] = jnp.where(ids[t] == i * 4 + b, spread, shift[t])
        out, back = sent_shifts[step], shifts[step]
        for t in range(2):
            out[t] = shift[t]
        back[0] = shift[0]
        for p in range(1, NY):
            send(
                out.at[p >> 1],
                back.at[p],
                st_sem.at[step, 4],
                st_sem.at[step, 5],
                at_cluster(0, p),
            )
        later(back.at[pl.ds(1, 3)], st_sem.at[step, 4])

    def weigh(step):
        back = shifts[step]
        landed(back.at[pl.ds(1, 3)], st_sem.at[step, 5])
        for k in range(NZ):
            for t in range(2):
                shift = jnp.where(low, back[2 * t, k : k + 1, :], back[2 * t + 1, k : k + 1, :])
                lanes = pl.ds(k * 256 + t * 128, 128)
                half_lanes = slice(t * 128, (t + 1) * 128)
                if step == 0:
                    scale = jnp.exp(tops[k, :, half_lanes] - shift)
                    w[:, lanes] = (scores[k, :, half_lanes] * scale).astype(BF16)
                    continue
                for at in range(NX):
                    scale = jnp.exp(tops4[at, k, :, half_lanes] - shift)
                    for first in (at * 64, 256 + at * 64):
                        rows = slice(first, first + 64)
                        w[rows, lanes] = (scores[k, rows, half_lanes] * scale).astype(BF16)

    def half_sums(which, n):
        rows = w[pl.ds(pl.multiple_of(which * 256, 256), 256), :]
        cols = xs[0][:, :, n * 256 : (n + 1) * 256].reshape(64 * PB, 256)
        return jnp.dot(rows, cols, preferred_element_type=F32)

    def rows64(at, count=64, shift=0):
        return pl.ds(pl.multiple_of(at * 64 + shift, 32), count)

    def rf(n):
        psend[n] = half_sums(1 - core, n)
        send(psend.at[n], precv.at[n], dp_send.at[0], dp_recv.at[n], dev_core)

    def ro(n):
        phold[n] = half_sums(core, n)

    def rc(n):
        landed(precv.at[n], dp_recv.at[n])
        far = rows64(xo)
        phold[n, far, :] = phold[n, far, :] + precv[n, far, :]
        sides = ((rows64(xo, 32), dev_xp), (rows64(xo, 32, 32), dev_xm))
        for i, (part, dev) in enumerate(sides):
            send(phold.at[n, part, :], h1.at[i, n], dp_send.at[1], dp_recv.at[4 + n], dev)

    def re(n):
        for at in (xp, xm, x):
            near = rows64(at)
            phold[n, near, :] = phold[n, near, :] + precv[n, near, :]
        for i, (at, shift, dev) in enumerate(((xp, 32, dev_xp), (xm, 0, dev_xm))):
            second_hop(n, i, at, shift, dev)

    def second_hop(n, i, at, shift, dev):
        src = phold.at[n, rows64(at, 32, shift), :]
        send(src, h2.at[i, n, pl.ds(shift, 32)], dp_send.at[2], dp_recv.at[8], dev)

    def rh(n):
        landed(h2.at[0, n], dp_recv.at[4 + n])
        for i, (at, shift, dev) in enumerate(((xp, 0, dev_xp), (xm, 32, dev_xm))):
            part = rows64(at, 32, shift)
            phold[n, part, :] = phold[n, part, :] + h1[i, n]
            second_hop(n, i, at, shift, dev)

    def cur_rows(which_core, at, count=64, shift=0):
        return pl.ds(pl.multiple_of(which_core * 256 + at * 64 + shift, 32), count)

    def update():
        landed(h2, dp_recv.at[8])
        own = rows64(x)
        mine = cur_rows(core, x)
        v = [
            cent[mine, n * 256 : (n + 1) * 256].astype(F32)
            + (phold[n, own, :] + h2[0, n] + h2[1, n])
            for n in range(4)
        ]
        square = sum(jnp.sum(part * part, axis=1, keepdims=True) for part in v)
        norm = jnp.sqrt(square + 1e-06)
        for n in range(4):
            cur1[mine, n * 256 : (n + 1) * 256] = (v[n] / norm).astype(BF16)
        own_rows(0)
        to_core(cur1.at[mine], 0)

    def own_rows(second):
        for i, (shift, dev) in enumerate(((0, dev_xp), (32, dev_xm))):
            part = cur1.at[cur_rows(core, x, 32, 32 - shift if second else shift)]
            send(part, part, dp_send.at[3], dp_recv.at[9 + 2 * second + i], dev)

    def ub():
        own_rows(1)

    def to_core(part, group):
        send(part, part, dp_send.at[3], dp_recv.at[15 + group], dev_core)

    def gather1():
        for i, (at, shift, dev) in enumerate(((xm, 0, dev_xp), (xp, 32, dev_xm))):
            part = cur1.at[cur_rows(core, at, 32, shift)]
            landed(part, dp_recv.at[9 + i])
            send(part, part, dp_send.at[3], dp_recv.at[13 + i], dev)
            to_core(part, 1)

    def gather1b():
        for i, (at, shift) in enumerate(((xm, 32), (xp, 0))):
            part = cur1.at[cur_rows(core, at, 32, shift)]
            landed(part, dp_recv.at[11 + i])
            to_core(part, 1)

    def gather2():
        for i, shift in enumerate((0, 32)):
            part = cur1.at[cur_rows(core, xo, 32, shift)]
            landed(part, dp_recv.at[13 + i])
            to_core(part, 2)

    def gw(group):
        landed(cur1.at[pl.ds(0, (64, 128, 64)[group])], dp_recv.at[15 + group])

    def ls(j):
        lanes = pl.ds(pl.multiple_of((xo, xp, xm, x)[j] * 256, 256), 256)
        cols = xs[1][:, :, lanes].reshape(64 * PB, 256)
        part = jnp.dot(w[...], cols, preferred_element_type=F32)
        fb[j, 0] = part[:, :128]
        fb[j, 1] = part[:, 128:]
        fs[j] = fb[j, 1 - core].astype(BF16)
        send(fs.at[j], fr.at[j], fin_send.at[0], fin_recv.at[j], dev_core)
        if j == 3:
            later(fs, fin_send.at[0])

    def both(j):
        landed(fr.at[j], fin_recv.at[j])
        return fb[j, core] + fr[j].astype(F32)

    def lq():
        g[0] = both(0).astype(BF16)
        for i, dev in enumerate((dev_xp, dev_xm)):
            rows = pl.ds(256 * i, 256)
            send(g.at[0, rows], q.at[i], fin_send.at[2], fin_recv.at[5 + i], dev)

    def last_hop(i, rows):
        dev = (dev_xp, dev_xm)[i]
        send(g.at[1 + i, rows], u.at[i, rows], fin_send.at[3], fin_recv.at[7 + i], dev)

    def lv():
        for i in range(2):
            part = both(1 + i)
            rest = pl.ds(256 - 256 * i, 256)
            fb[1 + i, core] = part
            g[1 + i, rest] = part[256 - 256 * i : 512 - 256 * i].astype(BF16)
            last_hop(i, rest)

    def lu():
        for i in range(2):
            landed(q.at[i], fin_recv.at[5 + i])
            rows = pl.ds(256 * i, 256)
            g[1 + i, rows] = (fb[1 + i, core, rows, :] + q[i].astype(F32)).astype(BF16)
            last_hop(i, rows)

    def cnt():
        ones = jnp.ones((8, 64 * PB), BF16)
        count = lax.dot_general(
            ones, w[...], (((1,), (1,)), ((), ())), preferred_element_type=F32
        )
        cnts[dp] = count[0:1]
        for j in range(1, NX * NC):
            send(
                cnts.at[dp],
                cnts.at[dp],
                fin_send.at[1],
                fin_recv.at[4],
                {"dp": lax.rem(dp + j, NX * NC)},
            )
        later(cnts.at[pl.ds(0, 7)], fin_send.at[1])

    def own():
        fb[3, core] = both(3)
        landed(cnts.at[pl.ds(0, 7)], fin_recv.at[4])
        count = cnts[0]
        for j in range(1, NX * NC):
            count = count + cnts[j]
        for j in range(4):
            out_counts[j : j + 1, :] = count[:, j * 128 : (j + 1) * 128]
        drain()
        landed(q, fin_send.at[2])

    def fin():
        landed(u.at[0], fin_recv.at[7])
        landed(u.at[1], fin_recv.at[8])
        landed(u, fin_send.at[3])
        out_sums[...] = fb[3, core] + (u[0].astype(F32) + u[1].astype(F32))

    parts = dict(
        zs=z_start,
        ze=z_event,
        pr=pr,
        pp=pp,
        re=re,
        ub=ub,
        relay=relay,
        score=score,
        share=share,
        partial=partial,
        whole=whole,
        weigh=weigh,
        rf=rf,
        ro=ro,
        rc=rc,
        rh=rh,
        update=update,
        gather1=gather1,
        gather1b=gather1b,
        gather2=gather2,
        gw=gw,
        sc=sc,
        ls=ls,
        lq=lq,
        lu=lu,
        lv=lv,
        cnt=cnt,
        own=own,
        fin=fin,
    )
    for name, *numbers in SCHEDULE:
        if (name, *numbers) == ("pr", 0, 0):
            tables()
            for load in loads:
                load.wait()
        parts[name](*numbers)
        if (name, *numbers) == ("relay", 0, 0):
            tables_in()
        if (name, *numbers) == ("partial", 1):
            points_sent(0)
            points_sent(1)
            landed(psend, dp_send.at[0])
            landed(h1, dp_send.at[1])
            landed(h2, dp_send.at[2])
            landed(cur1.at[pl.ds(0, 448)], dp_send.at[3])


def on_device(points, candidates, centroids):
    vmem, hbm = pl.BlockSpec(memory_space=pltpu.VMEM), pl.BlockSpec(memory_space=pl.ANY)
    sem = pltpu.SemaphoreType.DMA
    steps = points.shape[0]
    sums, counts = pl.pallas_call(
        kernel,
        out_shape=(
            jax.ShapeDtypeStruct((CBS, D // (NX * NC)), F32),
            jax.ShapeDtypeStruct((4, 128), F32),
        ),
        in_specs=[hbm, pl.BlockSpec(memory_space=pltpu.SMEM), hbm],
        out_specs=(vmem, vmem),
        scratch_shapes=[
            pltpu.VMEM((steps, NB, PB, D), BF16),
            pltpu.VMEM((CBS, D), BF16),
            [pltpu.VMEM((NB, PB, D), BF16) for _ in range(7 * steps)],
            [pltpu.VMEM((64, PB, D), BF16) for _ in range(steps)],
            [pltpu.VMEM((NZ, 6, PB, D), BF16) for _ in range(steps)],
            [pltpu.VMEM((NZ, 2, PB, D), BF16) for _ in range(steps)],
            pltpu.VMEM((NZ, 1, 512), jnp.int32),
            pltpu.VMEM((NZ, 1, 512), jnp.int32),
            pltpu.SMEM((NZ, 1, 512), jnp.int32),
            pltpu.VMEM((NZ, CBS, 256), F32),
            pltpu.VMEM((NZ, 1, 256), F32),
            pltpu.VMEM((NX, NZ, 1, 256), F32),
            pltpu.VMEM((NX, NZ, 1, 256), F32),
            pltpu.VMEM((CBS, 64 * PB), BF16),
            [pltpu.VMEM((2, 8, 128), F32) for _ in range(steps)],
            [pltpu.VMEM((4, 8, 128), F32) for _ in range(steps)],
            [pltpu.VMEM((16, 128), F32) for _ in range(steps)],
            [pltpu.VMEM((NZ, 16, 128), F32) for _ in range(steps)],
            [pltpu.VMEM((2, 8, 128), F32) for _ in range(steps)],
            [pltpu.VMEM((4, 8, 128), F32) for _ in range(steps)],
            pltpu.VMEM((4, 256, 256), F32),
            pltpu.VMEM((4, 256, 256), F32),
            pltpu.VMEM((4, 256, 256), F32),
            pltpu.VMEM((2, 4, 32, 256), F32),
            pltpu.VMEM((2, 4, 64, 256), F32),
            pltpu.VMEM((CBS, D), BF16),
            pltpu.VMEM((4, 2, CBS, 128), F32),
            pltpu.VMEM((4, CBS, 128), BF16),
            pltpu.VMEM((4, CBS, 128), BF16),
            pltpu.VMEM((3, CBS, 128), BF16),
            pltpu.VMEM((2, 256, 128), BF16),
            pltpu.VMEM((2, CBS, 128), BF16),
            pltpu.VMEM((NX * NC, 1, CBS), F32),
            sem((steps,)),
            sem((steps, 2, 7)),
            sem((steps,)),
            sem((steps, NZ)),
            sem((steps, NZ)),
            sem((steps,)),
            sem((steps, 6)),
            sem((3,)),
            sem((4,)),
            sem((18,)),
            sem((4,)),
            sem((9,)),
            sem((2,)),
        ],
        compiler_params=pltpu.CompilerParams(
            collective_id=0, has_side_effects=True, vmem_limit_bytes=54250 * 1024
        ),
    )(points.reshape(steps, NB, PB, D), jnp.transpose(candidates, (0, 2, 1)), centroids)
    return sums, counts.reshape(CBS)


def solution(mesh):
    placed = (
        P(None, ("dp", "cluster"), None),
        P(None, ("dp", "cluster"), None),
        P("cluster", None),
    )
    return jax.shard_map(
        on_device,
        mesh=mesh,
        in_specs=placed,
        out_specs=(P("cluster", "dp"), P("cluster")),
        check_vma=False,
    )
```

```python
import jax
import jax.numpy as jnp
from jax import lax
from jax.experimental import pallas as pl
from jax.experimental.pallas import tpu as pltpu
from jax.sharding import PartitionSpec as P

MESH = pl.DeviceIdType.MESH
F32 = jnp.float32
BF16 = jnp.bfloat16
BIG = 3.0e38
NZ, NY, NX, NC = 8, 4, 4, 2
NB, PB, D, CBS = 8, 32, 1024, 512
PLUS = ((1, 0), (1, 1), (2, 0), (2, 1), (3, 0), (3, 1), (4, 0))
MINUS = ((7, 1), (7, 0), (6, 1), (6, 0), (5, 1), (5, 0), (4, 1))
SCHEDULE = (
    ("zs", 0, 0, 0), ("zs", 0, 1, 0), ("pr", 0, 0), ("pp", 0, 0), ("zs", 0, 0, 1), ("pr", 1, 0), ("pp", 1, 0),
    ("zs", 0, 1, 1), ("relay", 1, 0), ("relay", 0, 0), ("ze", 0, 0, 0), ("ze", 0, 1, 0), ("ze", 0, 0, 1), ("pr", 0, 1),
    ("ze", 0, 1, 1), ("pr", 0, 7), ("pp", 0, 7), ("relay", 0, 1), ("pp", 0, 1), ("relay", 0, 7), ("ze", 0, 0, 2),
    ("ze", 0, 1, 2), ("ze", 0, 0, 3), ("pr", 0, 2), ("pp", 0, 2), ("score", 1), ("ze", 0, 1, 3), ("pr", 0, 6),
    ("pp", 0, 6), ("score", 0), ("relay", 0, 2), ("ze", 0, 1, 4), ("relay", 0, 6), ("ze", 0, 0, 4), ("ze", 0, 0, 5),
    ("pr", 0, 3), ("pp", 0, 3), ("ze", 0, 1, 5), ("pr", 0, 5), ("zs", 1, 0, 0), ("pp", 0, 5), ("zs", 1, 1, 0),
    ("score", 7), ("ze", 0, 0, 6), ("ze", 0, 1, 6), ("zs", 1, 0, 1), ("pr", 0, 4), ("relay", 0, 3), ("relay", 0, 5),
    ("score", 2), ("pp", 0, 4), ("zs", 1, 1, 1), ("score", 6), ("relay", 0, 4), ("ze", 1, 0, 0), ("score", 3),
    ("ze", 1, 1, 0), ("score", 5), ("ze", 1, 1, 1), ("pr", 1, 7), ("pp", 1, 7), ("score", 4), ("share", 0),
    ("ze", 1, 0, 1), ("pr", 1, 1), ("pp", 1, 1), ("partial", 0), ("relay", 1, 7), ("relay", 1, 1), ("ze", 1, 0, 2),
    ("ze", 1, 1, 2), ("whole", 0), ("ze", 1, 0, 3), ("pr", 1, 2), ("pp", 1, 2), ("ze", 1, 1, 3), ("pr", 1, 6),
    ("pp", 1, 6), ("wa",), ("rf", 0), ("wb",), ("ro", 0), ("rf", 1), ("ro", 1), ("rf", 2), ("ro", 2), ("rc", 0),
    ("re", 0), ("rf", 3), ("rc", 1), ("re", 1), ("relay", 1, 2), ("rc", 2), ("re", 2), ("ro", 3), ("rc", 3),
    ("ze", 1, 0, 4), ("ze", 1, 0, 5), ("pr", 1, 3), ("ze", 1, 1, 4), ("rh", 0), ("re", 3), ("rh", 1), ("relay", 1, 6),
    ("rh", 2), ("pp", 1, 3), ("rh", 3), ("relay", 1, 3), ("update",), ("ze", 1, 1, 5), ("pr", 1, 5), ("ze", 1, 1, 6),
    ("ub",), ("pp", 1, 5), ("gw", 0), ("sc", 0, 0), ("sc", 0, 7), ("sc", 0, 6), ("ze", 1, 0, 6), ("pr", 1, 4),
    ("gather1",), ("gather1b",), ("sc", 0, 3), ("relay", 1, 5), ("sc", 0, 1), ("pp", 1, 4), ("sc", 0, 2), ("gw", 1),
    ("sc", 1, 0), ("sc", 1, 2), ("gather2",), ("sc", 1, 3), ("sc", 1, 6), ("relay", 1, 4), ("sc", 1, 7), ("sc", 1, 1),
    ("gw", 2), ("sc", 2, 2), ("sc", 2, 3), ("sc", 2, 1), ("sc", 2, 0), ("sc", 2, 7), ("sc", 0, 5), ("sc", 2, 6),
    ("sc", 2, 5), ("sc", 1, 5), ("sc", 0, 4), ("sc", 2, 4), ("sc", 1, 4), ("share", 1), ("partial", 1), ("whole", 1),
    ("weigh",), ("ls", 0), ("ls", 1), ("ls", 2), ("lq",), ("ls", 3), ("lv",), ("cnt",), ("lu",), ("own",), ("fin",),
)


def kernel(
    pts_hbm,
    cands,
    cent_hbm,
    out_sums,
    out_counts,
    pts,
    cent,
    zbufs,
    xs,
    outs,
    relays,
    tab,
    tab_in,
    tab_sm,
    scores,
    tops,
    tops4,
    totals4,
    w,
    lses,
    stats,
    sent_parts,
    parts_in,
    sent_shifts,
    shifts,
    psend,
    precv,
    phold,
    h1,
    h2,
    cur1,
    fb,
    fs,
    fr,
    g,
    q,
    u,
    cnts,
    z_send,
    z_recv,
    y_send,
    x_recv,
    r_recv,
    r_send,
    st_sem,
    tab_sem,
    dp_send,
    dp_recv,
    fin_send,
    fin_recv,
    load_sem,
):
    dp = lax.axis_index("dp")
    cl = lax.axis_index("cluster")
    x, core = lax.div(dp, NC), lax.rem(dp, NC)
    z, y = lax.div(cl, NY), lax.rem(cl, NY)

    sign = 1 - 2 * core

    def at_cluster(k, dy):
        return {"cluster": lax.rem(z + sign * k + NZ, NZ) * NY + lax.rem(y + dy + NY, NY)}

    xp, xm, xo = lax.rem(x + 1, NX), lax.rem(x + 3, NX), lax.rem(x + 2, NX)
    dev_xp, dev_xm = {"dp": xp * NC + core}, {"dp": xm * NC + core}
    dev_core = {"dp": x * NC + 1 - core}
    z_devs = at_cluster(1, 0), at_cluster(-1, 0)
    y_up, y_down = at_cluster(0, 1), at_cluster(0, -1)

    loads = [
        pltpu.make_async_copy(pts_hbm, pts, load_sem.at[0]),
        pltpu.make_async_copy(cent_hbm, cent, load_sem.at[1]),
    ]
    for load in loads:
        load.start()

    barrier = pltpu.get_barrier_semaphore()
    for peer in [at_cluster(k, 0) for k in range(1, NZ)] + [at_cluster(0, p) for p in range(1, NY)]:
        pl.semaphore_signal(barrier, inc=1, device_id=peer, device_id_type=MESH)
    for j in range(1, NX * NC):
        pl.semaphore_signal(
            barrier, inc=1, device_id={"dp": lax.rem(dp + j, NX * NC)}, device_id_type=MESH
        )
    pl.semaphore_wait(barrier, NZ - 1 + NY - 1 + NX * NC - 1)

    drains = []

    def send(src, dst, ssem, rsem, dev):
        copy = pltpu.make_async_remote_copy(
            src_ref=src,
            dst_ref=dst,
            send_sem=ssem,
            recv_sem=rsem,
            device_id=dev,
            device_id_type=MESH,
        )
        copy.start()
        return copy

    def landed(ref, sem):
        pltpu.make_async_copy(ref, ref, sem).wait()

    def later(ref, sem):
        drains.append(lambda: landed(ref, sem))

    def drain():
        for wait in drains:
            wait()
        drains.clear()

    def half(ref, h):
        return ref.at[pl.ds(h * 4, 4)]

    def chunk(step, k):
        return pts.at[step] if k == 0 else zbufs[step * 7 + k - 1]

    def z_start(step, d, i):
        k, h = (PLUS, MINUS)[d][i]
        src = half(pts_hbm.at[step], h)
        dst = half(chunk(step, k), h)
        send(src, dst, z_send.at[step], z_recv.at[step, d, i], z_devs[d])

    def z_event(step, d, i):
        order = (PLUS, MINUS)[d]
        k, h = order[i]
        here = half(chunk(step, k), h)
        landed(here, z_recv.at[step, d, i])
        if i < 5:
            dst = half(chunk(step, order[i + 2][0]), h)
            send(here, dst, z_send.at[step], z_recv.at[step, d, i + 2], z_devs[d])

    def tables():
        row = lax.broadcasted_iota(jnp.int32, (8, 128), 0)
        lane = lax.broadcasted_iota(jnp.int32, (8, 128), 1)
        oz = (z + sign * row) & (NZ - 1)
        second = ((lane >> 5) & 1) == 1
        for step in range(2):
            for t in range(2):
                owner = oz * NY + ((y + t * 2 + (lane >> 6)) & (NY - 1))
                first = jnp.full((8, 128), NB, jnp.int32)
                last = jnp.full((8, 128), -1, jnp.int32)
                for b in range(NB):
                    hit = owner == cands[step, 0, b]
                    for j in range(1, 4):
                        hit = hit | (owner == cands[step, j, b])
                    last = jnp.where(hit, b, last)
                    first = jnp.minimum(first, jnp.where(hit, b, NB))
                lone = jnp.where(first < NB, first, -1)
                bid = jnp.where(second, jnp.where(last > first, last, -1), lone)
                off = step * 256 + t * 128
                tab[:, :, off : off + 128] = bid.reshape(8, 1, 128)
        for k in range(1, NZ):
            send(tab.at[k], tab_in.at[k], tab_sem.at[0], tab_sem.at[1], at_cluster(k, 0))
        later(tab_in.at[pl.ds(1, 7)], tab_sem.at[0])
        tab_in[0] = tab[0]
        to_scalars(tab, 0, 1)

    def to_scalars(table, first, count):
        rows = pl.ds(first, count)
        copy = pltpu.make_async_copy(table.at[rows], tab_sm.at[rows], tab_sem.at[2])
        copy.start()
        copy.wait()

    def tables_in():
        landed(tab_in.at[pl.ds(1, 7)], tab_sem.at[1])
        to_scalars(tab_in, 1, 7)

    def block(step, k, p, s):
        number = tab_sm[k, 0, step * 256 + p * 64 + s * 32]
        return chunk(step, k)[jnp.maximum(number, 0)]

    def pr(step, k):
        for s, dev in enumerate((y_up, y_down)):
            box = outs[step].at[k, 2 + s]
            box[...] = block(step, k, 2, s)
            send(box, relays[step].at[k, s], y_send.at[step], r_recv.at[step, k], dev)

    def pp(step, k):
        xr, box = xs[step], outs[step]
        for p, dev in ((1, y_up), (3, y_down)):
            first = 0 if p == 1 else 4
            for s in range(2):
                box[k, first + s] = block(step, k, p, s)
            there = xr.at[pl.ds(k * 8 + p * 2, 2)]
            send(box.at[k, pl.ds(first, 2)], there, y_send.at[step], x_recv.at[step, k], dev)
        for s in range(2):
            xr[k * 8 + s] = block(step, k, 0, s)

    def relay(step, k):
        landed(relays[step].at[k], r_recv.at[step, k])
        for s, dev in enumerate((y_up, y_down)):
            here, there = relays[step].at[k, s], xs[step].at[k * 8 + 4 + s]
            send(here, there, r_send.at[step], x_recv.at[step, k], dev)

    def points_sent(step):
        landed(xs[step].at[pl.ds(0, 56)], z_send.at[step])
        landed(outs[step], y_send.at[step])
        landed(relays[step], r_send.at[step])

    def arrived(step, k):
        landed(xs[step].at[pl.ds(k * 8 + 2, 6)], x_recv.at[step, k])

    def against(step, k, centroids):
        rows = xs[step][k * 8 : k * 8 + 8].reshape(8 * PB, D)
        return lax.dot_general(
            centroids, rows, (((1,), (1,)), ((), ())), preferred_element_type=F32
        )

    def exps(s):
        top = jnp.max(s, axis=0, keepdims=True)
        e = jnp.exp(s - top)
        return e, top, jnp.sum(e, axis=0, keepdims=True)

    def keep(step, k, lse):
        for i in range(2):
            lses[step][i, k : k + 1, :] = lse[:, i * 128 : (i + 1) * 128]

    def score(k):
        arrived(0, k)
        e, top, total = exps(against(0, k, cent[...]))
        scores[k] = e
        tops[k] = top
        keep(0, k, top + jnp.log(total))

    def sc(part, k):
        if part == 0:
            arrived(1, k)
        which = ((x,), (xm, xp), (xo,))[part]
        places = [cur_rows(c, at) for at in which for c in range(2)]
        s = against(1, k, jnp.concatenate([cur1[rows, :] for rows in places], axis=0))
        for i, at in enumerate(which):
            e, top, total = exps(s[i * 128 : i * 128 + 128])
            scores[k, places[2 * i], :] = e[:64]
            scores[k, places[2 * i + 1], :] = e[64:]
            tops4[at, k] = top
            totals4[at, k] = total

    def join():
        for k in range(NZ):
            top = jnp.maximum(
                jnp.maximum(tops4[0, k], tops4[1, k]), jnp.maximum(tops4[2, k], tops4[3, k])
            )
            total = sum(totals4[i, k] * jnp.exp(tops4[i, k] - top) for i in range(NX))
            keep(1, k, top + jnp.log(total))

    low = lax.broadcasted_iota(jnp.int32, (1, 128), 1) < 64
    group = lax.broadcasted_iota(jnp.int32, (1, 128), 1) >> 5

    def over_groups(op, value):
        value = op(value, pltpu.roll(value, 64, 1))
        return op(value, pltpu.roll(value, 32, 1))

    def block_ids(step):
        return [
            tab_in[:, :, step * 256 + i * 128 : step * 256 + i * 128 + 128].reshape(8, 128)
            for i in range(2)
        ]

    def share(step):
        if step == 1:
            join()
        for p in range(1, NY):
            send(
                lses[step].at[p >> 1],
                stats[step].at[p],
                st_sem.at[step, 0],
                st_sem.at[step, 1],
                at_cluster(0, -p),
            )
        stats[step][0] = lses[step][0]
        later(stats[step].at[pl.ds(1, 3)], st_sem.at[step, 0])

    def partial(step):
        got = stats[step]
        landed(got.at[pl.ds(1, 3)], st_sem.at[step, 1])
        have = [jnp.where(low, got[2 * i], got[2 * i + 1]) for i in range(2)]
        ids = block_ids(step)
        packed = [jnp.full((8, 128), -BIG, F32) for _ in range(2)]
        for b in range(NB):
            mine = [ids[i] == b for i in range(2)]
            masked = [jnp.where(mine[i], have[i], -BIG) for i in range(2)]
            top = over_groups(jnp.maximum, jnp.maximum(masked[0], masked[1]))
            each = [jnp.where(mine[i], jnp.exp(have[i] - top), 0.0) for i in range(2)]
            total = over_groups(jnp.add, each[0] + each[1])
            value = jnp.where(total > 0.0, top + jnp.log(total), -BIG)
            packed[b >> 2] = jnp.where(group == (b & 3), value, packed[b >> 2])
        out = sent_parts[step]
        for i in range(2):
            out[i * 8 : i * 8 + 8, :] = packed[i]
        for j in (4, 3, 5, 2, 6, 1, 7):
            send(
                out,
                parts_in[step].at[j],
                st_sem.at[step, 2],
                st_sem.at[step, 3],
                at_cluster(j, 0),
            )
        later(parts_in[step].at[pl.ds(1, 7)], st_sem.at[step, 2])

    def whole(step):
        into = parts_in[step]
        landed(into.at[pl.ds(1, 7)], st_sem.at[step, 3])
        ids = block_ids(step)
        shift = [jnp.full((8, 128), BIG, F32) for _ in range(2)]
        for i in range(2):
            rows = slice(i * 8, i * 8 + 8)
            seen = [sent_parts[step][rows, :]]
            for j in range(1, NZ):
                seen.append(pltpu.roll(into[j, rows, :], j, 0))
            top = seen[0]
            for j in range(1, NZ):
                top = jnp.maximum(top, seen[j])
            total = jnp.exp(seen[0] - top)
            for j in range(1, NZ):
                total = total + jnp.exp(seen[j] - top)
            value = top + jnp.log(total)
            for b in range(4):
                spread = over_groups(jnp.maximum, jnp.where(group == b, value, -BIG))
                for t in range(2):
                    shift[t] = jnp.where(ids[t] == i * 4 + b, spread, shift[t])
        out, back = sent_shifts[step], shifts[step]
        for t in range(2):
            out[t] = shift[t]
        back[0] = shift[0]
        for p in range(1, NY):
            send(
                out.at[p >> 1],
                back.at[p],
                st_sem.at[step, 4],
                st_sem.at[step, 5],
                at_cluster(0, p),
            )
        later(back.at[pl.ds(1, 3)], st_sem.at[step, 4])

    def wa():
        landed(shifts[0].at[pl.ds(1, 3)], st_sem.at[0, 5])
        weigh_half(1 - core)

    def wb():
        weigh_half(core)

    def weigh_half(which):
        back = shifts[0]
        rows = pl.ds(pl.multiple_of(which * 256, 256), 256)
        for k in range(NZ):
            for t in range(2):
                shift = jnp.where(low, back[2 * t, k : k + 1, :], back[2 * t + 1, k : k + 1, :])
                half_lanes = slice(t * 128, (t + 1) * 128)
                scale = jnp.exp(tops[k, :, half_lanes] - shift)
                lanes = pl.ds(k * 256 + t * 128, 128)
                w[rows, lanes] = (scores[k, rows, half_lanes] * scale).astype(BF16)

    def weigh():
        back = shifts[1]
        landed(back.at[pl.ds(1, 3)], st_sem.at[1, 5])
        for k in range(NZ):
            for t in range(2):
                shift = jnp.where(low, back[2 * t, k : k + 1, :], back[2 * t + 1, k : k + 1, :])
                lanes = pl.ds(k * 256 + t * 128, 128)
                half_lanes = slice(t * 128, (t + 1) * 128)
                for at in range(NX):
                    scale = jnp.exp(tops4[at, k, :, half_lanes] - shift)
                    for first in (at * 64, 256 + at * 64):
                        rows = slice(first, first + 64)
                        w[rows, lanes] = (scores[k, rows, half_lanes] * scale).astype(BF16)

    def half_sums(which, n):
        rows = w[pl.ds(pl.multiple_of(which * 256, 256), 256), :]
        cols = xs[0][:, :, n * 256 : (n + 1) * 256].reshape(64 * PB, 256)
        return jnp.dot(rows, cols, preferred_element_type=F32)

    def rows64(at, count=64, shift=0):
        return pl.ds(pl.multiple_of(at * 64 + shift, 32), count)

    def rf(n):
        psend[n] = half_sums(1 - core, n)
        send(psend.at[n], precv.at[n], dp_send.at[0], dp_recv.at[n], dev_core)

    def ro(n):
        phold[n] = half_sums(core, n)

    def rc(n):
        landed(precv.at[n], dp_recv.at[n])
        far = rows64(xo)
        phold[n, far, :] = phold[n, far, :] + precv[n, far, :]
        sides = ((rows64(xo, 32), dev_xp), (rows64(xo, 32, 32), dev_xm))
        for i, (part, dev) in enumerate(sides):
            send(phold.at[n, part, :], h1.at[i, n], dp_send.at[1], dp_recv.at[4 + n], dev)

    def re(n):
        for at in (xp, xm, x):
            near = rows64(at)
            phold[n, near, :] = phold[n, near, :] + precv[n, near, :]
        for i, (at, shift, dev) in enumerate(((xp, 32, dev_xp), (xm, 0, dev_xm))):
            second_hop(n, i, at, shift, dev)

    def second_hop(n, i, at, shift, dev):
        src = phold.at[n, rows64(at, 32, shift), :]
        send(src, h2.at[i, n, pl.ds(shift, 32)], dp_send.at[2], dp_recv.at[8], dev)

    def rh(n):
        landed(h2.at[0, n], dp_recv.at[4 + n])
        for i, (at, shift, dev) in enumerate(((xp, 0, dev_xp), (xm, 32, dev_xm))):
            part = rows64(at, 32, shift)
            phold[n, part, :] = phold[n, part, :] + h1[i, n]
            second_hop(n, i, at, shift, dev)

    def cur_rows(which_core, at, count=64, shift=0):
        return pl.ds(pl.multiple_of(which_core * 256 + at * 64 + shift, 32), count)

    def update():
        landed(h2, dp_recv.at[8])
        own = rows64(x)
        mine = cur_rows(core, x)
        v = [
            cent[mine, n * 256 : (n + 1) * 256].astype(F32)
            + (phold[n, own, :] + h2[0, n] + h2[1, n])
            for n in range(4)
        ]
        square = sum(jnp.sum(part * part, axis=1, keepdims=True) for part in v)
        norm = jnp.sqrt(square + 1e-06)
        for n in range(4):
            cur1[mine, n * 256 : (n + 1) * 256] = (v[n] / norm).astype(BF16)
        own_rows(0)
        to_core(cur1.at[mine], 0)

    def own_rows(second):
        for i, (shift, dev) in enumerate(((0, dev_xp), (32, dev_xm))):
            part = cur1.at[cur_rows(core, x, 32, 32 - shift if second else shift)]
            send(part, part, dp_send.at[3], dp_recv.at[9 + 2 * second + i], dev)

    def ub():
        own_rows(1)

    def to_core(part, group):
        send(part, part, dp_send.at[3], dp_recv.at[15 + group], dev_core)

    def gather1():
        for i, (at, shift, dev) in enumerate(((xm, 0, dev_xp), (xp, 32, dev_xm))):
            part = cur1.at[cur_rows(core, at, 32, shift)]
            landed(part, dp_recv.at[9 + i])
            send(part, part, dp_send.at[3], dp_recv.at[13 + i], dev)
            to_core(part, 1)

    def gather1b():
        for i, (at, shift) in enumerate(((xm, 32), (xp, 0))):
            part = cur1.at[cur_rows(core, at, 32, shift)]
            landed(part, dp_recv.at[11 + i])
            to_core(part, 1)

    def gather2():
        for i, shift in enumerate((0, 32)):
            part = cur1.at[cur_rows(core, xo, 32, shift)]
            landed(part, dp_recv.at[13 + i])
            to_core(part, 2)

    def gw(group):
        landed(cur1.at[pl.ds(0, (64, 128, 64)[group])], dp_recv.at[15 + group])

    def ls(j):
        lanes = pl.ds(pl.multiple_of((xo, xp, xm, x)[j] * 256, 256), 256)
        cols = xs[1][:, :, lanes].reshape(64 * PB, 256)
        part = jnp.dot(w[...], cols, preferred_element_type=F32)
        fb[j, 0] = part[:, :128]
        fb[j, 1] = part[:, 128:]
        fs[j] = fb[j, 1 - core].astype(BF16)
        send(fs.at[j], fr.at[j], fin_send.at[0], fin_recv.at[j], dev_core)
        if j == 3:
            later(fs, fin_send.at[0])

    def both(j):
        landed(fr.at[j], fin_recv.at[j])
        return fb[j, core] + fr[j].astype(F32)

    def lq():
        g[0] = both(0).astype(BF16)
        for i, dev in enumerate((dev_xp, dev_xm)):
            rows = pl.ds(256 * i, 256)
            send(g.at[0, rows], q.at[i], fin_send.at[2], fin_recv.at[5 + i], dev)

    def last_hop(i, rows):
        dev = (dev_xp, dev_xm)[i]
        send(g.at[1 + i, rows], u.at[i, rows], fin_send.at[3], fin_recv.at[7 + i], dev)

    def lv():
        for i in range(2):
            part = both(1 + i)
            rest = pl.ds(256 - 256 * i, 256)
            fb[1 + i, core] = part
            g[1 + i, rest] = part[256 - 256 * i : 512 - 256 * i].astype(BF16)
            last_hop(i, rest)

    def lu():
        for i in range(2):
            landed(q.at[i], fin_recv.at[5 + i])
            rows = pl.ds(256 * i, 256)
            g[1 + i, rows] = (fb[1 + i, core, rows, :] + q[i].astype(F32)).astype(BF16)
            last_hop(i, rows)

    def cnt():
        ones = jnp.ones((8, 64 * PB), BF16)
        count = lax.dot_general(
            ones, w[...], (((1,), (1,)), ((), ())), preferred_element_type=F32
        )
        cnts[dp] = count[0:1]
        for j in range(1, NX * NC):
            send(
                cnts.at[dp],
                cnts.at[dp],
                fin_send.at[1],
                fin_recv.at[4],
                {"dp": lax.rem(dp + j, NX * NC)},
            )
        later(cnts.at[pl.ds(0, 7)], fin_send.at[1])

    def own():
        fb[3, core] = both(3)
        landed(cnts.at[pl.ds(0, 7)], fin_recv.at[4])
        count = cnts[0]
        for j in range(1, NX * NC):
            count = count + cnts[j]
        for j in range(4):
            out_counts[j : j + 1, :] = count[:, j * 128 : (j + 1) * 128]
        drain()
        landed(q, fin_send.at[2])

    def fin():
        landed(u.at[0], fin_recv.at[7])
        landed(u.at[1], fin_recv.at[8])
        landed(u, fin_send.at[3])
        out_sums[...] = fb[3, core] + (u[0].astype(F32) + u[1].astype(F32))

    parts = dict(
        zs=z_start,
        ze=z_event,
        pr=pr,
        pp=pp,
        re=re,
        ub=ub,
        relay=relay,
        score=score,
        share=share,
        partial=partial,
        whole=whole,
        weigh=weigh,
        wa=wa,
        wb=wb,
        rf=rf,
        ro=ro,
        rc=rc,
        rh=rh,
        update=update,
        gather1=gather1,
        gather1b=gather1b,
        gather2=gather2,
        gw=gw,
        sc=sc,
        ls=ls,
        lq=lq,
        lu=lu,
        lv=lv,
        cnt=cnt,
        own=own,
        fin=fin,
    )
    for name, *numbers in SCHEDULE:
        if (name, *numbers) == ("pr", 0, 0):
            tables()
            for load in loads:
                load.wait()
        parts[name](*numbers)
        if (name, *numbers) == ("relay", 0, 0):
            tables_in()
        if (name, *numbers) == ("partial", 1):
            points_sent(0)
            points_sent(1)
            landed(psend, dp_send.at[0])
            landed(h1, dp_send.at[1])
            landed(h2, dp_send.at[2])
            landed(cur1.at[pl.ds(0, 448)], dp_send.at[3])


def on_device(points, candidates, centroids):
    vmem, hbm = pl.BlockSpec(memory_space=pltpu.VMEM), pl.BlockSpec(memory_space=pl.ANY)
    sem = pltpu.SemaphoreType.DMA
    steps = points.shape[0]
    sums, counts = pl.pallas_call(
        kernel,
        out_shape=(
            jax.ShapeDtypeStruct((CBS, D // (NX * NC)), F32),
            jax.ShapeDtypeStruct((4, 128), F32),
        ),
        in_specs=[hbm, pl.BlockSpec(memory_space=pltpu.SMEM), hbm],
        out_specs=(vmem, vmem),
        scratch_shapes=[
            pltpu.VMEM((steps, NB, PB, D), BF16),
            pltpu.VMEM((CBS, D), BF16),
            [pltpu.VMEM((NB, PB, D), BF16) for _ in range(7 * steps)],
            [pltpu.VMEM((64, PB, D), BF16) for _ in range(steps)],
            [pltpu.VMEM((NZ, 6, PB, D), BF16) for _ in range(steps)],
            [pltpu.VMEM((NZ, 2, PB, D), BF16) for _ in range(steps)],
            pltpu.VMEM((NZ, 1, 512), jnp.int32),
            pltpu.VMEM((NZ, 1, 512), jnp.int32),
            pltpu.SMEM((NZ, 1, 512), jnp.int32),
            pltpu.VMEM((NZ, CBS, 256), F32),
            pltpu.VMEM((NZ, 1, 256), F32),
            pltpu.VMEM((NX, NZ, 1, 256), F32),
            pltpu.VMEM((NX, NZ, 1, 256), F32),
            pltpu.VMEM((CBS, 64 * PB), BF16),
            [pltpu.VMEM((2, 8, 128), F32) for _ in range(steps)],
            [pltpu.VMEM((4, 8, 128), F32) for _ in range(steps)],
            [pltpu.VMEM((16, 128), F32) for _ in range(steps)],
            [pltpu.VMEM((NZ, 16, 128), F32) for _ in range(steps)],
            [pltpu.VMEM((2, 8, 128), F32) for _ in range(steps)],
            [pltpu.VMEM((4, 8, 128), F32) for _ in range(steps)],
            pltpu.VMEM((4, 256, 256), F32),
            pltpu.VMEM((4, 256, 256), F32),
            pltpu.VMEM((4, 256, 256), F32),
            pltpu.VMEM((2, 4, 32, 256), F32),
            pltpu.VMEM((2, 4, 64, 256), F32),
            pltpu.VMEM((CBS, D), BF16),
            pltpu.VMEM((4, 2, CBS, 128), F32),
            pltpu.VMEM((4, CBS, 128), BF16),
            pltpu.VMEM((4, CBS, 128), BF16),
            pltpu.VMEM((3, CBS, 128), BF16),
            pltpu.VMEM((2, 256, 128), BF16),
            pltpu.VMEM((2, CBS, 128), BF16),
            pltpu.VMEM((NX * NC, 1, CBS), F32),
            sem((steps,)),
            sem((steps, 2, 7)),
            sem((steps,)),
            sem((steps, NZ)),
            sem((steps, NZ)),
            sem((steps,)),
            sem((steps, 6)),
            sem((3,)),
            sem((4,)),
            sem((18,)),
            sem((4,)),
            sem((9,)),
            sem((2,)),
        ],
        compiler_params=pltpu.CompilerParams(
            collective_id=0, has_side_effects=True, vmem_limit_bytes=54250 * 1024
        ),
    )(points.reshape(steps, NB, PB, D), jnp.transpose(candidates, (0, 2, 1)), centroids)
    return sums, counts.reshape(CBS)


def solution(mesh):
    placed = (
        P(None, ("dp", "cluster"), None),
        P(None, ("dp", "cluster"), None),
        P("cluster", None),
    )
    return jax.shard_map(
        on_device,
        mesh=mesh,
        in_specs=placed,
        out_specs=(P("cluster", "dp"), P("cluster")),
        check_vma=False,
    )
```
